128 devices in a mesh: row: 4 (over x_hi, core), col: 32 (over y, x_lo, z).
Axes of the slice: x: 4 (x_hi: 2, x_lo: 2; x = x_hi * 2 + x_lo), y: 4, z: 4, core: 2. Of those that a mesh axis runs over, the one named last changes fastest.
Arguments:
- states: bfloat16 [4096, 2048], P('col', 'row'), may hold values from -6 to 6
- teacher: bfloat16 [4096, 2048], P('col', 'row'), may hold values from -10 to 10
- firstgain: float32 [2048], P('row'), may hold values from 0.5 to 1.5
- wquery: bfloat16 [3072, 2048], P('col', 'row'), may hold values from -0.25 to 0.25
- wlatent: bfloat16 [2048, 576], P('row', 'col'), may hold values from -0.125 to 0.125
- latentgain: float32 [512], P('row'), may hold values from 0.5 to 1.5
- wkeyvalue: bfloat16 [512, 4096], P('row', 'col'), may hold values from -0.25 to 0.25
- woutput: bfloat16 [2048, 2048], P('row', 'col'), may hold values from -0.5 to 0.5
- secondgain: float32 [2048], P('row'), may hold values from 0.5 to 1.5
- wrouter: bfloat16 [2048, 8], P('row'), may hold values from -0.0625 to 0.0625
- sharedgate: bfloat16 [2048, 2816], P('row', 'col'), may hold values from -0.125 to 0.125
- sharedup: bfloat16 [2048, 2816], P('row', 'col'), may hold values from -0.125 to 0.125
- shareddown: bfloat16 [2816, 2048], P('row', 'col'), may hold values from -0.109375 to 0.109375
- expertgate: bfloat16 [11264, 2048], P('col', 'row'), may hold values from -0.125 to 0.125
- expertup: bfloat16 [11264, 2048], P('col', 'row'), may hold values from -0.125 to 0.125
- expertdown: bfloat16 [1408, 16384], P('row', 'col'), may hold values from -0.625 to 0.625
- routes: int32 [4096, 6], P('col'), may hold values from 0 to 7, all different within a row
- lengths: int32 [8], replicated, may hold values from 1 to 4000, as said below
- dealing: int32 [4096], replicated, may hold values from 0 to 4095, as said below
Outputs:
- output: bfloat16 [4096, 2048], P('col', 'row')
- loss_value: float32 [], replicated
- grad_states: float32 [4096, 2048], P('col', 'row')
- grad_firstgain: float32 [2048], P(('row', 'col'))
- grad_wquery: float32 [3072, 2048], P('col', 'row')
- grad_wlatent: float32 [2048, 576], P('row', 'col')
- grad_latentgain: float32 [512], P(('row', 'col'))
- grad_wkeyvalue: float32 [512, 4096], P('row', 'col')
- grad_woutput: float32 [2048, 2048], P('row', 'col')
- grad_secondgain: float32 [2048], P(('row', 'col'))
- grad_wrouter: float32 [2048, 8], P(('row', 'col'))
- grad_sharedgate: float32 [2048, 2816], P('row', 'col')
- grad_sharedup: float32 [2048, 2816], P('row', 'col')
- grad_shareddown: float32 [2816, 2048], P('row', 'col')
- grad_expertgate: float32 [11264, 2048], P('col', 'row')
- grad_expertup: float32 [11264, 2048], P('col', 'row')
- grad_expertdown: float32 [1408, 16384], P('row', 'col')
The draws below stay inside these ranges and needn't reach their ends.
Inputs may be any that keep to these rules, and one draw needn't show every extreme that they name: `routes`: each row names 6 different experts. 8 sequence lengths in the packed order; their sum is under 4096, and the places after the last sequence are padding. `dealing`: a permutation of the 4096 places; with n = 32, row j of every block of 128 rows holds a place from j * n to j * n + n - 1.
All inputs are finite; a program needn't handle non-finite values.
Results may differ from the reference program's by a relative error of at most 0.015.
The reference program's roundings to bfloat16 on the way count: a program that leaves them out, or rounds other values in their place, can miss the bound.
Values may be sent and summed in bfloat16 or wider, within the bound.
No kernel may reach another device: no remote copies, remote signals or barrier semaphores. Data moves between devices by JAX's collectives and lax.ppermute only.
A program may use at most 256 MiB of HBM per device.

```python
import math
import jax
import jax.numpy as jnp
from jax import lax

D = 2048
HEADS = 16
NOPE = 128
ROPE = 64
VDIM = 128
KV_RANK = 512
F = 1408
TOPK = 6
EXPERTS = 8
SEQS = 8
TOK_DEV = 128
SH_FF = 2816
TOKENS = 4096


def draw_lengths(key, part):
    key = jax.random.fold_in(key, 11)
    keys_split = jax.random.split(key, 2)
    shorter = jax.random.randint(keys_split[0], (SEQS,), 1, TOK_DEV // 16 + 1)
    longest = jax.random.randint(keys_split[1], (), 0, SEQS)
    numbers = jnp.arange(SEQS)
    marked = numbers == longest
    single = numbers == (longest + 1) % SEQS
    result = jnp.where(marked, TOKENS - 3 * TOK_DEV // 4, jnp.where(single, 1, shorter))
    return result.astype(jnp.int32)


def draw_dealing(key, part):
    key = jax.random.fold_in(key, 17)
    groups = TOKENS // TOK_DEV
    shifts = jax.random.randint(key, (TOK_DEV,), 0, groups)
    device_ids = jnp.arange(groups, dtype=jnp.int32)[:, None]
    row_ids = jnp.arange(TOK_DEV, dtype=jnp.int32)[None, :]
    places = row_ids * groups + (device_ids - shifts[None, :]) % groups
    return places.reshape(TOKENS).astype(jnp.int32)


def draw_teacher(key, part):
    key = jax.random.fold_in(key, 5)
    row_share = jnp.arange(TOKENS, dtype=jnp.float32) / TOKENS
    scales = 0.5 + 1.5 * row_share
    values = jnp.clip(jax.random.normal(key, (TOKENS, D), jnp.float32), -5.0, 5.0)
    return (values * scales[:, None]).astype(jnp.bfloat16)


def level_of(stream_key, dims, cuts, smallest, high):
    def one(axis_at, parts):
        heights = jax.random.uniform(jax.random.fold_in(jax.random.fold_in(stream_key, 6), axis_at), (parts,), jnp.float32, smallest / len(cuts), high / len(cuts))
        return jnp.repeat(jnp.exp(heights), dims[axis_at] // parts).reshape((-1,) + (1,) * (len(dims) - axis_at - 1))

    loudness = one(*cuts[0])
    for cut in cuts[1:]:
        loudness = loudness * one(*cut)
    return loudness


def picks_of(stream_key, rows, count, top, lift):
    ranking = jax.random.permutation(jax.random.fold_in(stream_key, 1), count)
    pull = ranking
    for power in range(3):
        pull = pull * pull // count
    pull = pull * lift // count
    chance = jax.random.randint(jax.random.fold_in(stream_key, 2), (rows, count), 0, 4096) + pull
    fixed_rows = jax.random.permutation(jax.random.fold_in(stream_key, 3), rows)[jnp.arange(count) % rows]
    chance = jnp.where(jnp.arange(rows)[:, None] == fixed_rows[None, :], 1 << 14, chance)
    priority = chance * count + jnp.arange(count)
    return lax.top_k(priority.astype(jnp.int32), top)[1].astype(jnp.int32)


def scatter_about(stream_key, extent, spread, bound, shards=(), held_as=jnp.bfloat16):
    entries = jax.random.normal(stream_key, extent, jnp.float32) * spread
    if len(shards) > 0:
        entries = level_of(stream_key, extent, shards, -0.22, 0.18) * entries
    return jnp.clip(entries, min=-bound, max=bound).astype(held_as)


def setup_inputs(seed: int = 0) -> dict:
    keys = jax.random.split(jax.random.key(seed), 20)
    return {
        "states": scatter_about(keys[0], (TOKENS, D), 1.0, 6.0, ((0, 32), (1, 4))),
        "teacher": draw_teacher(jax.random.fold_in(keys[19], 71), 0),
        "firstgain": jnp.clip(1.0 + 0.1 * jax.random.normal(keys[2], (D,), jnp.float32), 0.5, 1.5),
        "wquery": scatter_about(keys[3], (HEADS * (NOPE + ROPE), D), (D // 4) ** -0.5, 0.25, ((0, 32), (1, 4))),
        "wlatent": scatter_about(keys[4], (D, KV_RANK + ROPE), D ** -0.5, 0.125, ((0, 4), (1, 32))),
        "latentgain": jnp.clip(1.0 + 0.1 * jax.random.normal(keys[5], (KV_RANK,), jnp.float32), 0.5, 1.5),
        "wkeyvalue": scatter_about(keys[6], (KV_RANK, HEADS * (NOPE + VDIM)), KV_RANK ** -0.5, 0.25, ((0, 4), (1, 32))),
        "woutput": scatter_about(keys[7], (HEADS * VDIM, D), (HEADS * VDIM // 16) ** -0.5, 0.5, ((0, 4), (1, 32))),
        "secondgain": jnp.clip(1.0 + 0.1 * jax.random.normal(keys[8], (D,), jnp.float32), 0.5, 1.5),
        "wrouter": scatter_about(keys[9], (D, EXPERTS), (4 * D) ** -0.5, 0.0625, ((0, 4),)),
        "sharedgate": scatter_about(keys[10], (D, SH_FF), D ** -0.5, 0.125, ((0, 4), (1, 32))),
        "sharedup": scatter_about(keys[11], (D, SH_FF), D ** -0.5, 0.125, ((0, 4), (1, 32))),
        "shareddown": scatter_about(keys[12], (SH_FF, D), SH_FF ** -0.5, 0.109375, ((0, 4), (1, 32))),
        "expertgate": scatter_about(keys[13], (EXPERTS * F, D), D ** -0.5, 0.125, ((0, 32), (1, 4))),
        "expertup": scatter_about(keys[14], (EXPERTS * F, D), D ** -0.5, 0.125, ((0, 32), (1, 4))),
        "expertdown": scatter_about(keys[15], (F, EXPERTS * D), (F // 16) ** -0.5, 0.625, ((0, 4), (1, 32))),
        "routes": picks_of(keys[16], TOKENS, EXPERTS, TOPK, 6144),
        "lengths": draw_lengths(jax.random.fold_in(keys[19], 71), 0),
        "dealing": draw_dealing(jax.random.fold_in(keys[19], 71), 0),
    }


@jax.custom_vjp
def low(v):
    return lax.optimization_barrier(v.astype(jnp.bfloat16)).astype(jnp.float32)

@jax.custom_vjp
def low_back(v):
    return v

def low_keep(v):
    return (low(v), None)

def low_pass(kept, grad):
    return (grad,)

def back_keep(v):
    return (v, None)

def back_low(kept, grad):
    return (low(grad),)
low.defvjp(low_keep, low_pass)
low_back.defvjp(back_keep, back_low)
norm_epsilon = 1e-06
negative_fill = -1e+30
rope_base = 10000.0
highest = lax.Precision.HIGHEST

def widen(array):
    return array.astype(jnp.float32)

def matmul(leftside, rightside):
    return jnp.dot(leftside, rightside, precision=highest, preferred_element_type=jnp.float32)

def norm_rows(values, gain):
    return values * lax.rsqrt(lax.optimization_barrier(jnp.mean(values * values, axis=-1, keepdims=True)) + norm_epsilon) * gain

def rotate(values, angles):
    halfway = values.shape[-1] // 2
    cosine = jnp.cos(angles)
    sine_part = jnp.sin(angles)
    leading = values[..., :halfway]
    trailing = values[..., halfway:]
    return jnp.concatenate([leading * cosine - trailing * sine_part, trailing * cosine + leading * sine_part], axis=-1)

def rope_angles(position, rope_width):
    exponents = jnp.arange(rope_width // 2, dtype=jnp.float32) * (2.0 / rope_width)
    frequency = jnp.exp(-math.log(rope_base) * exponents)
    return position.astype(jnp.float32)[:, None] * frequency[None, :]

def token_layout(lengths, places):
    seq_ends = jnp.cumsum(lengths).astype(jnp.int32)
    starts = jnp.concatenate([jnp.zeros((1,), jnp.int32), seq_ends]).astype(jnp.int32)
    places = places.astype(jnp.int32)
    segment = lax.optimization_barrier(jnp.sum((places[:, None] >= seq_ends[None, :]).astype(jnp.int32), axis=1)).astype(jnp.int32)
    numbers = jnp.arange(seq_ends.shape[0] + 1, dtype=jnp.int32)
    begins = lax.optimization_barrier(jnp.sum(jnp.where(segment[:, None] == numbers[None, :], starts[None, :], 0), axis=1)).astype(jnp.int32)
    return (segment, (places - begins).astype(jnp.int32))

def attend_block(blocked, keys_nope, keys_rope, values, key_segment, key_index):
    query_block, query_segment, query_index = blocked
    raw_scores = jnp.einsum('qhd,khd->hqk', query_block[..., :NOPE], keys_nope, precision=highest)
    raw_scores = raw_scores + jnp.einsum('qhd,kd->hqk', query_block[..., NOPE:], keys_rope, precision=highest)
    scores = low_back(raw_scores * (NOPE + ROPE) ** (-0.5))
    allowed = (query_segment[:, None] == key_segment[None, :]) & (key_index[None, :] <= query_index[:, None])
    scores = jnp.where(allowed[None, :, :], scores, negative_fill)
    weights = jax.nn.softmax(scores, axis=-1)
    return jnp.einsum('hqk,khd->qhd', weights, values, precision=highest)

def reference(states, teacher, firstgain, wquery, wlatent, latentgain, wkeyvalue, woutput, secondgain, wrouter, sharedgate, sharedup, shareddown, expertgate, expertup, expertdown, routes, lengths, dealing):
    indices = dealing.astype(jnp.int32)
    segment, position = token_layout(lengths, indices)
    angles = rope_angles(position, ROPE)
    valid_rows = (segment < SEQS).astype(jnp.float32)
    valid_count = jnp.sum(lengths).astype(jnp.float32)
    chosen = lax.optimization_barrier(jnp.sum((routes[:, :, None] == jnp.arange(EXPERTS, dtype=jnp.int32)[None, None, :]).astype(jnp.float32), axis=1))
    block_rows = math.gcd(TOKENS, 512)
    block_count = TOKENS // block_rows

    def forward(states, firstgain, wquery, wlatent, latentgain, wkeyvalue, woutput, secondgain, wrouter, sharedgate, sharedup, shareddown, expertgate, expertup, expertdown):
        normed_in = low(norm_rows(states, firstgain))
        query_proj = low_back(matmul(normed_in, wquery.T)).reshape(TOKENS, HEADS, NOPE + ROPE)
        latent = low_back(matmul(normed_in, wlatent))
        compressed = low(norm_rows(latent[:, :KV_RANK], latentgain))
        keyvalue = low_back(matmul(compressed, wkeyvalue)).reshape(TOKENS, HEADS, NOPE + VDIM)
        query_in = low(jnp.concatenate([query_proj[..., :NOPE], rotate(query_proj[..., NOPE:], angles[:, None, :])], axis=-1))
        keys_nope = low(keyvalue[..., :NOPE])
        values = low(keyvalue[..., NOPE:])
        keys_rope = low(rotate(latent[:, KV_RANK:], angles))

        def attend(blocked):
            return attend_block(blocked, keys_nope, keys_rope, values, segment, indices)
        attended = lax.map(jax.checkpoint(attend), (query_in.reshape(block_count, block_rows, HEADS, NOPE + ROPE), segment.reshape(block_count, block_rows), indices.reshape(block_count, block_rows)))
        attended = low(low_back(attended.reshape(TOKENS, HEADS * VDIM)))
        residual = states + low_back(matmul(attended, woutput))
        normed_mid = low(norm_rows(residual, secondgain))
        logits = low_back(matmul(normed_mid, wrouter))
        combine = jax.nn.softmax(logits, axis=-1) * chosen
        shared_hidden = low(jax.nn.silu(low_back(matmul(normed_mid, sharedgate))) * low_back(matmul(normed_mid, sharedup)))

        def expert_step(running, stacked):
            gate_part, upper_part, lower_part, column = stacked
            gate_value = low_back(matmul(normed_mid, gate_part.T))
            lifted = low_back(matmul(normed_mid, upper_part.T))
            hidden = low(column[:, None] * jax.nn.silu(gate_value) * lifted)
            return (running + matmul(hidden, lower_part), None)
        gate_stack = expertgate.reshape(EXPERTS, F, D)
        upper_stack = expertup.reshape(EXPERTS, F, D)
        lower_stack = jnp.transpose(expertdown.reshape(F, EXPERTS, D), (1, 0, 2))
        routed, unused = lax.scan(jax.checkpoint(expert_step), jnp.zeros((TOKENS, D), jnp.float32), (gate_stack, upper_stack, lower_stack, combine.T))
        return residual + low_back(matmul(shared_hidden, shareddown) + routed)
    final_state, pullback = jax.vjp(forward, widen(states), widen(firstgain), widen(wquery), widen(wlatent), widen(latentgain), widen(wkeyvalue), widen(woutput), widen(secondgain), widen(wrouter), widen(sharedgate), widen(sharedup), widen(shareddown), widen(expertgate), widen(expertup), widen(expertdown))
    difference = (final_state - widen(teacher)) * valid_rows[:, None]
    loss_value = jnp.sum(difference * difference) / (valid_count * D)
    gradients = pullback(difference * (TOKENS / valid_count))
    return (final_state.astype(jnp.bfloat16), loss_value, gradients[0], gradients[1], gradients[2], gradients[3], gradients[4], gradients[5], gradients[6], gradients[7], gradients[8], gradients[9], gradients[10], gradients[11], gradients[12], gradients[13], gradients[14])
```

```python
import math

import jax
import jax.numpy as jnp
from jax import lax
from jax.sharding import Mesh, PartitionSpec as P

HEADS = 16
NOPE = 128
ROPE = 64
VDIM = 128
KV_RANK = 512
F = 1408
EXPERTS = 8
D = 2048

norm_epsilon = 1e-06
negative_fill = -1e30
rope_base = 10000.0

ROW = ("xh", "co")
COL = ("y", "xl", "z")
WEIGHT = ("xh", "co", "y")
TOKEN = ("xl", "z")
TOKEN_Z = ("z", "xl")

bf16 = jnp.bfloat16
f32 = jnp.float32


def dot(spec, a, b):
    return jnp.einsum(spec, a, b, preferred_element_type=f32)


def exchange(x, axes):
    return lax.all_to_all(x, axes, 0, 0, tiled=True)


def spread(x, axes, n):
    return exchange(jnp.broadcast_to(x[None], (n,) + x.shape), axes)


def pieces(x, n):
    parts = []
    for _ in range(n):
        part = lax.reduce_precision(x, 8, 7)
        parts.append(part.astype(bf16))
        x = x - part
    return parts


def swap_row_y(x):
    pairs = [(r * 4 + y, y * 4 + r) for r in range(4) for y in range(4)]
    return lax.ppermute(x, WEIGHT, pairs)


def swap_row_token(x):
    pairs = [
        (r * 8 + q * 2 + low, q * 8 + r * 2 + low)
        for r in range(4)
        for q in range(4)
        for low in range(2)
    ]
    return lax.ppermute(x, ROW + TOKEN, pairs)


def rotate_rows(v, cosine, sine):
    a, b = v[: ROPE // 2], v[ROPE // 2 :]
    return jnp.concatenate([a * cosine - b * sine, b * cosine + a * sine], axis=0)


def rotate_back_rows(g, cosine, sine):
    a, b = g[: ROPE // 2], g[ROPE // 2 :]
    return jnp.concatenate([a * cosine + b * sine, b * cosine - a * sine], axis=0)


def rope_angles(position):
    exponents = jnp.arange(ROPE // 2, dtype=f32) * (2.0 / ROPE)
    frequency = jnp.exp(-math.log(rope_base) * exponents)
    return frequency[:, None] * position.astype(f32)[None, :]


def places_of(lengths, places):
    seq_ends = jnp.cumsum(lengths)
    starts = jnp.concatenate([jnp.zeros((1,), jnp.int32), seq_ends])
    segment = jnp.sum((places[:, None] >= seq_ends[None, :]).astype(jnp.int32), axis=1)
    numbers = jnp.arange(seq_ends.shape[0] + 1, dtype=jnp.int32)
    begins = jnp.sum(jnp.where(segment[:, None] == numbers[None, :], starts[None, :], 0), axis=1)
    return begins, segment < lengths.shape[0]


def to_owners(partial):
    return partial.reshape(4, 128, 4, 512).transpose(2, 0, 1, 3).reshape(16, 128, 512)


def from_owners(blocks):
    return blocks.reshape(4, 4, 128, 512).transpose(1, 2, 0, 3).reshape(512, D)


def shards(
    states,
    teacher,
    firstgain,
    wquery,
    wlatent,
    latentgain,
    wkeyvalue,
    woutput,
    secondgain,
    wrouter,
    sharedgate,
    sharedup,
    shareddown,
    expertgate,
    expertup,
    expertdown,
    routes,
    lengths,
    dealing,
):
    y_index = lax.axis_index("y")
    group = lax.axis_index("xl") * 4 + lax.axis_index("z")
    score_scale = (NOPE + ROPE) ** (-0.5)

    dealt = dealing.reshape(4, 8, 128)
    key_place = dealt.transpose(1, 0, 2).reshape(4096)
    place = lax.dynamic_index_in_dim(dealt, group, 1, keepdims=False).reshape(512)
    begin, valid = places_of(lengths, place)
    angles = rope_angles(place - begin)
    cosine, sine = jnp.cos(angles), jnp.sin(angles)
    own_valid = lax.dynamic_slice_in_dim(valid.astype(f32), y_index * 128, 128, 0)
    valid_count = jnp.sum(lengths).astype(f32)
    chosen_own = jnp.sum(
        (routes[:, :, None] == jnp.arange(EXPERTS, dtype=jnp.int32)[None, None, :]).astype(f32),
        axis=1,
    )

    extra = jnp.concatenate(
        [p[None] for p in pieces(firstgain, 3)]
        + [wrouter.T]
        + [jnp.pad(jnp.concatenate(pieces(latentgain, 3)), (0, 128))[None]]
        + [chosen_own.astype(bf16).reshape(2, 512)]
        + [jnp.zeros((2, 512), bf16)],
        axis=0,
    )
    first = spread(jnp.concatenate([states, extra], axis=0), WEIGHT, 16).reshape(4, 4, 144, 512)

    pack = jnp.concatenate(
        [wquery, wkeyvalue.T.reshape(32, 512), wlatent.T, jnp.zeros((6, 512), bf16)], axis=0
    )
    pack = spread(swap_row_token(pack), TOKEN, 8).reshape(4, 2, 152, 512)
    wq = pack[:, :, :96].transpose(1, 2, 0, 3).reshape(192, D)
    wkv_t = (
        pack[:, :, 96:128].reshape(4, 2, 128, 128).transpose(1, 2, 0, 3).reshape(256, KV_RANK)
    )
    wlat = pack[:, :, 128:146].transpose(1, 2, 0, 3).reshape(36, D)

    down_pack = jnp.concatenate(
        [
            woutput.T.reshape(64, 4, 128).transpose(1, 0, 2),
            jnp.pad(
                shareddown.T.reshape(64, 8, 4, 22).transpose(2, 0, 1, 3),
                ((0, 0), (0, 0), (0, 0), (0, 2)),
            ).reshape(4, 64, 192),
        ],
        axis=2,
    )
    down_pack = swap_row_y(down_pack)
    shared_pack = jnp.pad(
        jnp.stack([sharedgate.T, sharedup.T]).reshape(2, 4, 22, 512),
        ((0, 0), (0, 0), (0, 2), (0, 0)),
    ).transpose(1, 0, 2, 3)
    routed = exchange(
        jnp.concatenate(
            [
                down_pack.reshape(4, 40, 512),
                shared_pack.reshape(4, 48, 512),
                expertgate.reshape(4, 88, 512),
                expertup.reshape(4, 88, 512),
                expertdown.reshape(4, 88, 512),
            ],
            axis=1,
        ),
        ROW,
    )
    down_pack = lax.all_gather(
        routed[:, :40].reshape(256, 320), TOKEN, axis=0, tiled=True
    ).reshape(8, 4, 64, 320)
    down_pack = down_pack.transpose(1, 0, 2, 3).reshape(4, 512, 320)
    wo_t = down_pack[:, :, :128]
    sd_t = down_pack[:, :, 128:]

    def gather_units(block):
        rows = block.shape[1]
        return lax.all_gather(
            block.transpose(1, 0, 2).reshape(rows, D), TOKEN, axis=0, tiled=True
        )

    shared_in = gather_units(routed[:, 40:88]).reshape(8, 2, 24, D)
    wsg = shared_in[:, 0].reshape(192, D)
    wsu = shared_in[:, 1].reshape(192, D)
    wg = gather_units(routed[:, 88:176])
    wu = gather_units(routed[:, 176:264])
    wd = lax.all_gather(
        routed[:, 264:352].reshape(352, 512), TOKEN_Z, axis=0, tiled=True
    ).reshape(4, 704, 512)

    gain_in = jnp.sum(first[:, 0, 128:131].astype(f32), axis=1).reshape(D)
    router = first[:, 0, 131:139].transpose(1, 0, 2).reshape(8, D)
    rank_gain = jnp.sum(first[:, 0, 139, :384].astype(f32).reshape(4, 3, 128), axis=1).reshape(
        KV_RANK
    )
    chosen = first[0, :, 140:142].astype(f32).reshape(512, 8)
    wide = from_owners(first[:, :, :128].reshape(16, 128, 512)).astype(f32)
    inverse_one = lax.rsqrt(jnp.mean(wide * wide, axis=1) + norm_epsilon)
    normed_in = (wide * inverse_one[:, None] * gain_in).astype(bf16)
    query = dot("od,td->ot", wq, normed_in)
    query = jnp.concatenate(
        [query[:NOPE], rotate_rows(query[NOPE:], cosine, sine)], axis=0
    ).astype(bf16)
    latent = spread(dot("cd,td->ct", wlat, normed_in), WEIGHT, 16)
    latent = latent.reshape(4, 4, 36, 512).transpose(1, 0, 2, 3).reshape(576, 512)
    latent_head = latent[:KV_RANK]
    latent_inverse = lax.rsqrt(jnp.mean(latent_head * latent_head, axis=0) + norm_epsilon)
    compressed = (latent_head * latent_inverse[None, :] * rank_gain[:, None]).astype(bf16)
    keyvalue = dot("or,rt->ot", wkv_t, compressed)
    rope_key = rotate_rows(latent[KV_RANK:], cosine, sine)
    key_pack = spread(
        jnp.concatenate([keyvalue[:NOPE], rope_key, keyvalue[NOPE:]], axis=0).astype(bf16),
        TOKEN,
        8,
    )
    key_pack = key_pack.transpose(1, 0, 2).reshape(320, 4096)
    keys, values = key_pack[:192], key_pack[192:]

    allowed = (key_place[None, :] >= begin[:, None]) & (key_place[None, :] <= place[:, None])
    scores = jnp.where(allowed, dot("dt,ds->ts", query, keys) * score_scale, negative_fill)
    top = jnp.max(scores, axis=1, keepdims=True)
    weights = jnp.where(allowed, jnp.exp(scores - top), 0.0)
    total = jnp.sum(weights, axis=1, keepdims=True)
    probs = weights / total
    attended = dot("ts,ds->td", weights.astype(bf16), values) / total
    attn_in = attended.astype(bf16)
    partial = dot("td,rod->rto", attn_in, wo_t).astype(bf16)
    mixed_sum = exchange(partial.reshape(16, 128, 512), WEIGHT)
    mixed = states.astype(f32) + jnp.sum(mixed_sum.astype(f32), axis=0)

    squares = lax.psum(jnp.sum(mixed * mixed, axis=1), ROW)
    inverse_two = lax.rsqrt(squares / D + norm_epsilon)
    normed_mid_own = (mixed * inverse_two[:, None] * secondgain).astype(bf16)
    normed_mid = from_owners(spread(normed_mid_own, WEIGHT, 16))

    logits = dot("td,ed->te", normed_mid, router)
    routing = jax.nn.softmax(logits, axis=1)
    combine = routing * chosen
    combine_pair = lax.dynamic_slice_in_dim(combine, 2 * y_index, 2, 1)
    factor = jnp.broadcast_to(combine_pair[:, :, None], (512, 2, 352)).reshape(512, 704)
    gate_shared = dot("td,fd->tf", normed_mid, wsg)
    up_shared = dot("td,fd->tf", normed_mid, wsu)
    gate_routed = dot("td,fd->tf", normed_mid, wg)
    up_routed = dot("td,fd->tf", normed_mid, wu)
    sig_shared = jax.nn.sigmoid(gate_shared)
    sig_routed = jax.nn.sigmoid(gate_routed)
    silu_shared = gate_shared * sig_shared
    silu_routed = gate_routed * sig_routed
    act_routed = silu_routed * up_routed
    hidden_shared = (silu_shared * up_shared).astype(bf16)
    hidden_routed = (factor * act_routed).astype(bf16)
    branch = dot("tf,zfo->zto", hidden_routed, wd) + dot("tf,rof->rto", hidden_shared, sd_t)
    branch = exchange(branch.astype(bf16).reshape(16, 128, 512), WEIGHT)
    final = mixed + jnp.sum(branch.astype(f32), axis=0)
    output = final.astype(bf16)

    difference = (final - teacher.astype(f32)) * own_valid[:, None]
    error_own = jnp.sum(difference * difference)
    grad_final = difference * (4096.0 / valid_count)
    grad_branch = spread(grad_final.astype(bf16), WEIGHT, 16).reshape(4, 512, 512)

    grad_hidden_shared = sum(dot("to,of->tf", grad_branch[r], sd_t[r]) for r in range(4))
    grad_hidden_routed = sum(dot("to,fo->tf", grad_branch[r], wd[r]) for r in range(4))
    grad_down = dot("tf,zto->zfo", hidden_routed, grad_branch).astype(bf16)
    grad_sd = dot("rto,tf->rof", grad_branch, hidden_shared).astype(bf16)
    grad_combine = jnp.sum((grad_hidden_routed * act_routed).reshape(512, 2, 352), axis=2)
    grad_act = grad_hidden_routed * factor
    grad_gate_shared = (
        grad_hidden_shared * up_shared * sig_shared * (1.0 + gate_shared * (1.0 - sig_shared))
    ).astype(bf16)
    grad_up_shared = (grad_hidden_shared * silu_shared).astype(bf16)
    grad_gate_routed = (
        grad_act * up_routed * sig_routed * (1.0 + gate_routed * (1.0 - sig_routed))
    ).astype(bf16)
    grad_up_routed = (grad_act * silu_routed).astype(bf16)
    grad_mid = (
        dot("tf,fd->td", grad_gate_shared, wsg)
        + dot("tf,fd->td", grad_up_shared, wsu)
        + dot("tf,fd->td", grad_gate_routed, wg)
        + dot("tf,fd->td", grad_up_routed, wu)
    )
    grad_wsg = dot("tf,td->fd", grad_gate_shared, normed_mid).astype(bf16)
    grad_wsu = dot("tf,td->fd", grad_up_shared, normed_mid).astype(bf16)
    grad_wg = dot("tf,td->fd", grad_gate_routed, normed_mid).astype(bf16)
    grad_wu = dot("tf,td->fd", grad_up_routed, normed_mid).astype(bf16)

    def behind(vals, rows):
        flat = jnp.concatenate(pieces(vals, 2), axis=1)
        return jnp.pad(flat, ((0, 0), (0, rows * 512 - flat.shape[1]))).reshape(16, rows, 512)

    def read_behind(rows, n):
        flat = rows.astype(f32).reshape(16, -1)
        return flat[:, :n] + flat[:, n : 2 * n]

    inner_two = jnp.sum(grad_mid * normed_mid.astype(f32), axis=1).reshape(4, 128)
    side = jnp.concatenate(
        [inner_two, grad_combine.reshape(4, 128, 2).transpose(0, 2, 1).reshape(4, 256)], axis=1
    )
    side = jnp.broadcast_to(side[None], (4, 4, 384)).reshape(16, 384)
    got = exchange(
        jnp.concatenate([to_owners(grad_mid).astype(bf16), behind(side, 8)], axis=1), WEIGHT
    )
    grad_mid_own = jnp.sum(got[:, :128].astype(f32), axis=0)
    side = read_behind(got[:, 128:], 384)
    inner_own = jnp.sum(side[:, :128], axis=0)
    combine_own = jnp.sum(side[:, 128:].reshape(4, 8, 128), axis=0).T
    routing_own = lax.dynamic_slice_in_dim(routing, y_index * 128, 128, 0)
    logits_own = lax.dynamic_slice_in_dim(logits, y_index * 128, 128, 0)
    grad_routing = combine_own * chosen_own
    grad_logits = (
        routing_own
        * (grad_routing - jnp.sum(routing_own * grad_routing, axis=1, keepdims=True))
    ).astype(bf16)
    grad_router = dot("td,te->de", normed_mid_own, grad_logits)
    grad_mid_own = grad_mid_own + dot("te,de->td", grad_logits, wrouter)
    inner_own = inner_own + jnp.sum(grad_logits.astype(f32) * logits_own, axis=1)
    grad_mixed = (
        grad_final
        + grad_mid_own * secondgain * inverse_two[:, None]
        - mixed * (inverse_two * inverse_two * inner_own / D)[:, None]
    )
    grad_second = jnp.sum(grad_mid_own * mixed * inverse_two[:, None], axis=0)

    grad_attn = spread(grad_mixed.astype(bf16), WEIGHT, 16).reshape(4, 512, 512)
    grad_attended = sum(dot("to,od->td", grad_attn[r], wo_t[r]) for r in range(4)).astype(bf16)
    grad_wo = dot("rto,td->rod", grad_attn, attn_in).astype(bf16)
    delta = jnp.sum(grad_attended.astype(f32) * attended, axis=1, keepdims=True)
    grad_probs = dot("td,ds->ts", grad_attended, values)
    grad_scores = (probs * (grad_probs - delta)).astype(bf16)
    grad_query = dot("ds,ts->dt", keys, grad_scores) * score_scale
    grad_keys = dot("dt,ts->ds", query, grad_scores) * score_scale
    grad_values = dot("td,ts->ds", grad_attended, probs.astype(bf16))
    grad_kv = jnp.concatenate([grad_keys, grad_values], axis=0).astype(bf16)
    grad_kv = exchange(grad_kv.reshape(320, 8, 512).transpose(1, 0, 2), TOKEN)
    grad_kv = jnp.sum(grad_kv.astype(f32), axis=0)
    grad_rope = rotate_back_rows(grad_kv[NOPE : NOPE + ROPE], cosine, sine)
    grad_keyvalue = jnp.concatenate([grad_kv[:NOPE], grad_kv[NOPE + ROPE :]], axis=0).astype(bf16)
    grad_wkv = dot("ot,rt->or", grad_keyvalue, compressed)
    grad_compressed = dot("or,ot->rt", wkv_t, grad_keyvalue)
    scaled = grad_compressed * rank_gain[:, None]
    inner_rank = jnp.sum(scaled * latent_head, axis=0)
    grad_rank_gain = jnp.sum(grad_compressed * latent_head * latent_inverse[None, :], axis=1)
    grad_latent = jnp.concatenate(
        [
            scaled * latent_inverse[None, :]
            - latent_head
            * (latent_inverse * latent_inverse * latent_inverse * inner_rank / KV_RANK)[None, :],
            grad_rope,
        ],
        axis=0,
    )
    grad_latent = exchange(
        grad_latent.astype(bf16).reshape(4, 4, 36, 512).transpose(1, 0, 2, 3).reshape(16, 36, 512),
        WEIGHT,
    )
    grad_latent = jnp.sum(grad_latent.astype(f32), axis=0).astype(bf16)
    grad_query = jnp.concatenate(
        [grad_query[:NOPE], rotate_back_rows(grad_query[NOPE:], cosine, sine)], axis=0
    ).astype(bf16)
    grad_wq = dot("ot,td->od", grad_query, normed_in)
    grad_wlat = dot("ct,td->cd", grad_latent, normed_in)
    grad_in = dot("ot,od->td", grad_query, wq) + dot("ct,cd->td", grad_latent, wlat)
    inner_one = jnp.sum(grad_in * normed_in.astype(f32), axis=1).reshape(4, 128)
    side = jnp.concatenate(
        [
            jnp.broadcast_to(inner_one[None], (4, 4, 128)),
            jnp.broadcast_to(grad_rank_gain.reshape(4, 1, 128), (4, 4, 128)),
            jnp.broadcast_to(error_own, (4, 4, 1)),
        ],
        axis=2,
    ).reshape(16, 257)
    got = exchange(
        jnp.concatenate([to_owners(grad_in).astype(bf16), behind(side, 8)], axis=1), WEIGHT
    )
    grad_in_own = jnp.sum(got[:, :128].astype(f32), axis=0)
    side = jnp.sum(read_behind(got[:, 128:], 257), axis=0)
    own_wide = states.astype(f32)
    inverse_own = lax.dynamic_slice_in_dim(inverse_one, y_index * 128, 128, 0)
    grad_states = (
        grad_mixed
        + grad_in_own * firstgain * inverse_own[:, None]
        - own_wide * (inverse_own * inverse_own * side[:128] / D)[:, None]
    )
    grad_first = jnp.sum(grad_in_own * own_wide * inverse_own[:, None], axis=0)

    small = jnp.concatenate(
        [
            grad_first.reshape(32, 16),
            grad_second.reshape(32, 16),
            grad_router.reshape(32, 128),
            0.25 * side[128:256].reshape(32, 4),
            jnp.broadcast_to(0.25 * side[256], (32, 1)),
            jnp.zeros((32, 91), f32),
        ],
        axis=1,
    )
    small = jnp.sum(exchange(small, COL), axis=0)
    loss_value = small[164] / (valid_count * D)

    def sum_units(block, axes=TOKEN):
        return lax.psum_scatter(block, axes, scatter_dimension=0, tiled=True)

    grad_wg = sum_units(grad_wg)
    grad_wu = sum_units(grad_wu)
    grad_down = sum_units(grad_down.reshape(2816, 512), TOKEN_Z)
    grad_shared = sum_units(
        jnp.concatenate([grad_wsg.reshape(8, 24, D), grad_wsu.reshape(8, 24, D)], axis=1).reshape(
            384, D
        )
    )
    grad_outs = sum_units(
        jnp.concatenate([grad_wo, grad_sd], axis=2)
        .reshape(4, 8, 64, 320)
        .transpose(1, 0, 2, 3)
        .reshape(2048, 320)
    )

    def split_units(block):
        return block.reshape(block.shape[0], 4, 512).transpose(1, 0, 2)

    back = exchange(
        jnp.concatenate(
            [
                grad_outs.reshape(4, 40, 512),
                split_units(grad_shared),
                split_units(grad_wg),
                split_units(grad_wu),
                grad_down.reshape(4, 88, 512),
            ],
            axis=1,
        ),
        ROW,
    )
    grad_outs = swap_row_y(back[:, :40].reshape(4, 64, 320)).astype(f32)
    grad_woutput = grad_outs[:, :, :128].transpose(0, 2, 1).reshape(512, 64)
    grad_shareddown = (
        grad_outs[:, :, 128:]
        .reshape(4, 64, 8, 24)[..., :22]
        .transpose(2, 0, 3, 1)
        .reshape(704, 64)
    )
    grad_shared = back[:, 40:88].reshape(4, 2, 24, 512)[:, :, :22].astype(f32)
    grad_sharedgate = grad_shared[:, 0].reshape(88, 512).T
    grad_sharedup = grad_shared[:, 1].reshape(88, 512).T
    grad_expertgate = back[:, 88:176].astype(f32).reshape(352, 512)
    grad_expertup = back[:, 176:264].astype(f32).reshape(352, 512)
    grad_expertdown = back[:, 264:352].astype(f32).reshape(352, 512)

    pack = jnp.concatenate(
        [
            grad_wq.reshape(2, 96, 4, 512).transpose(2, 0, 1, 3).reshape(8, 96, 512),
            grad_wkv.reshape(2, 128, 4, 128).transpose(2, 0, 1, 3).reshape(8, 32, 512),
            grad_wlat.reshape(2, 18, 4, 512).transpose(2, 0, 1, 3).reshape(8, 18, 512),
            jnp.zeros((8, 6, 512), f32),
        ],
        axis=1,
    ).astype(bf16)
    pack = jnp.sum(exchange(pack, TOKEN).astype(f32), axis=0)
    pack = swap_row_token(pack)
    grad_wquery = pack[:96]
    grad_wkeyvalue = pack[96:128].reshape(128, 128).T
    grad_wlatent = pack[128:146].T

    return (
        output,
        loss_value,
        grad_states,
        small[:16],
        grad_wquery,
        grad_wlatent,
        small[160:164],
        grad_wkeyvalue,
        grad_woutput,
        small[16:32],
        small[32:160].reshape(16, 8),
        grad_sharedgate,
        grad_sharedup,
        grad_shareddown,
        grad_expertgate,
        grad_expertup,
        grad_expertdown,
    )


def solution(mesh):
    parts = Mesh(mesh.devices.reshape(2, 2, 4, 2, 4), ("xh", "co", "y", "xl", "z"))
    both = ROW + COL
    return jax.shard_map(
        shards,
        mesh=parts,
        in_specs=(
            P(COL, ROW),
            P(COL, ROW),
            P(ROW),
            P(COL, ROW),
            P(ROW, COL),
            P(ROW),
            P(ROW, COL),
            P(ROW, COL),
            P(ROW),
            P(ROW, None),
            P(ROW, COL),
            P(ROW, COL),
            P(ROW, COL),
            P(COL, ROW),
            P(COL, ROW),
            P(ROW, COL),
            P(COL, None),
            P(),
            P(),
        ),
        out_specs=(
            P(COL, ROW),
            P(),
            P(COL, ROW),
            P(both),
            P(COL, ROW),
            P(ROW, COL),
            P(both),
            P(ROW, COL),
            P(ROW, COL),
            P(both),
            P(both, None),
            P(ROW, COL),
            P(ROW, COL),
            P(ROW, COL),
            P(COL, ROW),
            P(COL, ROW),
            P(ROW, COL),
        ),
        check_vma=False,
    )
```

```python
import math

import jax
import jax.numpy as jnp
from jax import lax
from jax.sharding import Mesh, PartitionSpec as P

HEADS = 16
NOPE = 128
ROPE = 64
VDIM = 128
KV_RANK = 512
F = 1408
EXPERTS = 8
D = 2048

norm_epsilon = 1e-06
negative_fill = -1e30
rope_base = 10000.0

ROW = ("xh", "co")
COL = ("y", "xl", "z")
CHIPS = ("xh", "y")
WEIGHT = ("xh", "co", "y")
TOKEN = ("xl", "z")

bf16 = jnp.bfloat16
f32 = jnp.float32


def dot(spec, a, b):
    return jnp.einsum(spec, a, b, preferred_element_type=f32)


def exchange(x, axes):
    return lax.all_to_all(x, axes, 0, 0, tiled=True)


def spread(x, axes, n):
    return exchange(jnp.broadcast_to(x[None], (n,) + x.shape), axes)


def pieces(x, n):
    parts = []
    for _ in range(n):
        part = lax.reduce_precision(x, 8, 7)
        parts.append(part.astype(bf16))
        x = x - part
    return parts


def to_rows(vals, rows, n):
    flat = jnp.concatenate(pieces(vals, n), axis=1)
    flat = jnp.pad(flat, ((0, 0), (0, rows * 512 - flat.shape[1])))
    return flat.reshape(vals.shape[0], rows, 512)


def from_rows(rows, m, n):
    flat = rows.astype(f32).reshape(rows.shape[0], -1)
    return sum(flat[:, k * m : (k + 1) * m] for k in range(n))


def mate(x):
    return lax.ppermute(x, "co", [(0, 1), (1, 0)])


def first_core():
    return lax.axis_index("co") == 0


def gather_owners(x):
    own = spread(x, CHIPS, 8).reshape(2, 4, *x.shape)
    other = mate(own)
    pair = [jnp.where(first_core(), own, other), jnp.where(first_core(), other, own)]
    return jnp.stack(pair, axis=1).reshape(4, 4, *x.shape)


def sum_owners(partial, side=None):
    rows = partial.shape[2]

    def halves(x):
        x = x.reshape(2, 2, *x.shape[1:])
        return (
            jnp.where(first_core(), x[:, 0], x[:, 1]),
            jnp.where(first_core(), x[:, 1], x[:, 0]),
        )

    def packed(block, vals):
        block = block.astype(bf16).reshape(8, rows, 512)
        if side is None:
            return block
        return jnp.concatenate([block, to_rows(vals.reshape(8, -1), 8, 2)], axis=1)

    mine, theirs = halves(partial)
    side_mine, side_theirs = halves(side) if side is not None else (None, None)
    got = mate(packed(theirs, side_theirs))
    mine = mine.reshape(8, rows, 512) + got[:, :rows].astype(f32)
    if side is not None:
        m = side.shape[2]
        side_mine = side_mine.reshape(8, m) + from_rows(got[:, rows:], m, 2)
    got = exchange(packed(mine, side_mine), CHIPS)
    total = jnp.sum(got[:, :rows].astype(f32), axis=0)
    if side is None:
        return total
    return total, jnp.sum(from_rows(got[:, rows:], m, 2), axis=0)


def row_exchange(x):
    me = lax.axis_index("xh") * 2 + lax.axis_index("co")
    got = [lax.dynamic_index_in_dim(x, me, 0, keepdims=False)]
    for k in (1, 2, 3):
        block = lax.dynamic_index_in_dim(x, me ^ k, 0, keepdims=False)
        got.append(lax.ppermute(block, ROW, [(r, r ^ k) for r in range(4)]))
    got = jnp.stack(got)
    return jnp.stack(
        [lax.dynamic_index_in_dim(got, me ^ r, 0, keepdims=False) for r in range(4)]
    )


def swap_row_y(x):
    pairs = [(r * 4 + y, y * 4 + r) for r in range(4) for y in range(4)]
    return lax.ppermute(x, WEIGHT, pairs)


def swap_row_token(x):
    pairs = [
        (r * 8 + q * 2 + low, q * 8 + r * 2 + low)
        for r in range(4)
        for q in range(4)
        for low in range(2)
    ]
    return lax.ppermute(x, ROW + TOKEN, pairs)


def lanes_in(x):
    k = 512 // x.shape[-1]
    n = x.shape[-2] // k
    return jnp.concatenate([x[..., i * n : (i + 1) * n, :] for i in range(k)], axis=-1)


def lanes_out(x, width):
    return jnp.concatenate(
        [x[..., i * width : (i + 1) * width] for i in range(512 // width)], axis=-2
    )


def rotate_rows(v, cosine, sine):
    a, b = v[: ROPE // 2], v[ROPE // 2 :]
    return jnp.concatenate([a * cosine - b * sine, b * cosine + a * sine], axis=0)


def rotate_back_rows(g, cosine, sine):
    a, b = g[: ROPE // 2], g[ROPE // 2 :]
    return jnp.concatenate([a * cosine + b * sine, b * cosine - a * sine], axis=0)


def rope_angles(position):
    exponents = jnp.arange(ROPE // 2, dtype=f32) * (2.0 / ROPE)
    frequency = jnp.exp(-math.log(rope_base) * exponents)
    return frequency[:, None] * position.astype(f32)[None, :]


def places_of(lengths, places):
    seq_ends = jnp.cumsum(lengths)
    starts = jnp.concatenate([jnp.zeros((1,), jnp.int32), seq_ends])
    segment = jnp.sum((places[:, None] >= seq_ends[None, :]).astype(jnp.int32), axis=1)
    numbers = jnp.arange(seq_ends.shape[0] + 1, dtype=jnp.int32)
    begins = jnp.sum(jnp.where(segment[:, None] == numbers[None, :], starts[None, :], 0), axis=1)
    return begins, segment < lengths.shape[0]


def pad_latent(x):
    x = jnp.pad(x, ((0, 576 - x.shape[0]), (0, 0))).reshape(4, 4, 2, 18, -1)
    x = jnp.pad(x, ((0, 0), (0, 0), (0, 0), (0, 6), (0, 0)))
    return x.transpose(1, 0, 2, 3, 4).reshape(768, -1)


def unpad_latent(x):
    return x.reshape(4, 4, 2, 24, -1).transpose(1, 0, 2, 3, 4)[:, :, :, :18].reshape(576, -1)


def take_rope(x):
    x = x.reshape(4, 4, 2, 24, -1)
    return jnp.concatenate([x[2, 3, 0, 8:18], x[2, 3, 1, :18], x[3, 3, 0, :18], x[3, 3, 1, :18]], axis=0)


def put_rope(head, rope):
    head = head.reshape(4, 4, 2, 24, -1)
    gap = jnp.zeros((6, rope.shape[1]), rope.dtype)
    two = jnp.stack(
        [
            jnp.concatenate([head[2, 3, 0, :8], rope[:10], gap], axis=0),
            jnp.concatenate([rope[10:28], gap], axis=0),
        ]
    )
    three = jnp.stack(
        [
            jnp.concatenate([rope[28:46], gap], axis=0),
            jnp.concatenate([rope[46:64], gap], axis=0),
        ]
    )
    return jnp.concatenate(
        [
            head[:2].reshape(16 * 24, -1),
            head[2, :3].reshape(6 * 24, -1),
            two.reshape(48, -1),
            head[3, :3].reshape(6 * 24, -1),
            three.reshape(48, -1),
        ],
        axis=0,
    )


def shards(
    states,
    teacher,
    firstgain,
    wquery,
    wlatent,
    latentgain,
    wkeyvalue,
    woutput,
    secondgain,
    wrouter,
    sharedgate,
    sharedup,
    shareddown,
    expertgate,
    expertup,
    expertdown,
    routes,
    lengths,
    dealing,
):
    y_index = lax.axis_index("y")
    group = lax.axis_index("xl") * 4 + lax.axis_index("z")
    score_scale = (NOPE + ROPE) ** (-0.5)

    dealt = dealing.reshape(4, 8, 128)
    key_place = dealt.transpose(1, 0, 2).reshape(4096)
    place = lax.dynamic_index_in_dim(dealt, group, 1, keepdims=False).reshape(512)
    begin, valid = places_of(lengths, place)
    angles = rope_angles(place - begin)
    cosine, sine = jnp.cos(angles), jnp.sin(angles)
    own_valid = lax.dynamic_slice_in_dim(valid.astype(f32), y_index * 128, 128, 0)
    valid_count = jnp.sum(lengths).astype(f32)
    chosen_own = jnp.sum(
        (routes[:, :, None] == jnp.arange(EXPERTS, dtype=jnp.int32)[None, None, :]).astype(f32),
        axis=1,
    )

    extra = jnp.concatenate(
        [p[None] for p in pieces(firstgain, 3)]
        + [wrouter.T]
        + [jnp.pad(jnp.concatenate(pieces(latentgain, 3)), (0, 128))[None]]
        + [chosen_own.astype(bf16).reshape(2, 512)]
        + [jnp.zeros((2, 512), bf16)],
        axis=0,
    )
    first = gather_owners(jnp.concatenate([states, extra], axis=0))

    pack = jnp.concatenate(
        [wquery, lanes_in(wkeyvalue), wlatent.T, jnp.zeros((6, 512), bf16)], axis=0
    )
    pack = spread(swap_row_token(pack), TOKEN, 8).reshape(4, 2, 152, 512)
    wq = pack[:, :, :96].reshape(4, 192, 512)
    wkv = lanes_out(pack[:, :, 96:128], 128).transpose(0, 2, 1, 3).reshape(KV_RANK, 256)
    wkv = pad_latent(wkv)
    wlat = pack[:, :, 128:152].reshape(4, 48, 512)

    outs_pack = jnp.concatenate(
        [
            lanes_in(woutput.T.reshape(64, 4, 128).transpose(1, 0, 2)),
            lanes_in(
                jnp.pad(
                    jnp.pad(
                        shareddown.T.reshape(64, 8, 4, 22).transpose(2, 0, 1, 3),
                        ((0, 0), (0, 0), (0, 0), (0, 2)),
                    ).reshape(4, 64, 192),
                    ((0, 0), (0, 0), (0, 64)),
                )
            ),
        ],
        axis=1,
    )
    shared_pack = jnp.pad(
        jnp.stack([sharedgate.T, sharedup.T]).reshape(2, 4, 22, 512),
        ((0, 0), (0, 0), (0, 2), (0, 0)),
    ).transpose(1, 0, 2, 3)
    units = row_exchange(
        jnp.concatenate(
            [
                swap_row_y(outs_pack),
                shared_pack.reshape(4, 48, 512),
                expertgate.reshape(4, 88, 512),
                expertup.reshape(4, 88, 512),
                expertdown.reshape(4, 88, 512),
            ],
            axis=1,
        )
    )
    units = lax.all_gather(units.reshape(4 * 360, 512), TOKEN, axis=0, tiled=True)
    units = units.reshape(8, 4, 360, 512)

    def by_row(low, high):
        return units[:, :, low:high].transpose(1, 0, 2, 3).reshape(4, 8 * (high - low), 512)

    wo_t = lanes_out(units[:, :, :16], 128).transpose(1, 0, 2, 3).reshape(4, 512, 128)
    sd_t = lanes_out(units[:, :, 16:48], 256).transpose(1, 0, 2, 3).reshape(4, 512, 256)
    sd_t = sd_t[:, :, :192]
    wsg = by_row(48, 72)
    wsu = by_row(72, 96)
    wg = by_row(96, 184)
    wu = by_row(184, 272)
    wd = (
        units[:, :, 272:360]
        .reshape(2, 4, 352, 512)
        .transpose(1, 0, 2, 3)
        .reshape(4, 704, 512)
    )

    gain_in = jnp.sum(first[:, 0, 128:131].astype(f32), axis=1)
    router = first[:, 0, 131:139]
    rank_gain = pad_latent(
        jnp.sum(first[:, 0, 139, :384].astype(f32).reshape(4, 3, 128), axis=1).reshape(KV_RANK, 1)
    )
    chosen = first[0, :, 140:142].astype(f32).reshape(512, 8)
    wide = first[:, :, :128].reshape(4, 512, 512).astype(f32)
    inverse_one = lax.rsqrt(jnp.sum(wide * wide, axis=(0, 2)) / D + norm_epsilon)
    normed_in = (wide * inverse_one[None, :, None] * gain_in[:, None, :]).astype(bf16)
    query = dot("rod,rtd->ot", wq, normed_in)
    query = jnp.concatenate(
        [query[:NOPE], rotate_rows(query[NOPE:], cosine, sine)], axis=0
    ).astype(bf16)
    latent = gather_owners(dot("rcd,rtd->ct", wlat, normed_in)).reshape(768, 512)
    is_rank = jnp.logical_not(
        put_rope(jnp.zeros((768, 1), jnp.bool_), jnp.ones((ROPE, 1), jnp.bool_))
    )
    latent_head = jnp.where(is_rank, latent, 0.0)
    latent_inverse = lax.rsqrt(
        jnp.sum(latent_head * latent_head, axis=0) / KV_RANK + norm_epsilon
    )
    compressed = (latent_head * latent_inverse[None, :] * rank_gain).astype(bf16)
    keyvalue = dot("ro,rt->ot", wkv, compressed)
    rope_key = rotate_rows(take_rope(latent), cosine, sine)
    key_pack = spread(
        jnp.concatenate([keyvalue[:NOPE], rope_key, keyvalue[NOPE:]], axis=0).astype(bf16),
        TOKEN,
        8,
    )
    key_pack = key_pack.transpose(1, 0, 2).reshape(320, 4096)
    keys, values = key_pack[:192], key_pack[192:]

    allowed = (key_place[None, :] >= begin[:, None]) & (key_place[None, :] <= place[:, None])
    scores = jnp.where(allowed, dot("dt,ds->ts", query, keys) * score_scale, negative_fill)
    top = jnp.max(scores, axis=1, keepdims=True)
    weights = jnp.where(allowed, jnp.exp(scores - top), 0.0)
    total = jnp.sum(weights, axis=1, keepdims=True)
    probs = weights / total
    attended = dot("ts,ds->td", weights.astype(bf16), values) / total
    attn_in = attended.astype(bf16)
    partial = dot("td,rod->rto", attn_in, wo_t)
    mixed = states.astype(f32) + sum_owners(partial.reshape(4, 4, 128, 512))

    squares = to_rows(jnp.sum(mixed * mixed, axis=1)[None], 8, 3)[0]
    second = gather_owners(
        jnp.concatenate([(mixed * secondgain).astype(bf16), squares], axis=0)
    )
    squares = jnp.sum(from_rows(second[:, :, 128:].reshape(16, 8, 512), 128, 3).reshape(4, 512), axis=0)
    inverse_two = lax.rsqrt(squares / D + norm_epsilon)
    gained = second[:, :, :128].reshape(4, 512, 512)
    scale_two = inverse_two[:, None]

    logits = dot("rtd,red->te", gained, router) * scale_two
    routing = jax.nn.softmax(logits, axis=1)
    combine = routing * chosen
    combine_pair = lax.dynamic_slice_in_dim(combine, 2 * y_index, 2, 1)
    factor = jnp.broadcast_to(combine_pair[:, :, None], (512, 2, 352)).reshape(512, 704)
    gate_shared = dot("rtd,rfd->tf", gained, wsg) * scale_two
    up_shared = dot("rtd,rfd->tf", gained, wsu) * scale_two
    gate_routed = dot("rtd,rfd->tf", gained, wg) * scale_two
    up_routed = dot("rtd,rfd->tf", gained, wu) * scale_two
    sig_shared = jax.nn.sigmoid(gate_shared)
    sig_routed = jax.nn.sigmoid(gate_routed)
    silu_shared = gate_shared * sig_shared
    silu_routed = gate_routed * sig_routed
    act_routed = silu_routed * up_routed
    hidden_shared = (silu_shared * up_shared).astype(bf16)
    hidden_routed = (factor * act_routed).astype(bf16)
    branch = dot("tf,zfo->zto", hidden_routed, wd) + dot("tf,rof->rto", hidden_shared, sd_t)
    final = mixed + sum_owners(branch.reshape(4, 4, 128, 512))
    output = final.astype(bf16)

    difference = (final - teacher.astype(f32)) * own_valid[:, None]
    error_own = jnp.sum(difference * difference)
    grad_final = difference * (4096.0 / valid_count)
    grad_branch = gather_owners(grad_final.astype(bf16)).reshape(4, 512, 512)

    grad_down = dot("tf,zto->zfo", hidden_routed, grad_branch).astype(bf16)
    grad_sd = dot("rto,tf->rof", grad_branch, hidden_shared).astype(bf16)

    def sum_units(block):
        rows = block.shape[2]
        block = lax.psum_scatter(
            block.reshape(8 * 4 * rows, 512), TOKEN, scatter_dimension=0, tiled=True
        )
        return block.reshape(4, rows, 512)

    def by_token(block):
        return block.reshape(4, 8, -1, 512).transpose(1, 0, 2, 3)

    down_sum = sum_units(
        jnp.concatenate(
            [
                grad_down.reshape(4, 2, 4, 88, 512)
                .transpose(1, 0, 2, 3, 4)
                .reshape(8, 4, 88, 512),
                lanes_in(
                    jnp.pad(grad_sd, ((0, 0), (0, 0), (0, 64)))
                    .reshape(4, 8, 64, 256)
                    .transpose(1, 0, 2, 3)
                ),
            ],
            axis=2,
        )
    )
    grad_hidden_shared = dot("rto,rof->tf", grad_branch, sd_t)
    grad_hidden_routed = dot("rto,rfo->tf", grad_branch, wd)
    grad_combine = jnp.sum((grad_hidden_routed * act_routed).reshape(512, 2, 352), axis=2)
    grad_act = grad_hidden_routed * factor
    gate_slope = grad_hidden_shared * up_shared * sig_shared * (1.0 + gate_shared * (1.0 - sig_shared))
    up_slope = grad_hidden_shared * silu_shared
    gate_slope_routed = grad_act * up_routed * sig_routed * (1.0 + gate_routed * (1.0 - sig_routed))
    up_slope_routed = grad_act * silu_routed
    grad_mid = (
        dot("tf,rfd->rtd", gate_slope.astype(bf16), wsg)
        + dot("tf,rfd->rtd", up_slope.astype(bf16), wsu)
        + dot("tf,rfd->rtd", gate_slope_routed.astype(bf16), wg)
        + dot("tf,rfd->rtd", up_slope_routed.astype(bf16), wu)
    )
    inner_two = (inverse_two * jnp.sum(grad_mid * gained.astype(f32), axis=(0, 2))).reshape(4, 128)
    side = jnp.concatenate(
        [inner_two, grad_combine.reshape(4, 128, 2).transpose(0, 2, 1).reshape(4, 256)], axis=1
    )
    place_y = (jnp.arange(4) == y_index).astype(f32)
    side = jnp.concatenate(
        [side[:, :128], (side[:, None, 128:] * place_y[None, :, None]).reshape(4, 1024)], axis=1
    )
    grad_mid_own, side = sum_owners(
        grad_mid.reshape(4, 4, 128, 512), jnp.broadcast_to(side[None], (4, 4, 1152))
    )
    inner_own = side[:128]
    combine_own = side[128:].reshape(8, 128).T
    grad_units = [
        dot("tf,rtd->rfd", (slope * scale_two).astype(bf16), gained).astype(bf16)
        for slope in (gate_slope, up_slope, gate_slope_routed, up_slope_routed)
    ]
    unit_sum = sum_units(jnp.concatenate([by_token(g) for g in grad_units], axis=2))
    routing_own = lax.dynamic_slice_in_dim(routing, y_index * 128, 128, 0)
    logits_own = lax.dynamic_slice_in_dim(logits, y_index * 128, 128, 0)
    inverse_two_own = lax.dynamic_slice_in_dim(inverse_two, y_index * 128, 128, 0)[:, None]
    grad_routing = combine_own * chosen_own
    grad_logits = (
        routing_own
        * (grad_routing - jnp.sum(routing_own * grad_routing, axis=1, keepdims=True))
    ).astype(bf16)
    normed_mid_own = (mixed * inverse_two_own * secondgain).astype(bf16)
    grad_router = dot("td,te->de", normed_mid_own, grad_logits)
    grad_mid_own = grad_mid_own + dot("te,de->td", grad_logits, wrouter)
    inner_own = inner_own + jnp.sum(grad_logits.astype(f32) * logits_own, axis=1)
    grad_mixed = (
        grad_final
        + grad_mid_own * secondgain * inverse_two_own
        - mixed * (inverse_two_own * inverse_two_own * inner_own[:, None] / D)
    )
    grad_second = jnp.sum(grad_mid_own * mixed * inverse_two_own, axis=0)

    grad_attn = gather_owners(grad_mixed.astype(bf16)).reshape(4, 512, 512)
    grad_attended = dot("rto,rod->td", grad_attn, wo_t).astype(bf16)
    grad_wo = dot("rto,td->rod", grad_attn, attn_in).astype(bf16)
    delta = jnp.sum(grad_attended.astype(f32) * attended, axis=1, keepdims=True)
    grad_probs = dot("td,ds->ts", grad_attended, values)
    grad_scores = (probs * (grad_probs - delta)).astype(bf16)
    grad_query = dot("ds,ts->dt", keys, grad_scores) * score_scale
    grad_keys = dot("dt,ts->ds", query, grad_scores) * score_scale
    grad_values = dot("td,ts->ds", grad_attended, probs.astype(bf16))
    grad_kv = jnp.concatenate([grad_keys, grad_values], axis=0).astype(bf16)
    grad_kv = exchange(grad_kv.reshape(320, 8, 512).transpose(1, 0, 2), TOKEN)
    grad_kv = jnp.sum(grad_kv.astype(f32), axis=0)
    grad_rope = rotate_back_rows(grad_kv[NOPE : NOPE + ROPE], cosine, sine)
    grad_keyvalue = jnp.concatenate([grad_kv[:NOPE], grad_kv[NOPE + ROPE :]], axis=0).astype(bf16)
    grad_wkv = dot("rt,ot->ro", compressed, grad_keyvalue)
    grad_compressed = dot("ro,ot->rt", wkv, grad_keyvalue)
    scaled = grad_compressed * rank_gain
    inner_rank = jnp.sum(scaled * latent_head, axis=0)
    grad_rank_gain = jnp.sum(grad_compressed * latent_head * latent_inverse[None, :], axis=1)
    grad_rank_gain = unpad_latent(grad_rank_gain[:, None])[:KV_RANK].reshape(4, 128)
    grad_latent = put_rope(
        scaled * latent_inverse[None, :]
        - latent_head
        * (latent_inverse * latent_inverse * latent_inverse * inner_rank / KV_RANK)[None, :],
        grad_rope,
    )
    grad_latent = sum_owners(grad_latent.reshape(4, 4, 48, 512)).astype(bf16)
    grad_query = jnp.concatenate(
        [grad_query[:NOPE], rotate_back_rows(grad_query[NOPE:], cosine, sine)], axis=0
    ).astype(bf16)
    grad_wq = dot("ot,rtd->rod", grad_query, normed_in)
    grad_wlat = dot("ct,rtd->rcd", grad_latent, normed_in)
    grad_in = dot("ot,rod->rtd", grad_query, wq) + dot("ct,rcd->rtd", grad_latent, wlat)
    inner_one = jnp.sum(grad_in * normed_in.astype(f32), axis=(0, 2)).reshape(4, 128)
    side = jnp.concatenate(
        [
            jnp.broadcast_to(inner_one[None], (4, 4, 128)),
            jnp.broadcast_to(grad_rank_gain[:, None], (4, 4, 128)),
            jnp.broadcast_to(error_own, (4, 4, 1)),
        ],
        axis=2,
    )
    grad_in_own, side = sum_owners(grad_in.reshape(4, 4, 128, 512), side)
    own_wide = states.astype(f32)
    inverse_own = lax.dynamic_slice_in_dim(inverse_one, y_index * 128, 128, 0)[:, None]
    grad_states = (
        grad_mixed
        + grad_in_own * firstgain * inverse_own
        - own_wide * (inverse_own * inverse_own * side[:128, None] / D)
    )
    grad_first = jnp.sum(grad_in_own * own_wide * inverse_own, axis=0)

    small = jnp.concatenate(
        [
            grad_first.reshape(32, 16),
            grad_second.reshape(32, 16),
            grad_router.reshape(32, 128),
            0.25 * side[128:256].reshape(32, 4),
            jnp.broadcast_to(0.25 * side[256], (32, 1)),
            jnp.zeros((32, 91), f32),
        ],
        axis=1,
    )
    small = jnp.sum(exchange(small, COL), axis=0)
    loss_value = small[164] / (valid_count * D)

    pack = jnp.concatenate(
        [
            grad_wq.reshape(8, 96, 512),
            lanes_in(
                unpad_latent(grad_wkv)[:KV_RANK]
                .reshape(4, 128, 2, 128)
                .transpose(0, 2, 1, 3)
                .reshape(8, 128, 128)
            ),
            grad_wlat.reshape(8, 24, 512),
            lanes_in(grad_wo.reshape(4, 8, 64, 128).transpose(1, 0, 2, 3)).reshape(8, 64, 512),
        ],
        axis=1,
    ).astype(bf16)
    pack = jnp.sum(exchange(pack, TOKEN).astype(f32), axis=0)
    wo_sum = pack[152:].astype(bf16).reshape(4, 16, 512)
    pack = swap_row_token(pack[:152])
    grad_wquery = pack[:96]
    grad_wkeyvalue = lanes_out(pack[96:128], 128)
    grad_wlatent = pack[128:146].T

    wo_sum = swap_row_y(row_exchange(wo_sum)).astype(f32)
    grad_woutput = lanes_out(wo_sum, 128).transpose(0, 2, 1).reshape(512, 64)
    down_sum = row_exchange(down_sum)
    grad_expertdown = down_sum[:, :88].astype(f32).reshape(352, 512)
    sd_sum = lanes_out(swap_row_y(down_sum[:, 88:]), 256)[:, :, :192].astype(f32)
    grad_shareddown = (
        sd_sum.reshape(4, 64, 8, 24)[..., :22].transpose(2, 0, 3, 1).reshape(704, 64)
    )
    unit_sum = row_exchange(unit_sum).astype(f32)
    grad_sharedgate = unit_sum[:, :22].reshape(88, 512).T
    grad_sharedup = unit_sum[:, 24:46].reshape(88, 512).T
    grad_expertgate = unit_sum[:, 48:136].reshape(352, 512)
    grad_expertup = unit_sum[:, 136:224].reshape(352, 512)

    return (
        output,
        loss_value,
        grad_states,
        small[:16],
        grad_wquery,
        grad_wlatent,
        small[160:164],
        grad_wkeyvalue,
        grad_woutput,
        small[16:32],
        small[32:160].reshape(16, 8),
        grad_sharedgate,
        grad_sharedup,
        grad_shareddown,
        grad_expertgate,
        grad_expertup,
        grad_expertdown,
    )


def solution(mesh):
    parts = Mesh(mesh.devices.reshape(2, 2, 4, 2, 4), ("xh", "co", "y", "xl", "z"))
    both = ROW + COL
    return jax.shard_map(
        shards,
        mesh=parts,
        in_specs=(
            P(COL, ROW),
            P(COL, ROW),
            P(ROW),
            P(COL, ROW),
            P(ROW, COL),
            P(ROW),
            P(ROW, COL),
            P(ROW, COL),
            P(ROW),
            P(ROW, None),
            P(ROW, COL),
            P(ROW, COL),
            P(ROW, COL),
            P(COL, ROW),
            P(COL, ROW),
            P(ROW, COL),
            P(COL, None),
            P(),
            P(),
        ),
        out_specs=(
            P(COL, ROW),
            P(),
            P(COL, ROW),
            P(both),
            P(COL, ROW),
            P(ROW, COL),
            P(both),
            P(ROW, COL),
            P(ROW, COL),
            P(both),
            P(both, None),
            P(ROW, COL),
            P(ROW, COL),
            P(ROW, COL),
            P(COL, ROW),
            P(COL, ROW),
            P(ROW, COL),
        ),
        check_vma=False,
    )
```

```python
import math

import jax
import jax.numpy as jnp
import numpy as np
from jax import lax
from jax.experimental import pallas as pl
from jax.experimental.pallas import tpu as pltpu
from jax.sharding import Mesh, PartitionSpec as P

HEADS = 16
NOPE = 128
ROPE = 64
VDIM = 128
KV_RANK = 512
F = 1408
EXPERTS = 8
D = 2048

norm_epsilon = 1e-06
negative_fill = -1e30
rope_base = 10000.0

ROW = ("xh", "co")
COL = ("y", "xl", "z")
CHIPS = ("xh", "y")
WEIGHT = ("xh", "co", "y")
TOKEN = ("xl", "z")

bf16 = jnp.bfloat16
f32 = jnp.float32


def dot(spec, a, b):
    return jnp.einsum(spec, a, b, preferred_element_type=f32)


def exchange(x, axes):
    return lax.all_to_all(x, axes, 0, 0, tiled=True)


def spread(x, axes, n):
    return exchange(jnp.broadcast_to(x[None], (n,) + x.shape), axes)


def pieces(x, n):
    parts = []
    for _ in range(n):
        part = lax.reduce_precision(x, 8, 7)
        parts.append(part.astype(bf16))
        x = x - part
    return parts


def to_rows(vals):
    return jnp.concatenate(pieces(vals, 2), axis=-2)


def from_rows(rows):
    rows = rows.astype(f32)
    return rows[..., :4, :] + rows[..., 4:8, :]


def after(x):
    return (x[(0,) * x.ndim].astype(f32) * 0.0).astype(jnp.int32)


def behind(x, zero):
    return jnp.where(zero == 0, x, jnp.zeros_like(x))


def mate(x):
    return lax.ppermute(x, "co", [(0, 1), (1, 0)])


def core_pick(zero, one):
    return jnp.where(lax.axis_index("co") == 0, zero, one)


def xh_pick(zero, one, later=0):
    return jnp.where(lax.axis_index("xh") + later == 0, zero, one)


def gather_owners(x):
    own = spread(x, CHIPS, 8).reshape(2, 4, *x.shape)
    return own, mate(own)


def sum_owners(mine, theirs, side=None, raw=False):
    rows = mine.shape[2]

    def packed(block, vals):
        block = block.astype(bf16).reshape(8, rows, 512)
        return block if side is None else jnp.concatenate([block, to_rows(vals)], axis=1)

    got = mate(packed(theirs, None if side is None else side[1]))
    mine = mine.reshape(8, rows, 512) + got[:, :rows].astype(f32)
    vals = None if side is None else side[0] + from_rows(got[:, rows:])
    ready = packed(mine, vals)
    got = exchange(ready, CHIPS)
    if raw:
        return got
    total = jnp.sum(got[:, :rows].astype(f32), axis=0)
    if side is None:
        return total
    return total, jnp.sum(from_rows(got[:, rows:]), axis=0), after(ready)


def other_xl(x):
    return lax.ppermute(x, "xl", [(0, 1), (1, 0)])


def xl_pick(zero, one):
    return jnp.where(lax.axis_index("xl") == 0, zero, one)


def xl_order(x, axis):
    return xl_pick(x, jnp.flip(x, axis))


def z_first(x):
    return jnp.swapaxes(x.reshape(2, 4, *x.shape[1:]), 0, 1)


def along_z(x):
    z, xl, n, m = x.shape
    x = lax.psum_scatter(x.reshape(8 * n, m), "z", scatter_dimension=0, tiled=True)
    return x.reshape(2, n, m)


def along_xl(x, later):
    return (x[0].astype(f32) + behind(other_xl(x[1]), later).astype(f32)).astype(bf16)


def row_permute(block, k):
    return lax.ppermute(block, ROW, [(r, r ^ k) for r in range(4)])


def row_scatter(x, start=0, end=0):
    me = lax.axis_index("xh") * 2 + lax.axis_index("co") + start
    got = [lax.dynamic_index_in_dim(x, me, 0, keepdims=False)]
    for k in (1, 2, 3):
        got.append(row_permute(lax.dynamic_index_in_dim(x, me ^ k, 0, keepdims=False), k))
    return jnp.stack(
        [
            jnp.stack([xh_pick(got[k], got[k + 2], end), xh_pick(got[k + 2], got[k], end)])
            for k in (0, 1)
        ]
    )


def row_return(x):
    got = []
    for k in range(4):
        near, far = x[k % 2, 0], x[k % 2, 1]
        block = xh_pick(near, far) if k < 2 else xh_pick(far, near)
        got.append(row_permute(block, k) if k else block)
    me = lax.axis_index("xh") * 2 + lax.axis_index("co")
    got = jnp.stack(got)
    return jnp.stack(
        [lax.dynamic_index_in_dim(got, me ^ r, 0, keepdims=False) for r in range(4)]
    )


def swap_row_y(x):
    pairs = [(r * 4 + y, y * 4 + r) for r in range(4) for y in range(4)]
    return lax.ppermute(x, WEIGHT, pairs)


def swap_row_z(x):
    pairs = [(r * 4 + z, z * 4 + r) for r in range(4) for z in range(4)]
    return lax.ppermute(x, ROW + ("z",), pairs)


def head_pairs():
    pairs = []
    for n in range(32):
        xh, co, xl, hi, lo = n >> 4, n >> 3 & 1, n >> 2 & 1, n >> 1 & 1, n & 1
        source = hi << 4 | (co ^ xl) << 3 | xh << 2 | co << 1 | lo
        pairs.append((source, n))
    return pairs


def to_head(x):
    return lax.ppermute(x, ROW + TOKEN, head_pairs())


def from_head(x):
    return lax.ppermute(x, ROW + TOKEN, [(b, a) for a, b in head_pairs()])


def lanes_in(x):
    k = 512 // x.shape[-1]
    n = x.shape[-2] // k
    return jnp.concatenate([x[..., i * n : (i + 1) * n, :] for i in range(k)], axis=-1)


def lanes_out(x, width):
    return jnp.concatenate(
        [x[..., i * width : (i + 1) * width] for i in range(512 // width)], axis=-2
    )


def rotate_rows(v, cosine, sine):
    a, b = v[: ROPE // 2], v[ROPE // 2 :]
    return jnp.concatenate([a * cosine - b * sine, b * cosine + a * sine], axis=0)


def rotate_back_rows(g, cosine, sine):
    a, b = g[: ROPE // 2], g[ROPE // 2 :]
    return jnp.concatenate([a * cosine + b * sine, b * cosine - a * sine], axis=0)


def rope_angles(position):
    exponents = jnp.arange(ROPE // 2, dtype=f32) * (2.0 / ROPE)
    frequency = jnp.exp(-math.log(rope_base) * exponents)
    return frequency[:, None] * position.astype(f32)[None, :]


def product(a, b, left=1, right=0):
    return lax.dot_general(a, b, (((left,), (right,)), ((), ())), preferred_element_type=f32)


def kernel_call(body, outs, args, flops, scratch=(), scalars=(), anchors=()):
    moved = sum(x.size * x.dtype.itemsize for x in list(args) + list(outs))
    vmem, smem = pl.BlockSpec(memory_space=pltpu.VMEM), pl.BlockSpec(memory_space=pltpu.SMEM)
    used = len(scalars) + len(args)

    def without_anchors(*refs):
        body(*refs[:used], *refs[used + len(anchors) :])

    return pl.pallas_call(
        without_anchors,
        out_shape=outs,
        in_specs=[smem] * len(scalars)
        + [vmem] * len(args)
        + [pl.BlockSpec(memory_space=pl.ANY)] * len(anchors),
        out_specs=[vmem] * len(outs),
        scratch_shapes=list(scratch),
        compiler_params=pltpu.CompilerParams(vmem_limit_bytes=48 * 2**20),
        cost_estimate=pl.CostEstimate(flops=flops, bytes_accessed=moved, transcendentals=0),
    )(*scalars, *args, *anchors)


SCORE_SCALE = (NOPE + ROPE) ** (-0.5)


def attend_body(query, key_pack, key_place, begin, place, wo_t, mine, theirs, attended, log_total):
    def block(b, state):
        top, total, acc = state
        keys, values = key_pack[b, :192, :], key_pack[b, 192:, :]
        scores = product(keys, query[...], 0, 0) * SCORE_SCALE
        at = key_place[b]
        allowed = (at >= begin[...]) & (at <= place[...])
        scores = jnp.where(allowed, scores, negative_fill)
        new_top = jnp.maximum(top, jnp.max(scores, axis=0, keepdims=True))
        weights = jnp.where(allowed, jnp.exp(scores - new_top), 0.0)
        factor = jnp.exp(top - new_top)
        total = total * factor + jnp.sum(weights, axis=0, keepdims=True)
        acc = acc * factor + product(values, weights.astype(bf16))
        return new_top, total, acc

    top, total, acc = lax.fori_loop(
        0,
        8,
        block,
        (
            jnp.full((1, 512), negative_fill, f32),
            jnp.zeros((1, 512), f32),
            jnp.zeros((VDIM, 512), f32),
        ),
    )
    result = acc / total
    attended[...] = result
    log_total[...] = top + jnp.log(total)
    attn_in = result.T.astype(bf16)
    for q in range(4):
        part = product(attn_in, wo_t[q], 1, 1)
        if q < 2:
            mine[q] = part
        else:
            theirs[q - 2] = part.astype(bf16)


def attend_back_body(
    this_xl, own, other, wo_t, query, key_pack, key_place, begin, place, attended, log_total, cosine,
    sine, normed_in, grad_shared_down,
    grad_kv, grad_query, outs_rows,
):
    attn_in = attended[...].astype(bf16)
    for q in range(4):
        grad = own[q] if q < 2 else other[q - 2]
        part = product(grad, attn_in, 0, 1).astype(bf16)
        for c in range(8):
            xl, z = c // 4, c % 4
            for k in range(4):
                at = c * 64 + k * 16
                lanes = slice(k * 128, k * 128 + 128)
                outs_rows[z, xl ^ this_xl[0], q * 16 : q * 16 + 16, lanes] = part[at : at + 16]
            rows = slice(64 + q * 32, 96 + q * 32)
            outs_rows[z, xl ^ this_xl[0], rows, :] = grad_shared_down[q, c]
    grad = product(own[0], wo_t[0]) + product(own[1], wo_t[1])
    grad = grad + product(other[0], wo_t[2]) + product(other[1], wo_t[3])
    grad = grad.T.astype(bf16)
    delta = jnp.sum(grad.astype(f32) * attended[...], axis=0, keepdims=True)

    def block(b, acc):
        keys, values = key_pack[b, :192, :], key_pack[b, 192:, :]
        scores = product(keys, query[...], 0, 0) * SCORE_SCALE
        at = key_place[b]
        allowed = (at >= begin[...]) & (at <= place[...])
        probs = jnp.where(allowed, jnp.exp(scores - log_total[...]), 0.0)
        grad_probs = product(values, grad, 0, 0)
        grad_scores = (probs * (grad_probs - delta)).astype(bf16)
        grad_kv[b, :192, :] = (product(query[...], grad_scores, 1, 1) * SCORE_SCALE).astype(bf16)
        grad_kv[b, 192:, :] = product(grad, probs.astype(bf16), 1, 1).astype(bf16)
        return acc + product(keys, grad_scores)

    acc = lax.fori_loop(0, 8, block, jnp.zeros((192, 512), f32)) * SCORE_SCALE
    a, b = acc[NOPE : NOPE + 32], acc[NOPE + 32 :]
    grad_query[:NOPE, :] = acc[:NOPE].astype(bf16)
    grad_query[NOPE:, :] = jnp.concatenate(
        [a * cosine[...] + b * sine[...], b * cosine[...] - a * sine[...]], axis=0
    ).astype(bf16)
    for q in range(4):
        part = product(grad_query[...], normed_in[q]).astype(bf16)
        for low in range(2):
            rows = part[low * 96 : low * 96 + 96]
            outs_rows[q % 2 * 2 + low, q // 2 ^ this_xl[0], 192:, :] = rows


def latent_back_body(
    core, got, cosine, sine, wkv, latent_head, latent_inverse, rank_gain, rope_rows, grad_query, wq,
    wlat_all, normed_in, gain_rows, gain,
    mine, theirs, grad_keyvalue, grad_latent, late,
    wlat,
):
    for side in range(2):
        for n in range(8):
            source = (n // 4) * 8 + (core[0] ^ side) * 4 + n % 4
            at = side * 384 + n * 48
            for q in range(4):
                wlat[q, at : at + 48, :] = wlat_all[source, q ^ (2 * side), :, :]
    total = got[0].astype(f32)
    for b in range(1, 8):
        total = total + got[b].astype(f32)
    a, b = total[NOPE : NOPE + 32], total[NOPE + 32 : NOPE + ROPE]
    grad_rope = jnp.concatenate(
        [a * cosine[...] + b * sine[...], b * cosine[...] - a * sine[...]], axis=0
    ).astype(bf16)
    grad = jnp.concatenate([total[:NOPE], total[NOPE + ROPE :]], axis=0).astype(bf16)
    grad_keyvalue[...] = grad
    grad_compressed = product(wkv[...], grad)
    lat, inv = latent_head[...], latent_inverse[...]
    scaled = grad_compressed * rank_gain[...]
    inner_rank = jnp.sum(scaled * lat, axis=0, keepdims=True)
    gain_sum = jnp.sum(grad_compressed * lat * inv, axis=1, keepdims=True)
    gain_row = jnp.broadcast_to(gain_sum, (768, 128)).T[:8]
    gain_high = gain_row.astype(bf16)
    gain_low = (gain_row - gain_high.astype(f32)).astype(bf16)
    unpad = lax.broadcasted_iota(jnp.int32, (768, 2048), 0) == gain_rows[...]
    unpad = unpad.astype(f32).astype(bf16)
    gain_row = product(gain_high, unpad) + product(gain_low, unpad)
    result = scaled * inv - lat * (inv * inv * inv * inner_rank / KV_RANK)
    result = (result + product(rope_rows[...], grad_rope)).astype(bf16)
    grad_latent[...] = result
    inner_sum = jnp.zeros((512, 1), f32)
    firsts = []
    for q in range(4):
        part = product(grad_query[...], wq[q], 0, 0) + product(result, wlat[q], 0, 0)
        if q < 2:
            mine[q] = part
        else:
            theirs[q - 2] = part.astype(bf16)
        weighted = part * normed_in[q].astype(f32)
        inner_sum = inner_sum + jnp.sum(weighted, axis=1, keepdims=True)
        firsts.append(jnp.sum(weighted, axis=0, keepdims=True) / gain[q : q + 1, :])
    inner = jnp.broadcast_to(inner_sum, (512, 128)).T[:1]
    late[...] = jnp.zeros((16, 4, 512), f32)
    for q in range(4):
        for y in range(4):
            at = q * 4 + y
            late[at, :1, :128] = inner[:, y * 128 : y * 128 + 128]
            late[at, :1, 128:256] = firsts[q][:, y * 128 : y * 128 + 128]
            late[at, :1, 384:512] = gain_row[:1, at * 128 : at * 128 + 128]


def fill_features(x2, parts):
    for side, part in enumerate(parts):
        for xh in range(2):
            at = side * 1024 + xh * 512
            for y in range(4):
                x2[y * 128 : y * 128 + 128, at : at + 512] = part[xh * 4 + y, :128, :]


def experts_body(
    own, other, units_own, units_beside, shared_down, router, chosen, first_expert, second_expert,
    mine, theirs, x2, inner, hidden_routed, hidden_shared, logits, routing, factors, inverse,
    routed, shared,
):
    fill_features(x2, (own, other))
    squares = []
    for y in range(4):
        total = jnp.zeros((1, 128), f32)
        for part in (own, other):
            for xh in range(2):
                rows = part[xh * 4 + y, 128:144, :].astype(f32)
                total = total + (rows[:1, :128] + rows[4:5, :128])
        squares.append(total)
    inv = lax.rsqrt(jnp.concatenate(squares, axis=1) / D + norm_epsilon)
    inverse[...] = inv
    scores = product(router[...], x2[...], 1, 1) * inv
    logits[...] = scores
    scores = jnp.exp(scores - jnp.max(scores, axis=0, keepdims=True))
    scores = scores / jnp.sum(scores, axis=0, keepdims=True)
    routing[...] = scores
    combine = scores * chosen[...]
    factors[:1, :] = jnp.sum(combine * first_expert[...], axis=0, keepdims=True)
    factors[1:, :] = jnp.sum(combine * second_expert[...], axis=0, keepdims=True)

    for p, units in enumerate((units_own, units_beside)):

        def block(z, carry, p=p, units=units):
            t = 2 * z + p
            h = product(units[z, :224, :], x2[...], 1, 1) * inv
            inner[t] = h
            gate, up = h[:112], h[112:]
            act = gate * jax.nn.sigmoid(gate) * up
            hidden = act[:88] * factors[p : p + 1, :]
            hidden = jnp.concatenate([hidden, jnp.zeros((8, 512), f32)], axis=0)
            routed[p, z] = hidden
            hidden_routed[t] = hidden.astype(bf16)
            shared[t] = act[88:]
            return carry

        lax.fori_loop(0, 4, block, 0)
    by_token = [routed[p].reshape(384, 512).T.astype(bf16) for p in range(2)]
    by_unit = shared[...].reshape(192, 512)
    hidden_shared[...] = by_unit.astype(bf16)
    shared_by_token = by_unit.T.astype(bf16)
    for q in range(4):
        at = q * 512
        part = product(shared_by_token, shared_down[:, at : at + 512])
        for p, units in enumerate((units_own, units_beside)):
            part = part + product(by_token[p], units[:, 224:, at : at + 512].reshape(384, 512))
        if q < 2:
            mine[q] = part
        else:
            theirs[q - 2] = part.astype(bf16)


def down_back_body(own, other, hidden_routed, hidden_shared, grad2, grad_down, grad_shared_down):
    fill_features(grad2, (own, other))
    grad_shared_down[...] = jnp.zeros((4, 8, 32, 512), bf16)
    for q in range(4):
        at = q * 512
        part = product(hidden_routed[...], grad2[:, at : at + 512])
        grad_down[:, at : at + 512] = part.astype(bf16)
        part = product(grad2[:, at : at + 512], hidden_shared[...], 0, 1).astype(bf16)
        for c in range(8):
            for k in range(2):
                at = c * 64 + k * 32
                grad_shared_down[q, c, :, k * 256 : k * 256 + 192] = part[at : at + 32]


def experts_back_body(
    grad2, units_own, units_beside, shared_down, inner, factors, inverse, x2, expert_place,
    mine, theirs, scaled, side,
    slopes, by_token, grad_shared,
):
    side[...] = jnp.zeros((4, 4, 512), f32)
    grad_shared[...] = product(shared_down[...], grad2[...], 1, 1).reshape(8, 24, 512)
    inv = inverse[...]
    for p, units in enumerate((units_own, units_beside)):
        factor = factors[p : p + 1, :]

        def block(z, reached, p=p, units=units, factor=factor):
            t = 2 * z + p
            grad = product(units[z, 224:, :], grad2[...], 1, 1)[:88]
            gate, up = inner[t, :112, :], inner[t, 112:, :]
            sig = jax.nn.sigmoid(gate)
            silu = gate * sig
            reached = reached + jnp.sum(grad * (silu * up)[:88], axis=0, keepdims=True)
            grad = jnp.concatenate([grad * factor, grad_shared[t]], axis=0)
            gate_slope = grad * up * sig * (1.0 + gate * (1.0 - sig))
            up_slope = grad * silu
            slopes[p, z, :112, :] = gate_slope.astype(bf16)
            slopes[p, z, 112:, :] = up_slope.astype(bf16)
            scaled[t, :112, :] = (gate_slope * inv).astype(bf16)
            scaled[t, 112:, :] = (up_slope * inv).astype(bf16)
            return reached

        reached = lax.fori_loop(0, 4, block, jnp.zeros((1, 512), f32))
        for y in range(4):
            part = reached[:, y * 128 : y * 128 + 128]
            part = jnp.concatenate([part] * 4, axis=1)
            side[y, 1:3, :] += part * expert_place[p]
        by_token[p] = slopes[p].reshape(896, 512).T
    total = jnp.zeros((512, 1), f32)
    for q in (2, 3, 0, 1):
        at = q * 512
        part = product(by_token[0], units_own[:, :224, at : at + 512].reshape(896, 512))
        part = part + product(by_token[1], units_beside[:, :224, at : at + 512].reshape(896, 512))
        if q < 2:
            mine[q] = part
        else:
            theirs[q - 2] = part.astype(bf16)
        part = part * x2[:, at : at + 512].astype(f32)
        total = total + jnp.sum(part, axis=1, keepdims=True)
    inner_sum = jnp.broadcast_to(total, (512, 128)).T[:1] * inv
    for y in range(4):
        side[y, :1, :128] = inner_sum[:, y * 128 : y * 128 + 128]


def last_body(got, wkv_rows, normed_in, grad_own, side, pack):
    total = got[0].astype(f32)
    for k in range(1, 8):
        total = total + got[k].astype(f32)
    grad_own[...] = total[:128]
    sums = total[176:180] + total[180:184]
    side[...] = sums
    high = sums.astype(bf16)
    low = (sums - high.astype(f32)).astype(bf16)
    rows = jnp.concatenate([high.astype(f32), low.astype(f32), jnp.zeros((8, 512), f32)], axis=0)
    rows = rows.astype(bf16)
    grad_latent = total[128:176].astype(bf16)
    for q in range(4):
        part = product(grad_latent, normed_in[q])
        for half in range(2):
            t = q * 2 + half
            pack[t, :32, :] = wkv_rows[t]
            entry = part[half * 24 : half * 24 + 24]
            entry = jnp.concatenate([entry, jnp.zeros((8, 512), f32)], axis=0)
            pack[t, 32:64, :] = entry.astype(bf16)
            pack[t, 64:, :] = rows


def places_of(lengths, places):
    seq_ends = jnp.cumsum(lengths)
    starts = jnp.concatenate([jnp.zeros((1,), jnp.int32), seq_ends])
    segment = jnp.sum((places[:, None] >= seq_ends[None, :]).astype(jnp.int32), axis=1)
    numbers = jnp.arange(seq_ends.shape[0] + 1, dtype=jnp.int32)
    begins = jnp.sum(jnp.where(segment[:, None] == numbers[None, :], starts[None, :], 0), axis=1)
    return begins, segment < lengths.shape[0]


def pad_latent(x):
    x = jnp.pad(x, ((0, 576 - x.shape[0]), (0, 0))).reshape(4, 2, 2, 2, 18, -1)
    x = jnp.pad(x, ((0, 0), (0, 0), (0, 0), (0, 0), (0, 6), (0, 0)))
    x = x.transpose(2, 1, 0, 3, 4, 5).reshape(2, 384, -1)
    return jnp.concatenate([core_pick(x[0], x[1]), core_pick(x[1], x[0])], axis=0)


def unpad_latent(x):
    x = x.reshape(2, 384, -1)
    x = jnp.stack([core_pick(x[0], x[1]), core_pick(x[1], x[0])])
    return x.reshape(2, 2, 4, 2, 24, -1)[:, :, :, :, :18].transpose(2, 1, 0, 3, 4, 5).reshape(576, -1)


def gain_row_table(core):
    table = np.full((16, 128), -1, np.int32)
    for side, xh, y, n in np.ndindex(2, 2, 4, 32):
        entry = (xh * 2 + (core ^ side)) * 128 + y * 32 + n
        block, column = divmod(entry, 18)
        source_y, source_row, half = block // 8, block // 2 % 4, block % 2
        near = (source_row % 2 ^ core) * 2 + source_row // 2
        table[(side * 2 + xh) * 4 + y, n] = (near * 4 + source_y) * 48 + half * 24 + column
    return jnp.asarray(table.reshape(1, 2048))


def take_rope(x):
    x = x.reshape(2, 2, 4, 48, -1)[:, 1, 3]
    two, three = core_pick(x[0], x[1]), core_pick(x[1], x[0])
    return jnp.concatenate([two[8:18], two[24:42], three[:18], three[24:42]], axis=0)


def put_rope(head, rope):
    head = head.reshape(2, 384, -1)
    gap = jnp.zeros((6, rope.shape[1]), rope.dtype)
    first = core_pick(head[0, 336:344], head[1, 336:344])
    two = jnp.concatenate([first, rope[:10], gap, rope[10:28], gap], axis=0)
    three = jnp.concatenate([rope[28:46], gap, rope[46:64], gap], axis=0)
    return jnp.concatenate(
        [head[0, :336], core_pick(two, three), head[1, :336], core_pick(three, two)], axis=0
    )


def shards(
    states,
    teacher,
    firstgain,
    wquery,
    wlatent,
    latentgain,
    wkeyvalue,
    woutput,
    secondgain,
    wrouter,
    sharedgate,
    sharedup,
    shareddown,
    expertgate,
    expertup,
    expertdown,
    routes,
    lengths,
    dealing,
):
    y_index = lax.axis_index("y")
    xl_index = lax.axis_index("xl")
    group = lax.axis_index("xl") * 4 + lax.axis_index("z")
    dealt = dealing.reshape(4, 8, 128)
    key_place = dealt.transpose(1, 0, 2).reshape(4096)
    place = lax.dynamic_index_in_dim(dealt, group, 1, keepdims=False).reshape(512)
    begin, valid = places_of(lengths, place)
    angles = rope_angles(place - begin)
    cosine, sine = jnp.cos(angles), jnp.sin(angles)
    own_valid = lax.dynamic_slice_in_dim(valid.astype(f32), y_index * 128, 128, 0)
    valid_count = jnp.sum(lengths).astype(f32)
    chosen_own = jnp.sum(
        (routes[:, :, None] == jnp.arange(EXPERTS, dtype=jnp.int32)[None, None, :]).astype(f32),
        axis=1,
    )

    extra = jnp.concatenate(
        [p[None] for p in pieces(firstgain, 3)]
        + [wrouter.T]
        + [jnp.pad(jnp.concatenate(pieces(latentgain, 3)), (0, 128))[None]]
        + [chosen_own.astype(bf16).reshape(2, 512)]
        + [jnp.zeros((2, 512), bf16)],
        axis=0,
    )
    first = gather_owners(jnp.concatenate([states, extra], axis=0))
    states_here = after(first[0])

    pack = jnp.concatenate(
        [wquery, lanes_in(wkeyvalue), wlatent.T, jnp.zeros((6, 512), bf16)], axis=0
    )
    pack = spread(to_head(pack), TOKEN, 8).reshape(4, 2, 152, 512)
    pack_here = after(pack)
    wq = pack[:, :, :96].reshape(4, 192, 512)
    wkv = lanes_out(pack[:, :, 96:128], 128).transpose(0, 2, 1, 3).reshape(2, 2, 128, 256)
    wkv = jnp.stack([core_pick(wkv[0], wkv[1]), core_pick(wkv[1], wkv[0])], axis=1)
    wkv = pad_latent(wkv.reshape(KV_RANK, 256))
    wlat = pack[:, :, 128:152].reshape(4, 48, 512)

    outs_pack = jnp.concatenate(
        [
            lanes_in(woutput.T.reshape(64, 4, 128).transpose(1, 0, 2)),
            lanes_in(
                jnp.pad(
                    jnp.pad(
                        shareddown.T.reshape(64, 2, 4, 4, 22)
                        .transpose(3, 0, 2, 1, 4)
                        .reshape(4, 64, 8, 22),
                        ((0, 0), (0, 0), (0, 0), (0, 2)),
                    ).reshape(4, 64, 192),
                    ((0, 0), (0, 0), (0, 64)),
                )
            ),
        ],
        axis=1,
    )
    shared_pack = jnp.pad(
        jnp.stack([sharedgate.T, sharedup.T]).reshape(2, 4, 22, 512),
        ((0, 0), (0, 0), (0, 2), (0, 0)),
    ).transpose(1, 0, 2, 3)

    units = row_scatter(
        jnp.concatenate(
            [
                swap_row_y(outs_pack),
                expertgate.reshape(4, 88, 512),
                shared_pack[:, 0],
                expertup.reshape(4, 88, 512),
                shared_pack[:, 1],
                swap_row_z(expertdown).reshape(4, 88, 512),
                jnp.zeros((4, 8, 512), bf16),
            ],
            axis=1,
        ),
        states_here,
        pack_here,
    ).reshape(4, 368, 512)
    outs_own = jnp.concatenate([units[q, :48] for q in range(4)], axis=1)
    outs_beside = other_xl(outs_own)
    outs_all = lax.all_gather(jnp.stack([outs_own, outs_beside]), "z", axis=1)
    units_beside = other_xl(lax.optimization_barrier(units)[:, 48:])
    units_own = jnp.concatenate([units[q, 48:] for q in range(4)], axis=1)
    units_own = lax.all_gather(units_own, "z", axis=0)

    def both(k, low, high):
        return jnp.concatenate([part[:, k, low:high] for part in first], axis=0)

    gain_in = jnp.sum(both(0, 128, 131).astype(f32), axis=1)
    router = both(0, 131, 139)
    router = jnp.concatenate([router[q] for q in range(4)], axis=1)
    rank_gain = jnp.sum(both(0, 139, 140)[:, 0, :384].astype(f32).reshape(2, 2, 3, 128), axis=2)
    rank_gain = jnp.stack(
        [core_pick(rank_gain[0], rank_gain[1]), core_pick(rank_gain[1], rank_gain[0])], axis=1
    )
    rank_gain = pad_latent(rank_gain.reshape(KV_RANK, 1))
    chosen = first[0][0, :, 140:142].astype(f32).reshape(512, 8).T
    wide = jnp.concatenate(
        [part[:, :, :128].reshape(2, 512, 512) for part in first], axis=0
    ).astype(f32)
    inverse_one = lax.rsqrt(jnp.sum(wide * wide, axis=(0, 2)) / D + norm_epsilon)
    normed_in = (wide * inverse_one[None, :, None] * gain_in[:, None, :]).astype(bf16)
    latent = gather_owners(dot("rcd,rtd->ct", wlat, normed_in))
    units_beside = behind(units_beside, after(latent[0]))
    units_beside = jnp.concatenate([units_beside[q] for q in range(4)], axis=1)
    units_beside = lax.all_gather(units_beside, "z", axis=0)
    outs_all = xl_order(outs_all, 0).reshape(8, 48, D)

    def by_side(x, width):
        x = x.reshape(8, x.shape[1], 4, 512).transpose(2, 0, 1, 3)
        return lanes_out(x, width).reshape(4, 512, width)

    wo_t = by_side(outs_all[:, :16], 128)
    shared_down = by_side(outs_all[:, 16:], 256)[:, :, :192].transpose(2, 0, 1).reshape(192, D)
    shared_down = xl_order(shared_down.reshape(4, 2, 24, D), 1).reshape(192, D)

    latent = jnp.concatenate([part.reshape(384, 512) for part in latent], axis=0)
    query = dot("rod,rtd->ot", wq, normed_in)
    query = jnp.concatenate(
        [query[:NOPE], rotate_rows(query[NOPE:], cosine, sine)], axis=0
    ).astype(bf16)
    is_rank = jnp.logical_not(
        put_rope(jnp.zeros((768, 1), jnp.bool_), jnp.ones((ROPE, 1), jnp.bool_))
    )
    latent_head = jnp.where(is_rank, latent, 0.0)
    latent_inverse = lax.rsqrt(
        jnp.sum(latent_head * latent_head, axis=0) / KV_RANK + norm_epsilon
    )
    compressed = (latent_head * latent_inverse[None, :] * rank_gain).astype(bf16)
    keyvalue = dot("ro,rt->ot", wkv, compressed)
    rope_key = rotate_rows(take_rope(latent), cosine, sine)
    key_pack = spread(
        jnp.concatenate([keyvalue[:NOPE], rope_key, keyvalue[NOPE:]], axis=0).astype(bf16),
        TOKEN,
        8,
    )
    rows = [begin[None, :], place[None, :]]
    key_place = key_place.reshape(8, 512, 1)
    shape = jax.ShapeDtypeStruct
    mine, theirs, attended, log_total = kernel_call(
        attend_body,
        [
            shape((2, 512, 512), f32),
            shape((2, 512, 512), bf16),
            shape((VDIM, 512), f32),
            shape((1, 512), f32),
        ],
        [query, key_pack, key_place, *rows, wo_t],
        2 * 512 * (4096 * 320 + 128 * 2048),
        anchors=[shared_down, router, chosen],
    )
    attn_in = attended.astype(bf16)

    def owner_blocks(x):
        return x.reshape(2, 4, 128, 512)

    mixed = states.astype(f32) + sum_owners(owner_blocks(mine), owner_blocks(theirs))

    squares = jnp.pad(jnp.sum(mixed * mixed, axis=1)[None], ((0, 3), (0, 384)))
    second = gather_owners(
        jnp.concatenate(
            [(mixed * secondgain).astype(bf16), to_rows(squares), jnp.zeros((8, 512), bf16)], axis=0
        )
    )
    wlat_all = lax.all_gather(behind(wlat, after(second[0])), WEIGHT, axis=0)
    numbers = jnp.arange(EXPERTS)[:, None]
    (
        mine,
        theirs,
        gained,
        inner,
        hidden_routed,
        hidden_shared,
        logits,
        routing,
        factors,
        inverse_two,
    ) = kernel_call(
        experts_body,
        [
            shape((2, 512, 512), f32),
            shape((2, 512, 512), bf16),
            shape((512, D), bf16),
            shape((8, 224, 512), f32),
            shape((8, 96, 512), bf16),
            shape((192, 512), bf16),
            shape((8, 512), f32),
            shape((8, 512), f32),
            shape((2, 512), f32),
            shape((1, 512), f32),
        ],
        [
            second[0].reshape(8, 144, 512),
            second[1].reshape(8, 144, 512),
            units_own,
            units_beside,
            shared_down,
            router,
            chosen,
            (numbers == 2 * y_index + xl_index).astype(f32),
            (numbers == 2 * y_index + 1 - xl_index).astype(f32),
        ],
        2 * 512 * D * 2752,
        [pltpu.VMEM((2, 4, 96, 512), f32), pltpu.VMEM((8, 24, 512), f32)],
    )
    final = mixed + sum_owners(owner_blocks(mine), owner_blocks(theirs))
    output = final.astype(bf16)

    difference = (final - teacher.astype(f32)) * own_valid[:, None]
    error_own = jnp.sum(difference * difference)
    grad_final = difference * (4096.0 / valid_count)
    grad_branch = gather_owners(grad_final.astype(bf16))

    def return_units(block, more):
        block = jnp.stack([block[:, q * 512 : q * 512 + 512] for q in range(4)])
        block = jnp.concatenate([block, more], axis=1)
        return row_return(block.reshape(2, 2, -1, 512))

    hidden_shared = xl_order(hidden_shared.reshape(4, 2, 24, 512), 1).reshape(192, 512)
    grad_branch, grad_down, grad_shared_down = kernel_call(
        down_back_body,
        [shape((512, D), bf16), shape((768, D), bf16), shape((4, 8, 32, 512), bf16)],
        [part.reshape(8, 128, 512) for part in grad_branch]
        + [hidden_routed.reshape(768, 512), hidden_shared],
        2 * 512 * D * 960,
        anchors=[wlat_all],
    )
    down_sum = along_z(grad_down.reshape(4, 2, 96, D))
    expert = 2 * y_index + jnp.stack([xl_index, 1 - xl_index])[:, None]
    expert_place = (jnp.arange(1024)[None, :] // 128 == expert).astype(f32).reshape(2, 2, 512)
    mine, theirs, scaled_slopes, side = kernel_call(
        experts_back_body,
        [
            shape((2, 512, 512), f32),
            shape((2, 512, 512), bf16),
            shape((8, 224, 512), bf16),
            shape((4, 4, 512), f32),
        ],
        [grad_branch, units_own, units_beside, shared_down, inner, factors, inverse_two, gained]
        + [expert_place],
        2 * 512 * D * 2752,
        [
            pltpu.VMEM((2, 4, 224, 512), bf16),
            pltpu.VMEM((2, 512, 896), bf16),
            pltpu.VMEM((8, 24, 512), f32),
        ],
    )
    side = jnp.broadcast_to(side[None, None], (2, 2, 4, 4, 512)).reshape(2, 8, 4, 512)
    grad_mid_own, side, ready = sum_owners(owner_blocks(mine), owner_blocks(theirs), side)
    inner_own = side[0, :128]
    combine_own = side[1:3].reshape(8, 128)
    grad_win = dot(
        "ft,td->fd", behind(scaled_slopes.reshape(1792, 512), ready), gained
    ).astype(bf16)
    unit_sum = along_z(grad_win.reshape(4, 2, 224, D))
    routing_own = lax.dynamic_slice_in_dim(routing, y_index * 128, 128, 1)
    logits_own = lax.dynamic_slice_in_dim(logits, y_index * 128, 128, 1)
    inverse_two_own = lax.dynamic_slice_in_dim(inverse_two[0], y_index * 128, 128, 0)[:, None]
    grad_routing = combine_own * chosen_own.T
    grad_logits = (
        routing_own
        * (grad_routing - jnp.sum(routing_own * grad_routing, axis=0, keepdims=True))
    ).astype(bf16)
    normed_mid_own = (mixed * inverse_two_own * secondgain).astype(bf16)
    grad_router = dot("et,td->ed", grad_logits, normed_mid_own)
    grad_mid_own = grad_mid_own + dot("et,de->td", grad_logits, wrouter)
    inner_own = inner_own + jnp.sum(grad_logits.astype(f32) * logits_own, axis=0)
    grad_mixed = (
        grad_final
        + grad_mid_own * secondgain * inverse_two_own
        - mixed * (inverse_two_own * inverse_two_own * inner_own[:, None] / D)
    )
    grad_second = jnp.sum(grad_mid_own * mixed * inverse_two_own, axis=0)


    grad_attn = [x.reshape(2, 512, 512) for x in gather_owners(grad_mixed.astype(bf16))]
    grad_kv, grad_query, outs_rows = kernel_call(
        attend_back_body,
        [shape((8, 320, 512), bf16), shape((192, 512), bf16), shape((4, 2, 288, 512), bf16)],
        [*grad_attn, wo_t, query, key_pack, key_place, *rows, attended, log_total, cosine, sine]
        + [normed_in, grad_shared_down],
        2 * 512 * (4096 * 832 + 512 * 2048),
        scalars=[xl_index.reshape(1)],
        anchors=[down_sum],
    )
    grad_kv = exchange(grad_kv, TOKEN)
    outs_sum = along_z(outs_rows)
    rope_rows = put_rope(jnp.zeros((768, ROPE), bf16), jnp.eye(ROPE, dtype=bf16))
    gain_rows = core_pick(gain_row_table(0), gain_row_table(1))
    mine, theirs, grad_keyvalue, grad_latent, late = kernel_call(
        latent_back_body,
        [
            shape((2, 512, 512), f32),
            shape((2, 512, 512), bf16),
            shape((256, 512), bf16),
            shape((768, 512), bf16),
            shape((16, 4, 512), f32),
        ],
        [
            grad_kv,
            cosine,
            sine,
            wkv,
            latent_head,
            latent_inverse[None, :],
            rank_gain,
            rope_rows,
            grad_query,
            wq,
            wlat_all,
            normed_in,
            gain_rows,
            gain_in,
        ],
        2 * 512 * (768 * 256 + 960 * 2048),
        [pltpu.VMEM((4, 768, 512), bf16)],
        [lax.axis_index("co").reshape(1)],
        [unit_sum],
    )
    grad_wkv = dot("rt,ot->ro", compressed, grad_keyvalue)

    own_xh = (jnp.arange(2) == lax.axis_index("xh")).astype(f32)[:, None, None]

    def to_own(x, n):
        x = own_xh * x.reshape(1, 4, n)
        return jnp.stack([x, jnp.zeros_like(x)])

    early = jnp.concatenate(
        [
            jnp.pad(to_own(grad_second, 128), ((0, 0),) * 3 + ((256, 128),))
            + error_own * (jnp.arange(512) == 511).astype(f32),
            to_own(grad_router.reshape(8, 4, 128).transpose(1, 0, 2), 1024),
            jnp.zeros((2, 2, 4, 512), f32),
        ],
        axis=3,
    ).reshape(2, 8, 4, 512)
    side = early + late.reshape(2, 8, 4, 512)
    grad_latent = grad_latent.reshape(2, 2, 4, 48, 512)
    got = sum_owners(
        jnp.concatenate([owner_blocks(mine), grad_latent[0].astype(f32)], axis=2),
        jnp.concatenate([owner_blocks(theirs), grad_latent[1]], axis=2),
        side,
        raw=True,
    )
    by_rank = unpad_latent(grad_wkv)[:KV_RANK].reshape(2, 2, 128, 256)
    by_rank = jnp.stack(
        [core_pick(by_rank[:, 0], by_rank[:, 1]), core_pick(by_rank[:, 1], by_rank[:, 0])]
    )
    wkv_rows = lanes_in(
        by_rank.reshape(4, 128, 2, 128).transpose(0, 2, 1, 3).reshape(8, 128, 128)
    ).astype(bf16)
    grad_in_own, side, pack = kernel_call(
        last_body,
        [shape((128, 512), f32), shape((4, 512), f32), shape((8, 80, 512), bf16)],
        [got, wkv_rows, normed_in],
        2 * 512 * 48 * 2048,
    )
    summed = after(grad_in_own)
    pack = exchange(pack, TOKEN)
    own_wide = states.astype(f32)
    inverse_own = lax.dynamic_slice_in_dim(inverse_one, y_index * 128, 128, 0)[:, None]
    grad_states = (
        grad_mixed
        + grad_in_own * firstgain * inverse_own
        - own_wide * (inverse_own * inverse_own * side[0, :128, None] / D)
    )

    outs_sum = along_xl(outs_sum, summed)

    pack = jnp.sum(pack.astype(f32), axis=0)
    sums = pack[64:68] + pack[68:72]

    def own_part(row, at, n):
        return lax.dynamic_slice_in_dim(sums[row, at : at + 8 * n], group * n, n, 0)

    router_part = sums[1:3].reshape(8, 8, 16)
    router_part = lax.dynamic_index_in_dim(router_part, group, 1, keepdims=False)
    pack = jnp.concatenate([pack[:56].astype(bf16), outs_sum[192:]], axis=0)
    pack = from_head(pack).astype(f32)
    grad_wkeyvalue = lanes_out(pack[:32], 128)
    grad_wlatent = pack[32:50].T
    grad_wquery = pack[56:]
    loss_value = sums[0, 511] / (valid_count * D)

    outs_part = jnp.concatenate(
        [outs_sum[:64].reshape(4, 16, 512), outs_sum[64:192].reshape(4, 32, 512)], axis=1
    )
    unit_sum = along_xl(jnp.concatenate([down_sum, unit_sum], axis=1), summed)
    unit_sum = return_units(unit_sum, outs_part)
    down_sum, outs_part, unit_sum = unit_sum[:, :88], unit_sum[:, 320:], unit_sum[:, 96:320]
    unit_sum = unit_sum.astype(f32)
    outs_part = swap_row_y(outs_part)
    grad_woutput = lanes_out(outs_part[:, :16], 128).astype(f32)
    grad_woutput = grad_woutput.transpose(0, 2, 1).reshape(512, 64)
    sd_sum = lanes_out(outs_part[:, 16:], 256)[:, :, :192].astype(f32)
    grad_shareddown = (
        sd_sum.reshape(4, 64, 4, 2, 24)[..., :22].transpose(3, 2, 0, 4, 1).reshape(704, 64)
    )
    grad_expertdown = swap_row_z(down_sum.reshape(352, 512)).astype(f32)
    grad_expertgate = unit_sum[:, :88].reshape(352, 512)
    grad_sharedgate = unit_sum[:, 88:110].reshape(88, 512).T
    grad_expertup = unit_sum[:, 112:200].reshape(352, 512)
    grad_sharedup = unit_sum[:, 200:222].reshape(88, 512).T

    return (
        output,
        loss_value,
        grad_states,
        own_part(0, 128, 16),
        grad_wquery,
        grad_wlatent,
        own_part(0, 384, 4),
        grad_wkeyvalue,
        grad_woutput,
        own_part(0, 256, 16),
        router_part.T,
        grad_sharedgate,
        grad_sharedup,
        grad_shareddown,
        grad_expertgate,
        grad_expertup,
        grad_expertdown,
    )


def solution(mesh):
    parts = Mesh(mesh.devices.reshape(2, 2, 4, 2, 4), ("xh", "co", "y", "xl", "z"))
    both = ROW + COL
    return jax.shard_map(
        shards,
        mesh=parts,
        in_specs=(
            P(COL, ROW),
            P(COL, ROW),
            P(ROW),
            P(COL, ROW),
            P(ROW, COL),
            P(ROW),
            P(ROW, COL),
            P(ROW, COL),
            P(ROW),
            P(ROW, None),
            P(ROW, COL),
            P(ROW, COL),
            P(ROW, COL),
            P(COL, ROW),
            P(COL, ROW),
            P(ROW, COL),
            P(COL, None),
            P(),
            P(),
        ),
        out_specs=(
            P(COL, ROW),
            P(),
            P(COL, ROW),
            P(both),
            P(COL, ROW),
            P(ROW, COL),
            P(both),
            P(ROW, COL),
            P(ROW, COL),
            P(both),
            P(both, None),
            P(ROW, COL),
            P(ROW, COL),
            P(ROW, COL),
            P(COL, ROW),
            P(COL, ROW),
            P(ROW, COL),
        ),
        check_vma=False,
    )
```

```python
import math

import jax
import jax.numpy as jnp
import numpy as np
from jax import lax
from jax.experimental import pallas as pl
from jax.experimental.pallas import tpu as pltpu
from jax.sharding import Mesh, PartitionSpec as P

HEADS = 16
NOPE = 128
ROPE = 64
VDIM = 128
KV_RANK = 512
F = 1408
EXPERTS = 8
D = 2048

norm_epsilon = 1e-06
negative_fill = -1e30
rope_base = 10000.0

ROW = ("xh", "co")
COL = ("y", "xl", "z")
CHIPS = ("xh", "y")
WEIGHT = ("xh", "co", "y")
TOKEN = ("xl", "z")

bf16 = jnp.bfloat16
f32 = jnp.float32


def dot(spec, a, b):
    return jnp.einsum(spec, a, b, preferred_element_type=f32)


def exchange(x, axes):
    return lax.all_to_all(x, axes, 0, 0, tiled=True)


def spread(x, axes, n):
    return exchange(jnp.broadcast_to(x[None], (n,) + x.shape), axes)


def pieces(x, n):
    parts = []
    for _ in range(n):
        part = lax.reduce_precision(x, 8, 7)
        parts.append(part.astype(bf16))
        x = x - part
    return parts


def to_rows(vals):
    return jnp.concatenate(pieces(vals, 2), axis=-2)


def from_rows(rows):
    rows = rows.astype(f32)
    return rows[..., :4, :] + rows[..., 4:8, :]


def after(x):
    return (x[(0,) * x.ndim].astype(f32) * 0.0).astype(jnp.int32)


def behind(x, zero):
    return jnp.where(zero == 0, x, jnp.zeros_like(x))


def mate(x):
    return lax.ppermute(x, "co", [(0, 1), (1, 0)])


def core_pick(zero, one):
    return jnp.where(lax.axis_index("co") == 0, zero, one)


def xh_pick(zero, one, later=0):
    return jnp.where(lax.axis_index("xh") + later == 0, zero, one)


def gather_owners(x):
    own = spread(x, CHIPS, 8).reshape(2, 4, *x.shape)
    return own, mate(own)


def sum_owners(mine, theirs, side=None, raw=False):
    rows = mine.shape[2]

    def packed(block, vals):
        block = block.astype(bf16).reshape(8, rows, 512)
        return block if side is None else jnp.concatenate([block, to_rows(vals)], axis=1)

    got = mate(packed(theirs, None if side is None else side[1]))
    mine = mine.reshape(8, rows, 512) + got[:, :rows].astype(f32)
    vals = None if side is None else side[0] + from_rows(got[:, rows:])
    ready = packed(mine, vals)
    got = exchange(ready, CHIPS)
    if raw:
        return got
    total = jnp.sum(got[:, :rows].astype(f32), axis=0)
    if side is None:
        return total
    return total, jnp.sum(from_rows(got[:, rows:]), axis=0), after(ready)


def other_xl(x):
    return lax.ppermute(x, "xl", [(0, 1), (1, 0)])


def xl_pick(zero, one):
    return jnp.where(lax.axis_index("xl") == 0, zero, one)


def xl_order(x, axis):
    return xl_pick(x, jnp.flip(x, axis))


def z_first(x):
    return jnp.swapaxes(x.reshape(2, 4, *x.shape[1:]), 0, 1)


def along_z(x):
    z, xl, n, m = x.shape
    x = lax.psum_scatter(x.reshape(8 * n, m), "z", scatter_dimension=0, tiled=True)
    return x.reshape(2, n, m)


def along_xl(x, later):
    return (x[0].astype(f32) + behind(other_xl(x[1]), later).astype(f32)).astype(bf16)


def row_permute(block, k):
    return lax.ppermute(block, ROW, [(r, r ^ k) for r in range(4)])


def row_scatter(x, start=0, end=0):
    me = lax.axis_index("xh") * 2 + lax.axis_index("co") + start
    got = [lax.dynamic_index_in_dim(x, me, 0, keepdims=False)]
    for k in (1, 2, 3):
        got.append(row_permute(lax.dynamic_index_in_dim(x, me ^ k, 0, keepdims=False), k))
    return jnp.stack(
        [
            jnp.stack([xh_pick(got[k], got[k + 2], end), xh_pick(got[k + 2], got[k], end)])
            for k in (0, 1)
        ]
    )


def row_return(x):
    got = []
    for k in range(4):
        near, far = x[k % 2, 0], x[k % 2, 1]
        block = xh_pick(near, far) if k < 2 else xh_pick(far, near)
        got.append(row_permute(block, k) if k else block)
    me = lax.axis_index("xh") * 2 + lax.axis_index("co")
    got = jnp.stack(got)
    return jnp.stack(
        [lax.dynamic_index_in_dim(got, me ^ r, 0, keepdims=False) for r in range(4)]
    )


def swap_row_y(x):
    pairs = [(r * 4 + y, y * 4 + r) for r in range(4) for y in range(4)]
    return lax.ppermute(x, WEIGHT, pairs)


def swap_row_z(x):
    pairs = [(r * 4 + z, z * 4 + r) for r in range(4) for z in range(4)]
    return lax.ppermute(x, ROW + ("z",), pairs)


def head_pairs():
    pairs = []
    for n in range(32):
        xh, co, xl, hi, lo = n >> 4, n >> 3 & 1, n >> 2 & 1, n >> 1 & 1, n & 1
        source = hi << 4 | (co ^ xl) << 3 | xh << 2 | co << 1 | lo
        pairs.append((source, n))
    return pairs


def to_head(x):
    return lax.ppermute(x, ROW + TOKEN, head_pairs())


def from_head(x):
    return lax.ppermute(x, ROW + TOKEN, [(b, a) for a, b in head_pairs()])


def lanes_in(x):
    k = 512 // x.shape[-1]
    n = x.shape[-2] // k
    return jnp.concatenate([x[..., i * n : (i + 1) * n, :] for i in range(k)], axis=-1)


def lanes_out(x, width):
    return jnp.concatenate(
        [x[..., i * width : (i + 1) * width] for i in range(512 // width)], axis=-2
    )


def rotate_rows(v, cosine, sine):
    a, b = v[: ROPE // 2], v[ROPE // 2 :]
    return jnp.concatenate([a * cosine - b * sine, b * cosine + a * sine], axis=0)


def rotate_back_rows(g, cosine, sine):
    a, b = g[: ROPE // 2], g[ROPE // 2 :]
    return jnp.concatenate([a * cosine + b * sine, b * cosine - a * sine], axis=0)


def rope_angles(position):
    exponents = jnp.arange(ROPE // 2, dtype=f32) * (2.0 / ROPE)
    frequency = jnp.exp(-math.log(rope_base) * exponents)
    return frequency[:, None] * position.astype(f32)[None, :]


def product(a, b, left=1, right=0):
    return lax.dot_general(a, b, (((left,), (right,)), ((), ())), preferred_element_type=f32)


def kernel_call(body, outs, args, flops, scratch=(), scalars=(), anchors=()):
    moved = sum(x.size * x.dtype.itemsize for x in list(args) + list(outs))
    vmem, smem = pl.BlockSpec(memory_space=pltpu.VMEM), pl.BlockSpec(memory_space=pltpu.SMEM)
    used = len(scalars) + len(args)

    def without_anchors(*refs):
        body(*refs[:used], *refs[used + len(anchors) :])

    return pl.pallas_call(
        without_anchors,
        out_shape=outs,
        in_specs=[smem] * len(scalars)
        + [vmem] * len(args)
        + [pl.BlockSpec(memory_space=pl.ANY)] * len(anchors),
        out_specs=[vmem] * len(outs),
        scratch_shapes=list(scratch),
        compiler_params=pltpu.CompilerParams(vmem_limit_bytes=48 * 2**20),
        cost_estimate=pl.CostEstimate(flops=flops, bytes_accessed=moved, transcendentals=0),
    )(*scalars, *args, *anchors)


SCORE_SCALE = (NOPE + ROPE) ** (-0.5)


def first_body(
    own, other, wq, wlat, cosine, sine,
    normed_in, latent, query, inverse, tails, chosen,
):
    blocks = []
    total = jnp.zeros((512, 1), f32)
    for q in range(4):
        part, xh = (own, other)[q // 2], q % 2
        x = [part[xh * 4 + y, :128, :].astype(f32) for y in range(4)]
        x = jnp.concatenate(x, axis=0)
        blocks.append(x)
        total = total + jnp.sum(x * x, axis=1, keepdims=True)
        tails[q] = part[xh * 4, 128:, :].astype(f32)
    inv = lax.rsqrt(total / D + norm_epsilon)
    inverse[...] = inv
    lat = jnp.zeros((48, 512), f32)
    acc = jnp.zeros((192, 512), f32)
    for q in range(4):
        gain = tails[q, 0:1, :] + tails[q, 1:2, :] + tails[q, 2:3, :]
        normed = (blocks[q] * inv * gain).astype(bf16)
        normed_in[q] = normed
        normed = normed.T
        lat = lat + product(wlat[q], normed)
        acc = acc + product(wq[q], normed)
    latent[...] = lat
    a, b = acc[NOPE : NOPE + 32], acc[NOPE + 32 :]
    query[:NOPE, :] = acc[:NOPE].astype(bf16)
    query[NOPE:, :] = jnp.concatenate(
        [a * cosine[...] - b * sine[...], b * cosine[...] + a * sine[...]], axis=0
    ).astype(bf16)
    for y in range(4):
        chosen[y] = own[y, 128:, :].astype(f32)


def latent_body(
    core, own, other, wkv, rank_gain, is_rank, rope_take, cosine, sine,
    key_pack, latent_head, latent_inverse, compressed,
):
    lat = jnp.concatenate([own[...].reshape(384, 512), other[...].reshape(384, 512)], axis=0)
    lat = lat * is_rank[...]
    latent_head[...] = lat
    inv = lax.rsqrt(jnp.sum(lat * lat, axis=0, keepdims=True) / KV_RANK + norm_epsilon)
    latent_inverse[...] = inv
    comp = (lat * inv * rank_gain[...]).astype(bf16)
    compressed[...] = comp
    keyvalue = product(wkv[...], comp, 0, 0)
    first = jnp.where(core[0] == 0, own[7], other[7])
    second = jnp.where(core[0] == 0, other[7], own[7])
    rope = lax.dot_general(
        rope_take[...],
        jnp.concatenate([first, second], axis=0),
        (((1,), (0,)), ((), ())),
        precision=lax.Precision.HIGHEST,
        preferred_element_type=f32,
    )
    a, b = rope[:32], rope[32:]
    key_pack[:NOPE, :] = keyvalue[:NOPE].astype(bf16)
    key_pack[NOPE : NOPE + ROPE, :] = jnp.concatenate(
        [a * cosine[...] - b * sine[...], b * cosine[...] + a * sine[...]], axis=0
    ).astype(bf16)
    key_pack[NOPE + ROPE :, :] = keyvalue[NOPE:].astype(bf16)


def returned_body(me, got0, got1, got2, got3, down, gate, up, shared):
    for k, got in enumerate((got0, got1, got2, got3)):
        block = got[...].astype(f32)
        at = me[0] ^ k
        down[at] = block[:88].astype(bf16)
        gate[at] = block[96:184]
        up[at] = block[208:296]
        shared[at, 0] = block[184:208]
        shared[at, 1] = block[296:320]


def attend_body(query, key_pack, key_place, begin, place, wo_t, mine, theirs, attended, log_total):
    def block(b, state):
        top, total, acc = state
        keys, values = key_pack[b, :192, :], key_pack[b, 192:, :]
        scores = product(keys, query[...], 0, 0) * SCORE_SCALE
        at = key_place[b]
        allowed = (at >= begin[...]) & (at <= place[...])
        scores = jnp.where(allowed, scores, negative_fill)
        new_top = jnp.maximum(top, jnp.max(scores, axis=0, keepdims=True))
        weights = jnp.where(allowed, jnp.exp(scores - new_top), 0.0)
        factor = jnp.exp(top - new_top)
        total = total * factor + jnp.sum(weights, axis=0, keepdims=True)
        acc = acc * factor + product(values, weights.astype(bf16))
        return new_top, total, acc

    top, total, acc = lax.fori_loop(
        0,
        8,
        block,
        (
            jnp.full((1, 512), negative_fill, f32),
            jnp.zeros((1, 512), f32),
            jnp.zeros((VDIM, 512), f32),
        ),
    )
    result = acc / total
    attended[...] = result
    log_total[...] = top + jnp.log(total)
    attn_in = result.T.astype(bf16)
    for q in range(4):
        part = product(attn_in, wo_t[q], 1, 1)
        if q < 2:
            mine[q] = part
        else:
            theirs[q - 2] = part.astype(bf16)


def attend_back_body(
    this_xl, own, other, wo_t, query, key_pack, key_place, begin, place, attended, log_total, cosine,
    sine, normed_in, grad_shared_down,
    grad_kv, grad_query, outs_rows,
):
    attn_in = attended[...].astype(bf16)
    for q in range(4):
        grad = own[q] if q < 2 else other[q - 2]
        part = product(attn_in, grad).T.astype(bf16)
        for c in range(8):
            xl, z = c // 4, c % 4
            for k in range(4):
                at = c * 64 + k * 16
                lanes = slice(k * 128, k * 128 + 128)
                outs_rows[z, xl ^ this_xl[0], q * 16 : q * 16 + 16, lanes] = part[at : at + 16]
            rows = slice(64 + q * 32, 96 + q * 32)
            outs_rows[z, xl ^ this_xl[0], rows, :] = grad_shared_down[q, c]
    grad = product(own[0], wo_t[0]) + product(own[1], wo_t[1])
    grad = grad + product(other[0], wo_t[2]) + product(other[1], wo_t[3])
    grad_by_token = grad.astype(bf16)
    grad = grad.T.astype(bf16)
    query_by_token = query[...].astype(f32).T.astype(bf16)
    delta = jnp.sum(grad.astype(f32) * attended[...], axis=0, keepdims=True)

    def block(b, acc):
        keys, values = key_pack[b, :192, :], key_pack[b, 192:, :]
        scores = product(keys, query[...], 0, 0) * SCORE_SCALE
        at = key_place[b]
        allowed = (at >= begin[...]) & (at <= place[...])
        probs = jnp.where(allowed, jnp.exp(scores - log_total[...]), 0.0)
        grad_probs = product(values, grad, 0, 0)
        grad_scores = (probs * (grad_probs - delta)).astype(bf16)
        part = product(grad_scores, query_by_token) * SCORE_SCALE
        grad_kv[b, :192, :] = part.T.astype(bf16)
        grad_kv[b, 192:, :] = product(probs.astype(bf16), grad_by_token).T.astype(bf16)
        return acc + product(keys, grad_scores)

    acc = lax.fori_loop(0, 8, block, jnp.zeros((192, 512), f32)) * SCORE_SCALE
    a, b = acc[NOPE : NOPE + 32], acc[NOPE + 32 :]
    grad_query[:NOPE, :] = acc[:NOPE].astype(bf16)
    grad_query[NOPE:, :] = jnp.concatenate(
        [a * cosine[...] + b * sine[...], b * cosine[...] - a * sine[...]], axis=0
    ).astype(bf16)
    for q in range(4):
        part = product(grad_query[...], normed_in[q]).astype(bf16)
        for low in range(2):
            rows = part[low * 96 : low * 96 + 96]
            outs_rows[q % 2 * 2 + low, q // 2 ^ this_xl[0], 192:, :] = rows


def latent_back_body(
    core, got, cosine, sine, wkv, latent_head, latent_inverse, rank_gain, rope_rows, grad_query, wq,
    wlat_all, normed_in, gain_rows, gain,
    mine, theirs, grad_keyvalue, grad_latent, late,
    wlat,
):
    for side in range(2):
        for n in range(8):
            source = (n // 4) * 8 + (core[0] ^ side) * 4 + n % 4
            at = side * 384 + n * 48
            for q in range(4):
                wlat[q, at : at + 48, :] = wlat_all[source, q ^ (2 * side), :, :]
    total = got[0].astype(f32)
    for b in range(1, 8):
        total = total + got[b].astype(f32)
    a, b = total[NOPE : NOPE + 32], total[NOPE + 32 : NOPE + ROPE]
    grad_rope = jnp.concatenate(
        [a * cosine[...] + b * sine[...], b * cosine[...] - a * sine[...]], axis=0
    ).astype(bf16)
    grad = jnp.concatenate([total[:NOPE], total[NOPE + ROPE :]], axis=0).astype(bf16)
    grad_keyvalue[...] = grad
    grad_compressed = product(wkv[...], grad)
    lat, inv = latent_head[...], latent_inverse[...]
    scaled = grad_compressed * rank_gain[...]
    inner_rank = jnp.sum(scaled * lat, axis=0, keepdims=True)
    gain_sum = jnp.sum(grad_compressed * lat * inv, axis=1, keepdims=True)
    gain_row = jnp.broadcast_to(gain_sum, (768, 128)).T[:8]
    gain_high = gain_row.astype(bf16)
    gain_low = (gain_row - gain_high.astype(f32)).astype(bf16)
    unpad = lax.broadcasted_iota(jnp.int32, (768, 2048), 0) == gain_rows[...]
    unpad = unpad.astype(f32).astype(bf16)
    gain_row = product(gain_high, unpad) + product(gain_low, unpad)
    result = scaled * inv - lat * (inv * inv * inv * inner_rank / KV_RANK)
    result = result + product(rope_rows[...], grad_rope)
    grad_latent[...] = result.astype(bf16)
    result = result.T.astype(bf16)
    grad_query_turned = grad_query[...].astype(f32).T.astype(bf16)
    inner_sum = jnp.zeros((512, 1), f32)
    firsts = []
    for q in range(4):
        part = product(grad_query_turned, wq[q]) + product(result, wlat[q])
        if q < 2:
            mine[q] = part
        else:
            theirs[q - 2] = part.astype(bf16)
        weighted = part * normed_in[q].astype(f32)
        inner_sum = inner_sum + jnp.sum(weighted, axis=1, keepdims=True)
        firsts.append(jnp.sum(weighted, axis=0, keepdims=True) / gain[q : q + 1, :])
    inner = jnp.broadcast_to(inner_sum, (512, 128)).T[:1]
    late[...] = jnp.zeros((16, 4, 512), f32)
    for q in range(4):
        for y in range(4):
            at = q * 4 + y
            late[at, :1, :128] = inner[:, y * 128 : y * 128 + 128]
            late[at, :1, 128:256] = firsts[q][:, y * 128 : y * 128 + 128]
            late[at, :1, 384:512] = gain_row[:1, at * 128 : at * 128 + 128]


def fill_features(x2, parts):
    for side, part in enumerate(parts):
        for xh in range(2):
            at = side * 1024 + xh * 512
            for y in range(4):
                x2[y * 128 : y * 128 + 128, at : at + 512] = part[xh * 4 + y, :128, :]


def experts_body(
    this_xl, own, other, units_own, units_beside, shared_down, router, chosen, first_expert, second_expert,
    mine, theirs, x2, inner, hidden_routed, hidden_shared, logits, routing, factors, inverse,
    routed, shared, x2_turned,
):
    fill_features(x2, (own, other))
    x2_turned[...] = x2[...].T
    squares = []
    for y in range(4):
        total = jnp.zeros((1, 128), f32)
        for part in (own, other):
            for xh in range(2):
                rows = part[xh * 4 + y, 128:144, :].astype(f32)
                total = total + (rows[:1, :128] + rows[4:5, :128])
        squares.append(total)
    inv = lax.rsqrt(jnp.concatenate(squares, axis=1) / D + norm_epsilon)
    inverse[...] = inv
    scores = product(router[...], x2_turned[...]) * inv
    logits[...] = scores
    scores = jnp.exp(scores - jnp.max(scores, axis=0, keepdims=True))
    scores = scores / jnp.sum(scores, axis=0, keepdims=True)
    routing[...] = scores
    combine = scores * chosen[...]
    factors[:1, :] = jnp.sum(combine * first_expert[...], axis=0, keepdims=True)
    factors[1:, :] = jnp.sum(combine * second_expert[...], axis=0, keepdims=True)

    for p, units in enumerate((units_own, units_beside)):

        def block(z, carry, p=p, units=units):
            t = 2 * z + p
            h = product(units[z, :224, :], x2_turned[...]) * inv
            inner[t] = h
            gate, up = h[:112], h[112:]
            act = gate * jax.nn.sigmoid(gate) * up
            hidden = act[:88] * factors[p : p + 1, :]
            hidden = jnp.concatenate([hidden, jnp.zeros((8, 512), f32)], axis=0)
            routed[p, z] = hidden
            hidden_routed[t] = hidden.astype(bf16)
            shared[t] = act[88:]
            hidden_shared[2 * z + (p ^ this_xl[0])] = act[88:].astype(bf16)
            return carry

        lax.fori_loop(0, 4, block, 0)
    by_token = [routed[p].reshape(384, 512).T.astype(bf16) for p in range(2)]
    shared_by_token = shared[...].reshape(192, 512).T.astype(bf16)
    for q in range(4):
        at = q * 512
        part = product(shared_by_token, shared_down[:, at : at + 512])
        for p, units in enumerate((units_own, units_beside)):
            part = part + product(by_token[p], units[:, 224:, at : at + 512].reshape(384, 512))
        if q < 2:
            mine[q] = part
        else:
            theirs[q - 2] = part.astype(bf16)


def down_back_body(own, other, hidden_routed, hidden_shared, grad2, grad_down, grad_shared_down):
    fill_features(grad2, (own, other))
    grad_shared_down[...] = jnp.zeros((4, 8, 32, 512), bf16)
    for q in range(4):
        at = q * 512
        part = product(hidden_routed[...], grad2[:, at : at + 512])
        grad_down[:, at : at + 512] = part.astype(bf16)
        part = product(hidden_shared[...], grad2[:, at : at + 512]).T.astype(bf16)
        for c in range(8):
            for k in range(2):
                at = c * 64 + k * 32
                grad_shared_down[q, c, :, k * 256 : k * 256 + 192] = part[at : at + 32]


def experts_back_body(
    grad2, units_own, units_beside, shared_down, inner, factors, inverse, x2, expert_place,
    mine, theirs, scaled, side,
    slopes, by_token, grad_shared, grad2_turned,
):
    side[...] = jnp.zeros((4, 4, 512), f32)
    grad2_turned[...] = grad2[...].T
    grad_shared[...] = product(shared_down[...], grad2_turned[...]).reshape(8, 24, 512)
    inv = inverse[...]
    for p, units in enumerate((units_own, units_beside)):
        factor = factors[p : p + 1, :]

        def block(z, reached, p=p, units=units, factor=factor):
            t = 2 * z + p
            grad = product(units[z, 224:, :], grad2_turned[...])[:88]
            gate, up = inner[t, :112, :], inner[t, 112:, :]
            sig = jax.nn.sigmoid(gate)
            silu = gate * sig
            reached = reached + jnp.sum(grad * (silu * up)[:88], axis=0, keepdims=True)
            grad = jnp.concatenate([grad * factor, grad_shared[t]], axis=0)
            gate_slope = grad * up * sig * (1.0 + gate * (1.0 - sig))
            up_slope = grad * silu
            slopes[p, z, :112, :] = gate_slope.astype(bf16)
            slopes[p, z, 112:, :] = up_slope.astype(bf16)
            scaled[t, :112, :] = (gate_slope * inv).astype(bf16)
            scaled[t, 112:, :] = (up_slope * inv).astype(bf16)
            return reached

        reached = lax.fori_loop(0, 4, block, jnp.zeros((1, 512), f32))
        for y in range(4):
            part = reached[:, y * 128 : y * 128 + 128]
            part = jnp.concatenate([part] * 4, axis=1)
            side[y, 1:3, :] += part * expert_place[p]
        by_token[p] = slopes[p].reshape(896, 512).T
    total = jnp.zeros((512, 1), f32)
    for q in (2, 3, 0, 1):
        at = q * 512
        part = product(by_token[0], units_own[:, :224, at : at + 512].reshape(896, 512))
        part = part + product(by_token[1], units_beside[:, :224, at : at + 512].reshape(896, 512))
        if q < 2:
            mine[q] = part
        else:
            theirs[q - 2] = part.astype(bf16)
        part = part * x2[:, at : at + 512].astype(f32)
        total = total + jnp.sum(part, axis=1, keepdims=True)
    inner_sum = jnp.broadcast_to(total, (512, 128)).T[:1] * inv
    for y in range(4):
        side[y, :1, :128] = inner_sum[:, y * 128 : y * 128 + 128]


def last_body(got, wkv_rows, normed_in, grad_own, side, pack):
    total = got[0].astype(f32)
    for k in range(1, 8):
        total = total + got[k].astype(f32)
    grad_own[...] = total[:128]
    sums = total[176:180] + total[180:184]
    side[...] = sums
    high = sums.astype(bf16)
    low = (sums - high.astype(f32)).astype(bf16)
    rows = jnp.concatenate([high.astype(f32), low.astype(f32), jnp.zeros((8, 512), f32)], axis=0)
    rows = rows.astype(bf16)
    grad_latent = total[128:176].astype(bf16)
    for q in range(4):
        part = product(grad_latent, normed_in[q])
        for half in range(2):
            t = q * 2 + half
            pack[t, :32, :] = wkv_rows[t]
            entry = part[half * 24 : half * 24 + 24]
            entry = jnp.concatenate([entry, jnp.zeros((8, 512), f32)], axis=0)
            pack[t, 32:64, :] = entry.astype(bf16)
            pack[t, 64:, :] = rows


def places_of(lengths, places):
    seq_ends = jnp.cumsum(lengths)
    starts = jnp.concatenate([jnp.zeros((1,), jnp.int32), seq_ends])
    segment = jnp.sum((places[:, None] >= seq_ends[None, :]).astype(jnp.int32), axis=1)
    numbers = jnp.arange(seq_ends.shape[0] + 1, dtype=jnp.int32)
    begins = jnp.sum(jnp.where(segment[:, None] == numbers[None, :], starts[None, :], 0), axis=1)
    return begins, segment < lengths.shape[0]


def pad_latent(x):
    x = jnp.pad(x, ((0, 576 - x.shape[0]), (0, 0))).reshape(4, 2, 2, 2, 18, -1)
    x = jnp.pad(x, ((0, 0), (0, 0), (0, 0), (0, 0), (0, 6), (0, 0)))
    x = x.transpose(2, 1, 0, 3, 4, 5).reshape(2, 384, -1)
    return jnp.concatenate([core_pick(x[0], x[1]), core_pick(x[1], x[0])], axis=0)


def unpad_latent(x):
    x = x.reshape(2, 384, -1)
    x = jnp.stack([core_pick(x[0], x[1]), core_pick(x[1], x[0])])
    return x.reshape(2, 2, 4, 2, 24, -1)[:, :, :, :, :18].transpose(2, 1, 0, 3, 4, 5).reshape(576, -1)


def gain_row_table(core):
    table = np.full((16, 128), -1, np.int32)
    for side, xh, y, n in np.ndindex(2, 2, 4, 32):
        entry = (xh * 2 + (core ^ side)) * 128 + y * 32 + n
        block, column = divmod(entry, 18)
        source_y, source_row, half = block // 8, block // 2 % 4, block % 2
        near = (source_row % 2 ^ core) * 2 + source_row // 2
        table[(side * 2 + xh) * 4 + y, n] = (near * 4 + source_y) * 48 + half * 24 + column
    return jnp.asarray(table.reshape(1, 2048))


def take_rope(x):
    x = x.reshape(2, 2, 4, 48, -1)[:, 1, 3]
    two, three = core_pick(x[0], x[1]), core_pick(x[1], x[0])
    return jnp.concatenate([two[8:18], two[24:42], three[:18], three[24:42]], axis=0)


def put_rope(head, rope):
    head = head.reshape(2, 384, -1)
    gap = jnp.zeros((6, rope.shape[1]), rope.dtype)
    first = core_pick(head[0, 336:344], head[1, 336:344])
    two = jnp.concatenate([first, rope[:10], gap, rope[10:28], gap], axis=0)
    three = jnp.concatenate([rope[28:46], gap, rope[46:64], gap], axis=0)
    return jnp.concatenate(
        [head[0, :336], core_pick(two, three), head[1, :336], core_pick(three, two)], axis=0
    )


def shards(
    states,
    teacher,
    firstgain,
    wquery,
    wlatent,
    latentgain,
    wkeyvalue,
    woutput,
    secondgain,
    wrouter,
    sharedgate,
    sharedup,
    shareddown,
    expertgate,
    expertup,
    expertdown,
    routes,
    lengths,
    dealing,
):
    y_index = lax.axis_index("y")
    xl_index = lax.axis_index("xl")
    group = lax.axis_index("xl") * 4 + lax.axis_index("z")
    dealt = dealing.reshape(4, 8, 128)
    key_place = dealt.transpose(1, 0, 2).reshape(4096)
    place = lax.dynamic_index_in_dim(dealt, group, 1, keepdims=False).reshape(512)
    begin, valid = places_of(lengths, place)
    angles = rope_angles(place - begin)
    cosine, sine = jnp.cos(angles), jnp.sin(angles)
    own_valid = lax.dynamic_slice_in_dim(valid.astype(f32), y_index * 128, 128, 0)
    valid_count = jnp.sum(lengths).astype(f32)
    chosen_own = jnp.sum(
        (routes[:, :, None] == jnp.arange(EXPERTS, dtype=jnp.int32)[None, None, :]).astype(f32),
        axis=1,
    )

    extra = jnp.concatenate(
        [p[None] for p in pieces(firstgain, 3)]
        + [wrouter.T]
        + [jnp.pad(jnp.concatenate(pieces(latentgain, 3)), (0, 128))[None]]
        + [chosen_own.astype(bf16).reshape(2, 512)]
        + [jnp.zeros((2, 512), bf16)],
        axis=0,
    )
    first = gather_owners(jnp.concatenate([states, extra], axis=0))
    states_here = after(first[0])

    pack = jnp.concatenate(
        [wquery, lanes_in(wkeyvalue), wlatent.T, jnp.zeros((6, 512), bf16)], axis=0
    )
    pack = spread(to_head(pack), TOKEN, 8).reshape(4, 2, 152, 512)
    pack_here = after(pack)
    wq = pack[:, :, :96].reshape(4, 192, 512)
    wkv = lanes_out(pack[:, :, 96:128], 128).transpose(0, 2, 1, 3).reshape(2, 2, 128, 256)
    wkv = jnp.stack([core_pick(wkv[0], wkv[1]), core_pick(wkv[1], wkv[0])], axis=1)
    wkv = pad_latent(wkv.reshape(KV_RANK, 256))
    wlat = pack[:, :, 128:152].reshape(4, 48, 512)

    outs_pack = jnp.concatenate(
        [
            lanes_in(woutput.T.reshape(64, 4, 128).transpose(1, 0, 2)),
            lanes_in(
                jnp.pad(
                    jnp.pad(
                        shareddown.T.reshape(64, 2, 4, 4, 22)
                        .transpose(3, 0, 2, 1, 4)
                        .reshape(4, 64, 8, 22),
                        ((0, 0), (0, 0), (0, 0), (0, 2)),
                    ).reshape(4, 64, 192),
                    ((0, 0), (0, 0), (0, 64)),
                )
            ),
        ],
        axis=1,
    )
    shared_pack = jnp.pad(
        jnp.stack([sharedgate.T, sharedup.T]).reshape(2, 4, 22, 512),
        ((0, 0), (0, 0), (0, 2), (0, 0)),
    ).transpose(1, 0, 2, 3)

    units = row_scatter(
        jnp.concatenate(
            [
                swap_row_y(outs_pack),
                expertgate.reshape(4, 88, 512),
                shared_pack[:, 0],
                expertup.reshape(4, 88, 512),
                shared_pack[:, 1],
                swap_row_z(expertdown).reshape(4, 88, 512),
                jnp.zeros((4, 8, 512), bf16),
            ],
            axis=1,
        ),
        states_here,
        pack_here,
    ).reshape(4, 368, 512)
    outs_own = jnp.concatenate([units[q, :48] for q in range(4)], axis=1)
    outs_beside = other_xl(outs_own)
    outs_all = lax.all_gather(jnp.stack([outs_own, outs_beside]), "z", axis=1)
    units_beside = other_xl(lax.optimization_barrier(units)[:, 48:])
    units_own = jnp.concatenate([units[q, 48:] for q in range(4)], axis=1)
    units_own = lax.all_gather(units_own, "z", axis=0)

    core = lax.axis_index("co").reshape(1)
    shape = jax.ShapeDtypeStruct
    normed_in, latent, query, inverse_one, tails, chosen_rows = kernel_call(
        first_body,
        [
            shape((4, 512, 512), bf16),
            shape((48, 512), f32),
            shape((192, 512), bf16),
            shape((512, 1), f32),
            shape((4, 16, 512), f32),
            shape((4, 16, 512), f32),
        ],
        [part.reshape(8, 144, 512) for part in first] + [wq, wlat, cosine, sine],
        2 * 512 * 240 * 2048,
    )
    latent = gather_owners(latent)
    gain_in = jnp.sum(tails[:, :3], axis=1)
    router = jnp.concatenate([tails[q, 3:11].astype(bf16) for q in range(4)], axis=1)
    rank_gain = jnp.sum(tails[:, 11, :384].reshape(2, 2, 3, 128), axis=2)
    rank_gain = jnp.stack(
        [core_pick(rank_gain[0], rank_gain[1]), core_pick(rank_gain[1], rank_gain[0])], axis=1
    )
    rank_gain = pad_latent(rank_gain.reshape(KV_RANK, 1))
    chosen = chosen_rows[:, 12:14].reshape(512, 8).T
    units_beside = behind(units_beside, after(latent[0]))
    units_beside = jnp.concatenate([units_beside[q] for q in range(4)], axis=1)
    units_beside = lax.all_gather(units_beside, "z", axis=0)
    outs_all = xl_order(outs_all, 0).reshape(8, 48, D)

    def by_side(x, width):
        x = x.reshape(8, x.shape[1], 4, 512).transpose(2, 0, 1, 3)
        return lanes_out(x, width).reshape(4, 512, width)

    wo_t = by_side(outs_all[:, :16], 128)
    shared_down = by_side(outs_all[:, 16:], 256)[:, :, :192].transpose(2, 0, 1).reshape(192, D)
    shared_down = xl_order(shared_down.reshape(4, 2, 24, D), 1).reshape(192, D)

    is_rank = 1.0 - put_rope(jnp.zeros((768, 1), f32), jnp.ones((ROPE, 1), f32))
    rope_take = np.zeros((ROPE, 96), np.float32)
    rope_take[np.arange(ROPE), np.r_[8:18, 24:42, 48:66, 72:90]] = 1.0
    key_pack, latent_head, latent_inverse, compressed = kernel_call(
        latent_body,
        [
            shape((320, 512), bf16),
            shape((768, 512), f32),
            shape((1, 512), f32),
            shape((768, 512), bf16),
        ],
        [part.reshape(8, 48, 512) for part in latent]
        + [wkv, rank_gain, is_rank, jnp.asarray(rope_take), cosine, sine],
        2 * 512 * 256 * 768,
        scalars=[core],
    )
    key_pack = spread(key_pack, TOKEN, 8)

    rows = [begin[None, :], place[None, :]]
    key_place = key_place.reshape(8, 512, 1)
    mine, theirs, attended, log_total = kernel_call(
        attend_body,
        [
            shape((2, 512, 512), f32),
            shape((2, 512, 512), bf16),
            shape((VDIM, 512), f32),
            shape((1, 512), f32),
        ],
        [query, key_pack, key_place, *rows, wo_t],
        2 * 512 * (4096 * 320 + 128 * 2048),
        anchors=[shared_down, router, chosen],
    )
    attn_in = attended.astype(bf16)

    def owner_blocks(x):
        return x.reshape(2, 4, 128, 512)

    mixed = states.astype(f32) + sum_owners(owner_blocks(mine), owner_blocks(theirs))

    squares = jnp.pad(jnp.sum(mixed * mixed, axis=1)[None], ((0, 3), (0, 384)))
    second = gather_owners(
        jnp.concatenate(
            [(mixed * secondgain).astype(bf16), to_rows(squares), jnp.zeros((8, 512), bf16)], axis=0
        )
    )
    wlat_all = lax.all_gather(behind(wlat, after(second[0])), WEIGHT, axis=0)
    numbers = jnp.arange(EXPERTS)[:, None]
    (
        mine,
        theirs,
        gained,
        inner,
        hidden_routed,
        hidden_shared,
        logits,
        routing,
        factors,
        inverse_two,
    ) = kernel_call(
        experts_body,
        [
            shape((2, 512, 512), f32),
            shape((2, 512, 512), bf16),
            shape((512, D), bf16),
            shape((8, 224, 512), f32),
            shape((8, 96, 512), bf16),
            shape((8, 24, 512), bf16),
            shape((8, 512), f32),
            shape((8, 512), f32),
            shape((2, 512), f32),
            shape((1, 512), f32),
        ],
        [
            second[0].reshape(8, 144, 512),
            second[1].reshape(8, 144, 512),
            units_own,
            units_beside,
            shared_down,
            router,
            chosen,
            (numbers == 2 * y_index + xl_index).astype(f32),
            (numbers == 2 * y_index + 1 - xl_index).astype(f32),
        ],
        2 * 512 * D * 2752,
        [
            pltpu.VMEM((2, 4, 96, 512), f32),
            pltpu.VMEM((8, 24, 512), f32),
            pltpu.VMEM((D, 512), bf16),
        ],
        [xl_index.reshape(1)],
    )
    final = mixed + sum_owners(owner_blocks(mine), owner_blocks(theirs))
    output = final.astype(bf16)

    difference = (final - teacher.astype(f32)) * own_valid[:, None]
    error_own = jnp.sum(difference * difference)
    grad_final = difference * (4096.0 / valid_count)
    grad_branch = gather_owners(grad_final.astype(bf16))

    grad_branch, grad_down, grad_shared_down = kernel_call(
        down_back_body,
        [shape((512, D), bf16), shape((768, D), bf16), shape((4, 8, 32, 512), bf16)],
        [part.reshape(8, 128, 512) for part in grad_branch]
        + [hidden_routed.reshape(768, 512), hidden_shared.reshape(192, 512)],
        2 * 512 * D * 960,
        anchors=[wlat_all],
    )
    down_sum = along_z(grad_down.reshape(4, 2, 96, D))
    expert = 2 * y_index + jnp.stack([xl_index, 1 - xl_index])[:, None]
    expert_place = (jnp.arange(1024)[None, :] // 128 == expert).astype(f32).reshape(2, 2, 512)
    mine, theirs, scaled_slopes, side = kernel_call(
        experts_back_body,
        [
            shape((2, 512, 512), f32),
            shape((2, 512, 512), bf16),
            shape((8, 224, 512), bf16),
            shape((4, 4, 512), f32),
        ],
        [grad_branch, units_own, units_beside, shared_down, inner, factors, inverse_two, gained]
        + [expert_place],
        2 * 512 * D * 2752,
        [
            pltpu.VMEM((2, 4, 224, 512), bf16),
            pltpu.VMEM((2, 512, 896), bf16),
            pltpu.VMEM((8, 24, 512), f32),
            pltpu.VMEM((D, 512), bf16),
        ],
    )
    side = jnp.broadcast_to(side[None, None], (2, 2, 4, 4, 512)).reshape(2, 8, 4, 512)
    grad_mid_own, side, ready = sum_owners(owner_blocks(mine), owner_blocks(theirs), side)
    inner_own = side[0, :128]
    combine_own = side[1:3].reshape(8, 128)
    grad_win = dot(
        "ft,td->fd", behind(scaled_slopes.reshape(1792, 512), ready), gained
    ).astype(bf16)
    unit_sum = along_z(grad_win.reshape(4, 2, 224, D))
    routing_own = lax.dynamic_slice_in_dim(routing, y_index * 128, 128, 1)
    logits_own = lax.dynamic_slice_in_dim(logits, y_index * 128, 128, 1)
    inverse_two_own = lax.dynamic_slice_in_dim(inverse_two[0], y_index * 128, 128, 0)[:, None]
    grad_routing = combine_own * chosen_own.T
    grad_logits = (
        routing_own
        * (grad_routing - jnp.sum(routing_own * grad_routing, axis=0, keepdims=True))
    ).astype(bf16)
    normed_mid_own = (mixed * inverse_two_own * secondgain).astype(bf16)
    grad_router = dot("et,td->ed", grad_logits, normed_mid_own)
    grad_mid_own = grad_mid_own + dot("et,de->td", grad_logits, wrouter)
    inner_own = inner_own + jnp.sum(grad_logits.astype(f32) * logits_own, axis=0)
    grad_mixed = (
        grad_final
        + grad_mid_own * secondgain * inverse_two_own
        - mixed * (inverse_two_own * inverse_two_own * inner_own[:, None] / D)
    )
    grad_second = jnp.sum(grad_mid_own * mixed * inverse_two_own, axis=0)


    grad_attn = [x.reshape(2, 512, 512) for x in gather_owners(grad_mixed.astype(bf16))]
    grad_kv, grad_query, outs_rows = kernel_call(
        attend_back_body,
        [shape((8, 320, 512), bf16), shape((192, 512), bf16), shape((4, 2, 288, 512), bf16)],
        [*grad_attn, wo_t, query, key_pack, key_place, *rows, attended, log_total, cosine, sine]
        + [normed_in, grad_shared_down],
        2 * 512 * (4096 * 832 + 512 * 2048),
        scalars=[xl_index.reshape(1)],
        anchors=[down_sum],
    )
    grad_kv = exchange(grad_kv, TOKEN)
    outs_sum = along_z(outs_rows)
    rope_rows = put_rope(jnp.zeros((768, ROPE), bf16), jnp.eye(ROPE, dtype=bf16))
    gain_rows = core_pick(gain_row_table(0), gain_row_table(1))
    mine, theirs, grad_keyvalue, grad_latent, late = kernel_call(
        latent_back_body,
        [
            shape((2, 512, 512), f32),
            shape((2, 512, 512), bf16),
            shape((256, 512), bf16),
            shape((768, 512), bf16),
            shape((16, 4, 512), f32),
        ],
        [
            grad_kv,
            cosine,
            sine,
            wkv,
            latent_head,
            latent_inverse,
            rank_gain,
            rope_rows,
            grad_query,
            wq,
            wlat_all,
            normed_in,
            gain_rows,
            gain_in,
        ],
        2 * 512 * (768 * 256 + 960 * 2048),
        [pltpu.VMEM((4, 768, 512), bf16)],
        [core],
        [unit_sum],
    )
    grad_wkv = dot("rt,ot->ro", compressed, grad_keyvalue)

    own_xh = (jnp.arange(2) == lax.axis_index("xh")).astype(f32)[:, None, None]

    def to_own(x, n):
        x = own_xh * x.reshape(1, 4, n)
        return jnp.stack([x, jnp.zeros_like(x)])

    early = jnp.concatenate(
        [
            jnp.pad(to_own(grad_second, 128), ((0, 0),) * 3 + ((256, 128),))
            + error_own * (jnp.arange(512) == 511).astype(f32),
            to_own(grad_router.reshape(8, 4, 128).transpose(1, 0, 2), 1024),
            jnp.zeros((2, 2, 4, 512), f32),
        ],
        axis=3,
    ).reshape(2, 8, 4, 512)
    unit_sum = jnp.concatenate([down_sum, unit_sum], axis=1)
    beside_sum = other_xl(unit_sum[1])
    side = early + late.reshape(2, 8, 4, 512) + after(beside_sum)
    grad_latent = grad_latent.reshape(2, 2, 4, 48, 512)
    got = sum_owners(
        jnp.concatenate([owner_blocks(mine), grad_latent[0].astype(f32)], axis=2),
        jnp.concatenate([owner_blocks(theirs), grad_latent[1]], axis=2),
        side,
        raw=True,
    )
    by_rank = unpad_latent(grad_wkv)[:KV_RANK].reshape(2, 2, 128, 256)
    by_rank = jnp.stack(
        [core_pick(by_rank[:, 0], by_rank[:, 1]), core_pick(by_rank[:, 1], by_rank[:, 0])]
    )
    wkv_rows = lanes_in(
        by_rank.reshape(4, 128, 2, 128).transpose(0, 2, 1, 3).reshape(8, 128, 128)
    ).astype(bf16)
    grad_in_own, side, pack = kernel_call(
        last_body,
        [shape((128, 512), f32), shape((4, 512), f32), shape((8, 80, 512), bf16)],
        [got, wkv_rows, normed_in],
        2 * 512 * 48 * 2048,
    )
    summed = after(grad_in_own)
    pack = exchange(pack, TOKEN)
    own_wide = states.astype(f32)
    inverse_own = lax.dynamic_slice_in_dim(inverse_one, y_index * 128, 128, 0)
    grad_states = (
        grad_mixed
        + grad_in_own * firstgain * inverse_own
        - own_wide * (inverse_own * inverse_own * side[0, :128, None] / D)
    )

    outs_sum = along_xl(outs_sum, summed)

    pack = jnp.sum(pack.astype(f32), axis=0)
    sums = pack[64:68] + pack[68:72]

    def own_part(row, at, n):
        return lax.dynamic_slice_in_dim(sums[row, at : at + 8 * n], group * n, n, 0)

    router_part = sums[1:3].reshape(8, 8, 16)
    router_part = lax.dynamic_index_in_dim(router_part, group, 1, keepdims=False)
    pack = jnp.concatenate([pack[:56].astype(bf16), outs_sum[192:]], axis=0)
    pack = from_head(pack).astype(f32)
    grad_wkeyvalue = lanes_out(pack[:32], 128)
    grad_wlatent = pack[32:50].T
    grad_wquery = pack[56:]
    loss_value = sums[0, 511] / (valid_count * D)

    unit_sum = (unit_sum[0].astype(f32) + beside_sum.astype(f32)).astype(bf16)
    me = lax.axis_index("xh") * 2 + lax.axis_index("co")
    back = []
    for k in range(4):
        at = (k % 2 * 2 + (lax.axis_index("xh") ^ (k // 2))) * 512 + after(got)
        block = lax.dynamic_slice_in_dim(unit_sum, at, 512, 1)
        back.append(row_permute(block, k) if k else block)
    grad_down, grad_gate, grad_up, grad_shared = kernel_call(
        returned_body,
        [
            shape((4, 88, 512), bf16),
            shape((4, 88, 512), f32),
            shape((4, 88, 512), f32),
            shape((4, 2, 24, 512), f32),
        ],
        back,
        0,
        scalars=[me.reshape(1)],
    )
    outs_part = jnp.concatenate(
        [outs_sum[:64].reshape(4, 16, 512), outs_sum[64:192].reshape(4, 32, 512)], axis=1
    )
    outs_part = swap_row_y(row_return(outs_part.reshape(2, 2, 48, 512)))
    grad_woutput = lanes_out(outs_part[:, :16], 128).astype(f32)
    grad_woutput = grad_woutput.transpose(0, 2, 1).reshape(512, 64)
    sd_sum = lanes_out(outs_part[:, 16:], 256)[:, :, :192].astype(f32)
    grad_shareddown = (
        sd_sum.reshape(4, 64, 4, 2, 24)[..., :22].transpose(3, 2, 0, 4, 1).reshape(704, 64)
    )
    grad_expertdown = swap_row_z(grad_down.reshape(352, 512)).astype(f32)
    grad_expertgate = grad_gate.reshape(352, 512)
    grad_expertup = grad_up.reshape(352, 512)
    grad_sharedgate = grad_shared[:, 0, :22].reshape(88, 512).T
    grad_sharedup = grad_shared[:, 1, :22].reshape(88, 512).T

    return (
        output,
        loss_value,
        grad_states,
        own_part(0, 128, 16),
        grad_wquery,
        grad_wlatent,
        own_part(0, 384, 4),
        grad_wkeyvalue,
        grad_woutput,
        own_part(0, 256, 16),
        router_part.T,
        grad_sharedgate,
        grad_sharedup,
        grad_shareddown,
        grad_expertgate,
        grad_expertup,
        grad_expertdown,
    )


def solution(mesh):
    parts = Mesh(mesh.devices.reshape(2, 2, 4, 2, 4), ("xh", "co", "y", "xl", "z"))
    both = ROW + COL
    return jax.shard_map(
        shards,
        mesh=parts,
        in_specs=(
            P(COL, ROW),
            P(COL, ROW),
            P(ROW),
            P(COL, ROW),
            P(ROW, COL),
            P(ROW),
            P(ROW, COL),
            P(ROW, COL),
            P(ROW),
            P(ROW, None),
            P(ROW, COL),
            P(ROW, COL),
            P(ROW, COL),
            P(COL, ROW),
            P(COL, ROW),
            P(ROW, COL),
            P(COL, None),
            P(),
            P(),
        ),
        out_specs=(
            P(COL, ROW),
            P(),
            P(COL, ROW),
            P(both),
            P(COL, ROW),
            P(ROW, COL),
            P(both),
            P(ROW, COL),
            P(ROW, COL),
            P(both),
            P(both, None),
            P(ROW, COL),
            P(ROW, COL),
            P(ROW, COL),
            P(COL, ROW),
            P(COL, ROW),
            P(ROW, COL),
        ),
        check_vma=False,
    )
```

```python
import math

import jax
import jax.numpy as jnp
import numpy as np
from jax import lax
from jax.experimental import pallas as pl
from jax.experimental.pallas import tpu as pltpu
from jax.sharding import Mesh, PartitionSpec as P

HEADS = 16
NOPE = 128
ROPE = 64
VDIM = 128
KV_RANK = 512
F = 1408
EXPERTS = 8
D = 2048

norm_epsilon = 1e-06
negative_fill = -1e30
rope_base = 10000.0

ROW = ("xh", "co")
COL = ("y", "xl", "z")
CHIPS = ("xh", "y")
WEIGHT = ("xh", "co", "y")
TOKEN = ("xl", "z")

bf16 = jnp.bfloat16
f32 = jnp.float32


def dot(spec, a, b):
    return jnp.einsum(spec, a, b, preferred_element_type=f32)


def exchange(x, axes):
    return lax.all_to_all(x, axes, 0, 0, tiled=True)


def spread(x, axes, n):
    return exchange(jnp.broadcast_to(x[None], (n,) + x.shape), axes)


def pieces(x, n):
    parts = []
    for _ in range(n):
        part = lax.reduce_precision(x, 8, 7)
        parts.append(part.astype(bf16))
        x = x - part
    return parts


def to_rows(vals):
    return jnp.concatenate(pieces(vals, 2), axis=-2)


def from_rows(rows):
    rows = rows.astype(f32)
    return rows[..., :4, :] + rows[..., 4:8, :]


def after(x):
    return (x[(0,) * x.ndim].astype(f32) * 0.0).astype(jnp.int32)


def behind(x, zero):
    return jnp.where(zero == 0, x, jnp.zeros_like(x))


def mate(x):
    return lax.ppermute(x, "co", [(0, 1), (1, 0)])


def core_pick(zero, one):
    return jnp.where(lax.axis_index("co") == 0, zero, one)


def xh_pick(zero, one, later=0):
    return jnp.where(lax.axis_index("xh") + later == 0, zero, one)


def gather_owners(x):
    own = spread(x, CHIPS, 8).reshape(2, 4, *x.shape)
    return own, mate(own)


def sum_owners(mine, theirs, side=None, raw=False):
    rows = mine.shape[2]

    def packed(block, vals):
        block = block.astype(bf16).reshape(8, rows, 512)
        return block if side is None else jnp.concatenate([block, to_rows(vals)], axis=1)

    got = mate(packed(theirs, None if side is None else side[1]))
    mine = mine.reshape(8, rows, 512) + got[:, :rows].astype(f32)
    vals = None if side is None else side[0] + from_rows(got[:, rows:])
    ready = packed(mine, vals)
    got = exchange(ready, CHIPS)
    if raw:
        return got
    total = jnp.sum(got[:, :rows].astype(f32), axis=0)
    if side is None:
        return total
    return total, jnp.sum(from_rows(got[:, rows:]), axis=0), after(ready)


def other_xl(x):
    return lax.ppermute(x, "xl", [(0, 1), (1, 0)])


def xl_pick(zero, one):
    return jnp.where(lax.axis_index("xl") == 0, zero, one)


def xl_order(x, axis):
    return xl_pick(x, jnp.flip(x, axis))


def z_first(x):
    return jnp.swapaxes(x.reshape(2, 4, *x.shape[1:]), 0, 1)


def along_z(x):
    z, xl, n, m = x.shape
    x = lax.psum_scatter(x.reshape(8 * n, m), "z", scatter_dimension=0, tiled=True)
    return x.reshape(2, n, m)


def along_xl(x, later):
    return (x[0].astype(f32) + behind(other_xl(x[1]), later).astype(f32)).astype(bf16)


def row_permute(block, k):
    return lax.ppermute(block, ROW, [(r, r ^ k) for r in range(4)])


def row_scatter(x, start=0, end=0):
    me = lax.axis_index("xh") * 2 + lax.axis_index("co") + start
    got = [lax.dynamic_index_in_dim(x, me, 0, keepdims=False)]
    for k in (1, 2, 3):
        got.append(row_permute(lax.dynamic_index_in_dim(x, me ^ k, 0, keepdims=False), k))
    return jnp.stack(
        [
            jnp.stack([xh_pick(got[k], got[k + 2], end), xh_pick(got[k + 2], got[k], end)])
            for k in (0, 1)
        ]
    )


def row_return(x):
    got = []
    for k in range(4):
        near, far = x[k % 2, 0], x[k % 2, 1]
        block = xh_pick(near, far) if k < 2 else xh_pick(far, near)
        got.append(row_permute(block, k) if k else block)
    me = lax.axis_index("xh") * 2 + lax.axis_index("co")
    got = jnp.stack(got)
    return jnp.stack(
        [lax.dynamic_index_in_dim(got, me ^ r, 0, keepdims=False) for r in range(4)]
    )


def swap_row_y(x):
    pairs = [(r * 4 + y, y * 4 + r) for r in range(4) for y in range(4)]
    return lax.ppermute(x, WEIGHT, pairs)


def swap_row_z(x):
    pairs = [(r * 4 + z, z * 4 + r) for r in range(4) for z in range(4)]
    return lax.ppermute(x, ROW + ("z",), pairs)


def head_pairs():
    pairs = []
    for n in range(32):
        xh, co, xl, hi, lo = n >> 4, n >> 3 & 1, n >> 2 & 1, n >> 1 & 1, n & 1
        source = hi << 4 | (co ^ xl) << 3 | xh << 2 | co << 1 | lo
        pairs.append((source, n))
    return pairs


def to_head(x):
    return lax.ppermute(x, ROW + TOKEN, head_pairs())


def from_head(x):
    return lax.ppermute(x, ROW + TOKEN, [(b, a) for a, b in head_pairs()])


def lanes_in(x):
    k = 512 // x.shape[-1]
    n = x.shape[-2] // k
    return jnp.concatenate([x[..., i * n : (i + 1) * n, :] for i in range(k)], axis=-1)


def lanes_out(x, width):
    return jnp.concatenate(
        [x[..., i * width : (i + 1) * width] for i in range(512 // width)], axis=-2
    )


def rotate_rows(v, cosine, sine):
    a, b = v[: ROPE // 2], v[ROPE // 2 :]
    return jnp.concatenate([a * cosine - b * sine, b * cosine + a * sine], axis=0)


def rotate_back_rows(g, cosine, sine):
    a, b = g[: ROPE // 2], g[ROPE // 2 :]
    return jnp.concatenate([a * cosine + b * sine, b * cosine - a * sine], axis=0)


def rope_angles(position):
    exponents = jnp.arange(ROPE // 2, dtype=f32) * (2.0 / ROPE)
    frequency = jnp.exp(-math.log(rope_base) * exponents)
    return frequency[:, None] * position.astype(f32)[None, :]


def product(a, b, left=1, right=0):
    return lax.dot_general(a, b, (((left,), (right,)), ((), ())), preferred_element_type=f32)


def kernel_call(body, outs, args, flops, scratch=(), scalars=(), anchors=()):
    moved = sum(x.size * x.dtype.itemsize for x in list(args) + list(outs))
    vmem, smem = pl.BlockSpec(memory_space=pltpu.VMEM), pl.BlockSpec(memory_space=pltpu.SMEM)
    used = len(scalars) + len(args)

    def without_anchors(*refs):
        body(*refs[:used], *refs[used + len(anchors) :])

    return pl.pallas_call(
        without_anchors,
        out_shape=outs,
        in_specs=[smem] * len(scalars)
        + [vmem] * len(args)
        + [pl.BlockSpec(memory_space=pl.ANY)] * len(anchors),
        out_specs=[vmem] * len(outs),
        scratch_shapes=list(scratch),
        compiler_params=pltpu.CompilerParams(vmem_limit_bytes=44 * 2**20),
        cost_estimate=pl.CostEstimate(flops=flops, bytes_accessed=moved, transcendentals=0),
    )(*scalars, *args, *anchors)


SCORE_SCALE = (NOPE + ROPE) ** (-0.5)


def first_body(
    own, other, wq, wlat, cosine, sine,
    normed_in, latent, query, inverse, tails, chosen,
):
    blocks = []
    total = jnp.zeros((512, 1), f32)
    for q in range(4):
        part, xh = (own, other)[q // 2], q % 2
        x = [part[xh * 4 + y, :128, :].astype(f32) for y in range(4)]
        x = jnp.concatenate(x, axis=0)
        blocks.append(x)
        total = total + jnp.sum(x * x, axis=1, keepdims=True)
        tails[q] = part[xh * 4, 128:, :].astype(f32)
    inv = lax.rsqrt(total / D + norm_epsilon)
    inverse[...] = inv
    lat = jnp.zeros((48, 512), f32)
    acc = jnp.zeros((192, 512), f32)
    for q in range(4):
        gain = tails[q, 0:1, :] + tails[q, 1:2, :] + tails[q, 2:3, :]
        normed = (blocks[q] * inv * gain).astype(bf16)
        normed_in[q] = normed
        normed = normed.T
        lat = lat + product(wlat[q], normed)
        acc = acc + product(wq[q], normed)
    latent[...] = lat
    a, b = acc[NOPE : NOPE + 32], acc[NOPE + 32 :]
    query[:NOPE, :] = acc[:NOPE].astype(bf16)
    query[NOPE:, :] = jnp.concatenate(
        [a * cosine[...] - b * sine[...], b * cosine[...] + a * sine[...]], axis=0
    ).astype(bf16)
    for y in range(4):
        chosen[y] = own[y, 128:, :].astype(f32)


def latent_body(
    core, own, other, wkv, rank_gain, is_rank, rope_take, cosine, sine,
    key_pack, latent_head, latent_inverse, compressed,
):
    lat = jnp.concatenate([own[...].reshape(384, 512), other[...].reshape(384, 512)], axis=0)
    lat = lat * is_rank[...]
    latent_head[...] = lat
    inv = lax.rsqrt(jnp.sum(lat * lat, axis=0, keepdims=True) / KV_RANK + norm_epsilon)
    latent_inverse[...] = inv
    comp = (lat * inv * rank_gain[...]).astype(bf16)
    compressed[...] = comp
    keyvalue = product(wkv[...], comp, 0, 0)
    first = jnp.where(core[0] == 0, own[7], other[7])
    second = jnp.where(core[0] == 0, other[7], own[7])
    rope = lax.dot_general(
        rope_take[...],
        jnp.concatenate([first, second], axis=0),
        (((1,), (0,)), ((), ())),
        precision=lax.Precision.HIGHEST,
        preferred_element_type=f32,
    )
    a, b = rope[:32], rope[32:]
    key_pack[:NOPE, :] = keyvalue[:NOPE].astype(bf16)
    key_pack[NOPE : NOPE + ROPE, :] = jnp.concatenate(
        [a * cosine[...] - b * sine[...], b * cosine[...] + a * sine[...]], axis=0
    ).astype(bf16)
    key_pack[NOPE + ROPE :, :] = keyvalue[NOPE:].astype(bf16)


def returned_body(me, got0, got1, got2, got3, down, gate, up, shared):
    for k, got in enumerate((got0, got1, got2, got3)):
        block = got[...].astype(f32)
        at = me[0] ^ k
        down[at] = block[:88].astype(bf16)
        gate[at] = block[96:184]
        up[at] = block[208:296]
        shared[at, 0] = block[184:208]
        shared[at, 1] = block[296:320]


def attend_body(query, key_pack, key_place, begin, place, wo_t, mine, theirs, attended, log_total):
    def block(b, state):
        top, total, acc = state
        keys, values = key_pack[b, :192, :], key_pack[b, 192:, :]
        scores = product(keys, query[...], 0, 0) * SCORE_SCALE
        at = key_place[b]
        allowed = (at >= begin[...]) & (at <= place[...])
        scores = jnp.where(allowed, scores, negative_fill)
        new_top = jnp.maximum(top, jnp.max(scores, axis=0, keepdims=True))
        weights = jnp.where(allowed, jnp.exp(scores - new_top), 0.0)
        factor = jnp.exp(top - new_top)
        total = total * factor + jnp.sum(weights, axis=0, keepdims=True)
        acc = acc * factor + product(values, weights.astype(bf16))
        return new_top, total, acc

    top, total, acc = lax.fori_loop(
        0,
        8,
        block,
        (
            jnp.full((1, 512), negative_fill, f32),
            jnp.zeros((1, 512), f32),
            jnp.zeros((VDIM, 512), f32),
        ),
    )
    result = acc / total
    attended[...] = result
    log_total[...] = top + jnp.log(total)
    attn_in = result.T.astype(bf16)
    for q in range(4):
        part = product(attn_in, wo_t[q], 1, 1)
        if q < 2:
            mine[q] = part
        else:
            theirs[q - 2] = part.astype(bf16)


def attend_back_body(
    this_xl, own, other, wo_t, query, key_pack, key_place, begin, place, attended, log_total, cosine,
    sine, normed_in, grad_shared_down,
    grad_kv, grad_query, outs_rows,
):
    attn_in = attended[...].astype(bf16)
    for q in range(4):
        grad = own[q] if q < 2 else other[q - 2]
        part = product(attn_in, grad).T.astype(bf16)
        for c in range(8):
            xl, z = c // 4, c % 4
            for k in range(4):
                at = c * 64 + k * 16
                lanes = slice(k * 128, k * 128 + 128)
                outs_rows[z, xl ^ this_xl[0], q * 16 : q * 16 + 16, lanes] = part[at : at + 16]
            rows = slice(64 + q * 32, 96 + q * 32)
            outs_rows[z, xl ^ this_xl[0], rows, :] = grad_shared_down[q, c]
    grad = product(own[0], wo_t[0]) + product(own[1], wo_t[1])
    grad = grad + product(other[0], wo_t[2]) + product(other[1], wo_t[3])
    grad_by_token = grad.astype(bf16)
    grad = grad.T.astype(bf16)
    query_by_token = query[...].astype(f32).T.astype(bf16)
    delta = jnp.sum(grad.astype(f32) * attended[...], axis=0, keepdims=True)

    def block(b, acc):
        keys, values = key_pack[b, :192, :], key_pack[b, 192:, :]
        scores = product(keys, query[...], 0, 0) * SCORE_SCALE
        at = key_place[b]
        allowed = (at >= begin[...]) & (at <= place[...])
        probs = jnp.where(allowed, jnp.exp(scores - log_total[...]), 0.0)
        grad_probs = product(values, grad, 0, 0)
        grad_scores = (probs * (grad_probs - delta)).astype(bf16)
        part = product(grad_scores, query_by_token) * SCORE_SCALE
        grad_kv[b, :192, :] = part.T.astype(bf16)
        grad_kv[b, 192:, :] = product(probs.astype(bf16), grad_by_token).T.astype(bf16)
        return acc + product(keys, grad_scores)

    acc = lax.fori_loop(0, 8, block, jnp.zeros((192, 512), f32)) * SCORE_SCALE
    a, b = acc[NOPE : NOPE + 32], acc[NOPE + 32 :]
    grad_query[:NOPE, :] = acc[:NOPE].astype(bf16)
    grad_query[NOPE:, :] = jnp.concatenate(
        [a * cosine[...] + b * sine[...], b * cosine[...] - a * sine[...]], axis=0
    ).astype(bf16)
    for q in range(4):
        part = product(grad_query[...], normed_in[q]).astype(bf16)
        for low in range(2):
            rows = part[low * 96 : low * 96 + 96]
            outs_rows[q % 2 * 2 + low, q // 2 ^ this_xl[0], 192:, :] = rows


def latent_back_body(
    core, got, cosine, sine, wkv, latent_head, latent_inverse, rank_gain, rope_rows, grad_query, wq,
    wlat_all, normed_in, gain_rows, gain,
    mine, theirs, grad_keyvalue, grad_latent, late,
    wlat,
):
    for side in range(2):
        for n in range(8):
            source = (n // 4) * 8 + (core[0] ^ side) * 4 + n % 4
            at = side * 384 + n * 48
            for q in range(4):
                wlat[q, at : at + 48, :] = wlat_all[source, q ^ (2 * side), :, :]
    total = got[0].astype(f32)
    for b in range(1, 8):
        total = total + got[b].astype(f32)
    a, b = total[NOPE : NOPE + 32], total[NOPE + 32 : NOPE + ROPE]
    grad_rope = jnp.concatenate(
        [a * cosine[...] + b * sine[...], b * cosine[...] - a * sine[...]], axis=0
    ).astype(bf16)
    grad = jnp.concatenate([total[:NOPE], total[NOPE + ROPE :]], axis=0).astype(bf16)
    grad_keyvalue[...] = grad
    grad_compressed = product(wkv[...], grad)
    lat, inv = latent_head[...], latent_inverse[...]
    scaled = grad_compressed * rank_gain[...]
    inner_rank = jnp.sum(scaled * lat, axis=0, keepdims=True)
    gain_sum = jnp.sum(grad_compressed * lat * inv, axis=1, keepdims=True)
    gain_row = jnp.broadcast_to(gain_sum, (768, 128)).T[:8]
    gain_high = gain_row.astype(bf16)
    gain_low = (gain_row - gain_high.astype(f32)).astype(bf16)
    unpad = lax.broadcasted_iota(jnp.int32, (768, 2048), 0) == gain_rows[...]
    unpad = unpad.astype(f32).astype(bf16)
    gain_row = product(gain_high, unpad) + product(gain_low, unpad)
    result = scaled * inv - lat * (inv * inv * inv * inner_rank / KV_RANK)
    result = result + product(rope_rows[...], grad_rope)
    grad_latent[...] = result.astype(bf16)
    result = result.T.astype(bf16)
    grad_query_turned = grad_query[...].astype(f32).T.astype(bf16)
    inner_sum = jnp.zeros((512, 1), f32)
    firsts = []
    for q in range(4):
        part = product(grad_query_turned, wq[q]) + product(result, wlat[q])
        if q < 2:
            mine[q] = part
        else:
            theirs[q - 2] = part.astype(bf16)
        weighted = part * normed_in[q].astype(f32)
        inner_sum = inner_sum + jnp.sum(weighted, axis=1, keepdims=True)
        firsts.append(jnp.sum(weighted, axis=0, keepdims=True) / gain[q : q + 1, :])
    inner = jnp.broadcast_to(inner_sum, (512, 128)).T[:1]
    late[...] = jnp.zeros((16, 4, 512), f32)
    for q in range(4):
        for y in range(4):
            at = q * 4 + y
            late[at, :1, :128] = inner[:, y * 128 : y * 128 + 128]
            late[at, :1, 128:256] = firsts[q][:, y * 128 : y * 128 + 128]
            late[at, :1, 384:512] = gain_row[:1, at * 128 : at * 128 + 128]


def fill_features(x2, parts):
    for side, part in enumerate(parts):
        for xh in range(2):
            at = side * 1024 + xh * 512
            for y in range(4):
                x2[y * 128 : y * 128 + 128, at : at + 512] = part[xh * 4 + y, :128, :]


def experts_body(
    this_xl, own, other, units_own, units_beside, shared_down, router, chosen, first_expert, second_expert,
    mine, theirs, x2, inner, hidden_routed, hidden_shared, logits, routing, factors, inverse,
    routed, shared, x2_turned,
):
    fill_features(x2, (own, other))
    x2_turned[...] = x2[...].T
    squares = []
    for y in range(4):
        total = jnp.zeros((1, 128), f32)
        for part in (own, other):
            for xh in range(2):
                rows = part[xh * 4 + y, 128:144, :].astype(f32)
                total = total + (rows[:1, :128] + rows[4:5, :128])
        squares.append(total)
    inv = lax.rsqrt(jnp.concatenate(squares, axis=1) / D + norm_epsilon)
    inverse[...] = inv
    scores = product(router[...], x2_turned[...]) * inv
    logits[...] = scores
    scores = jnp.exp(scores - jnp.max(scores, axis=0, keepdims=True))
    scores = scores / jnp.sum(scores, axis=0, keepdims=True)
    routing[...] = scores
    combine = scores * chosen[...]
    factors[:1, :] = jnp.sum(combine * first_expert[...], axis=0, keepdims=True)
    factors[1:, :] = jnp.sum(combine * second_expert[...], axis=0, keepdims=True)

    for p, units in enumerate((units_own, units_beside)):

        def block(z, carry, p=p, units=units):
            t = 2 * z + p
            h = product(units[z, :224, :], x2_turned[...]) * inv
            inner[t] = h
            gate, up = h[:112], h[112:]
            act = gate * jax.nn.sigmoid(gate) * up
            hidden = act[:88] * factors[p : p + 1, :]
            hidden = jnp.concatenate([hidden, jnp.zeros((8, 512), f32)], axis=0)
            routed[p, z] = hidden
            hidden_routed[t] = hidden.astype(bf16)
            shared[t] = act[88:]
            hidden_shared[2 * z + (p ^ this_xl[0])] = act[88:].astype(bf16)
            return carry

        lax.fori_loop(0, 4, block, 0)
    by_token = [routed[p].reshape(384, 512).T.astype(bf16) for p in range(2)]
    shared_by_token = shared[...].reshape(192, 512).T.astype(bf16)
    for q in range(4):
        at = q * 512
        part = product(shared_by_token, shared_down[:, at : at + 512])
        for p, units in enumerate((units_own, units_beside)):
            part = part + product(by_token[p], units[:, 224:, at : at + 512].reshape(384, 512))
        if q < 2:
            mine[q] = part
        else:
            theirs[q - 2] = part.astype(bf16)


def down_back_body(own, other, hidden_routed, hidden_shared, grad2, grad_down, grad_shared_down):
    fill_features(grad2, (own, other))
    grad_shared_down[...] = jnp.zeros((4, 8, 32, 512), bf16)
    for q in range(4):
        at = q * 512
        part = product(hidden_routed[...], grad2[:, at : at + 512])
        grad_down[:, at : at + 512] = part.astype(bf16)
        part = product(hidden_shared[...], grad2[:, at : at + 512]).T.astype(bf16)
        for c in range(8):
            for k in range(2):
                at = c * 64 + k * 32
                grad_shared_down[q, c, :, k * 256 : k * 256 + 192] = part[at : at + 32]


def experts_back_body(
    grad2, units_own, units_beside, shared_down, inner, factors, inverse, x2, expert_place,
    mine, theirs, scaled, side,
    slopes, by_token, grad_shared, grad2_turned,
):
    side[...] = jnp.zeros((4, 4, 512), f32)
    grad2_turned[...] = grad2[...].T
    grad_shared[...] = product(shared_down[...], grad2_turned[...]).reshape(8, 24, 512)
    inv = inverse[...]
    for p, units in enumerate((units_own, units_beside)):
        factor = factors[p : p + 1, :]

        def block(z, reached, p=p, units=units, factor=factor):
            t = 2 * z + p
            grad = product(units[z, 224:, :], grad2_turned[...])[:88]
            gate, up = inner[t, :112, :], inner[t, 112:, :]
            sig = jax.nn.sigmoid(gate)
            silu = gate * sig
            reached = reached + jnp.sum(grad * (silu * up)[:88], axis=0, keepdims=True)
            grad = jnp.concatenate([grad * factor, grad_shared[t]], axis=0)
            gate_slope = grad * up * sig * (1.0 + gate * (1.0 - sig))
            up_slope = grad * silu
            slopes[p, z, :112, :] = gate_slope.astype(bf16)
            slopes[p, z, 112:, :] = up_slope.astype(bf16)
            scaled[t, :112, :] = (gate_slope * inv).astype(bf16)
            scaled[t, 112:, :] = (up_slope * inv).astype(bf16)
            return reached

        reached = lax.fori_loop(0, 4, block, jnp.zeros((1, 512), f32))
        for y in range(4):
            part = reached[:, y * 128 : y * 128 + 128]
            part = jnp.concatenate([part] * 4, axis=1)
            side[y, 1:3, :] += part * expert_place[p]
        by_token[p] = slopes[p].reshape(896, 512).T
    total = jnp.zeros((512, 1), f32)
    for q in (2, 3, 0, 1):
        at = q * 512
        part = product(by_token[0], units_own[:, :224, at : at + 512].reshape(896, 512))
        part = part + product(by_token[1], units_beside[:, :224, at : at + 512].reshape(896, 512))
        if q < 2:
            mine[q] = part
        else:
            theirs[q - 2] = part.astype(bf16)
        part = part * x2[:, at : at + 512].astype(f32)
        total = total + jnp.sum(part, axis=1, keepdims=True)
    inner_sum = jnp.broadcast_to(total, (512, 128)).T[:1] * inv
    for y in range(4):
        side[y, :1, :128] = inner_sum[:, y * 128 : y * 128 + 128]


def last_body(got, wkv_rows, normed_in, grad_own, side, pack):
    total = got[0].astype(f32)
    for k in range(1, 8):
        total = total + got[k].astype(f32)
    grad_own[...] = total[:128]
    sums = total[176:180] + total[180:184]
    side[...] = sums
    high = sums.astype(bf16)
    low = (sums - high.astype(f32)).astype(bf16)
    rows = jnp.concatenate([high.astype(f32), low.astype(f32), jnp.zeros((8, 512), f32)], axis=0)
    rows = rows.astype(bf16)
    grad_latent = total[128:176].astype(bf16)
    for q in range(4):
        part = product(grad_latent, normed_in[q])
        for half in range(2):
            t = q * 2 + half
            pack[t, :32, :] = wkv_rows[t]
            entry = part[half * 24 : half * 24 + 24]
            entry = jnp.concatenate([entry, jnp.zeros((8, 512), f32)], axis=0)
            pack[t, 32:64, :] = entry.astype(bf16)
            pack[t, 64:, :] = rows


def places_of(lengths, places):
    seq_ends = jnp.cumsum(lengths)
    starts = jnp.concatenate([jnp.zeros((1,), jnp.int32), seq_ends])
    segment = jnp.sum((places[:, None] >= seq_ends[None, :]).astype(jnp.int32), axis=1)
    numbers = jnp.arange(seq_ends.shape[0] + 1, dtype=jnp.int32)
    begins = jnp.sum(jnp.where(segment[:, None] == numbers[None, :], starts[None, :], 0), axis=1)
    return begins, segment < lengths.shape[0]


def pad_latent(x):
    x = jnp.pad(x, ((0, 576 - x.shape[0]), (0, 0))).reshape(4, 2, 2, 2, 18, -1)
    x = jnp.pad(x, ((0, 0), (0, 0), (0, 0), (0, 0), (0, 6), (0, 0)))
    x = x.transpose(2, 1, 0, 3, 4, 5).reshape(2, 384, -1)
    return jnp.concatenate([core_pick(x[0], x[1]), core_pick(x[1], x[0])], axis=0)


def unpad_latent(x):
    x = x.reshape(2, 384, -1)
    x = jnp.stack([core_pick(x[0], x[1]), core_pick(x[1], x[0])])
    return x.reshape(2, 2, 4, 2, 24, -1)[:, :, :, :, :18].transpose(2, 1, 0, 3, 4, 5).reshape(576, -1)


def gain_row_table(core):
    table = np.full((16, 128), -1, np.int32)
    for side, xh, y, n in np.ndindex(2, 2, 4, 32):
        entry = (xh * 2 + (core ^ side)) * 128 + y * 32 + n
        block, column = divmod(entry, 18)
        source_y, source_row, half = block // 8, block // 2 % 4, block % 2
        near = (source_row % 2 ^ core) * 2 + source_row // 2
        table[(side * 2 + xh) * 4 + y, n] = (near * 4 + source_y) * 48 + half * 24 + column
    return jnp.asarray(table.reshape(1, 2048))


def take_rope(x):
    x = x.reshape(2, 2, 4, 48, -1)[:, 1, 3]
    two, three = core_pick(x[0], x[1]), core_pick(x[1], x[0])
    return jnp.concatenate([two[8:18], two[24:42], three[:18], three[24:42]], axis=0)


def put_rope(head, rope):
    head = head.reshape(2, 384, -1)
    gap = jnp.zeros((6, rope.shape[1]), rope.dtype)
    first = core_pick(head[0, 336:344], head[1, 336:344])
    two = jnp.concatenate([first, rope[:10], gap, rope[10:28], gap], axis=0)
    three = jnp.concatenate([rope[28:46], gap, rope[46:64], gap], axis=0)
    return jnp.concatenate(
        [head[0, :336], core_pick(two, three), head[1, :336], core_pick(three, two)], axis=0
    )


def shards(
    states,
    teacher,
    firstgain,
    wquery,
    wlatent,
    latentgain,
    wkeyvalue,
    woutput,
    secondgain,
    wrouter,
    sharedgate,
    sharedup,
    shareddown,
    expertgate,
    expertup,
    expertdown,
    routes,
    lengths,
    dealing,
):
    y_index = lax.axis_index("y")
    xl_index = lax.axis_index("xl")
    group = lax.axis_index("xl") * 4 + lax.axis_index("z")
    dealt = dealing.reshape(4, 8, 128)
    key_place = dealt.transpose(1, 0, 2).reshape(4096)
    place = lax.dynamic_index_in_dim(dealt, group, 1, keepdims=False).reshape(512)
    begin, valid = places_of(lengths, place)
    angles = rope_angles(place - begin)
    cosine, sine = jnp.cos(angles), jnp.sin(angles)
    own_valid = lax.dynamic_slice_in_dim(valid.astype(f32), y_index * 128, 128, 0)
    valid_count = jnp.sum(lengths).astype(f32)
    chosen_own = jnp.sum(
        (routes[:, :, None] == jnp.arange(EXPERTS, dtype=jnp.int32)[None, None, :]).astype(f32),
        axis=1,
    )

    extra = jnp.concatenate(
        [p[None] for p in pieces(firstgain, 3)]
        + [wrouter.T]
        + [jnp.pad(jnp.concatenate(pieces(latentgain, 3)), (0, 128))[None]]
        + [chosen_own.astype(bf16).reshape(2, 512)]
        + [jnp.zeros((2, 512), bf16)],
        axis=0,
    )
    first = gather_owners(jnp.concatenate([states, extra], axis=0))
    states_here = after(first[0])

    pack = jnp.concatenate(
        [wquery, lanes_in(wkeyvalue), wlatent.T, jnp.zeros((6, 512), bf16)], axis=0
    )
    pack = spread(to_head(pack), TOKEN, 8).reshape(4, 2, 152, 512)
    pack_here = after(pack)
    wq = pack[:, :, :96].reshape(4, 192, 512)
    wkv = lanes_out(pack[:, :, 96:128], 128).transpose(0, 2, 1, 3).reshape(2, 2, 128, 256)
    wkv = jnp.stack([core_pick(wkv[0], wkv[1]), core_pick(wkv[1], wkv[0])], axis=1)
    wkv = pad_latent(wkv.reshape(KV_RANK, 256))
    wlat = pack[:, :, 128:152].reshape(4, 48, 512)

    outs_pack = jnp.concatenate(
        [
            lanes_in(woutput.T.reshape(64, 4, 128).transpose(1, 0, 2)),
            lanes_in(
                jnp.pad(
                    jnp.pad(
                        shareddown.T.reshape(64, 2, 4, 4, 22)
                        .transpose(3, 0, 2, 1, 4)
                        .reshape(4, 64, 8, 22),
                        ((0, 0), (0, 0), (0, 0), (0, 2)),
                    ).reshape(4, 64, 192),
                    ((0, 0), (0, 0), (0, 64)),
                )
            ),
        ],
        axis=1,
    )
    shared_pack = jnp.pad(
        jnp.stack([sharedgate.T, sharedup.T]).reshape(2, 4, 22, 512),
        ((0, 0), (0, 0), (0, 2), (0, 0)),
    ).transpose(1, 0, 2, 3)

    units = row_scatter(
        jnp.concatenate(
            [
                swap_row_y(outs_pack),
                expertgate.reshape(4, 88, 512),
                shared_pack[:, 0],
                expertup.reshape(4, 88, 512),
                shared_pack[:, 1],
                swap_row_z(expertdown).reshape(4, 88, 512),
                jnp.zeros((4, 8, 512), bf16),
            ],
            axis=1,
        ),
        states_here,
        pack_here,
    ).reshape(4, 368, 512)
    outs_own = jnp.concatenate([units[q, :48] for q in range(4)], axis=1)
    outs_beside = other_xl(outs_own)
    outs_all = lax.all_gather(jnp.stack([outs_own, outs_beside]), "z", axis=1)
    units_beside = other_xl(lax.optimization_barrier(units)[:, 48:])
    units_own = jnp.concatenate([units[q, 48:] for q in range(4)], axis=1)
    units_own = lax.all_gather(units_own, "z", axis=0)

    core = lax.axis_index("co").reshape(1)
    shape = jax.ShapeDtypeStruct
    normed_in, latent, query, inverse_one, tails, chosen_rows = kernel_call(
        first_body,
        [
            shape((4, 512, 512), bf16),
            shape((48, 512), f32),
            shape((192, 512), bf16),
            shape((512, 1), f32),
            shape((4, 16, 512), f32),
            shape((4, 16, 512), f32),
        ],
        [part.reshape(8, 144, 512) for part in first] + [wq, wlat, cosine, sine],
        2 * 512 * 240 * 2048,
    )
    latent = gather_owners(latent)
    gain_in = jnp.sum(tails[:, :3], axis=1)
    router = jnp.concatenate([tails[q, 3:11].astype(bf16) for q in range(4)], axis=1)
    rank_gain = jnp.sum(tails[:, 11, :384].reshape(2, 2, 3, 128), axis=2)
    rank_gain = jnp.stack(
        [core_pick(rank_gain[0], rank_gain[1]), core_pick(rank_gain[1], rank_gain[0])], axis=1
    )
    rank_gain = pad_latent(rank_gain.reshape(KV_RANK, 1))
    chosen = chosen_rows[:, 12:14].reshape(512, 8).T
    units_beside = behind(units_beside, after(latent[0]))
    units_beside = jnp.concatenate([units_beside[q] for q in range(4)], axis=1)
    units_beside = lax.all_gather(units_beside, "z", axis=0)
    outs_all = xl_order(outs_all, 0).reshape(8, 48, D)

    def by_side(x, width):
        x = x.reshape(8, x.shape[1], 4, 512).transpose(2, 0, 1, 3)
        return lanes_out(x, width).reshape(4, 512, width)

    wo_t = by_side(outs_all[:, :16], 128)
    shared_down = by_side(outs_all[:, 16:], 256)[:, :, :192].transpose(2, 0, 1).reshape(192, D)
    shared_down = xl_order(shared_down.reshape(4, 2, 24, D), 1).reshape(192, D)

    is_rank = 1.0 - put_rope(jnp.zeros((768, 1), f32), jnp.ones((ROPE, 1), f32))
    rope_take = np.zeros((ROPE, 96), np.float32)
    rope_take[np.arange(ROPE), np.r_[8:18, 24:42, 48:66, 72:90]] = 1.0
    key_pack, latent_head, latent_inverse, compressed = kernel_call(
        latent_body,
        [
            shape((320, 512), bf16),
            shape((768, 512), f32),
            shape((1, 512), f32),
            shape((768, 512), bf16),
        ],
        [part.reshape(8, 48, 512) for part in latent]
        + [wkv, rank_gain, is_rank, jnp.asarray(rope_take), cosine, sine],
        2 * 512 * 256 * 768,
        scalars=[core],
    )
    key_pack = spread(key_pack, TOKEN, 8)

    rows = [begin[None, :], place[None, :]]
    key_place = key_place.reshape(8, 512, 1)
    mine, theirs, attended, log_total = kernel_call(
        attend_body,
        [
            shape((2, 512, 512), f32),
            shape((2, 512, 512), bf16),
            shape((VDIM, 512), f32),
            shape((1, 512), f32),
        ],
        [query, key_pack, key_place, *rows, wo_t],
        2 * 512 * (4096 * 320 + 128 * 2048),
        anchors=[shared_down, router, chosen],
    )
    attn_in = attended.astype(bf16)

    def owner_blocks(x):
        return x.reshape(2, 4, 128, 512)

    mixed = states.astype(f32) + sum_owners(owner_blocks(mine), owner_blocks(theirs))

    squares = jnp.pad(jnp.sum(mixed * mixed, axis=1)[None], ((0, 3), (0, 384)))
    second = gather_owners(
        jnp.concatenate(
            [(mixed * secondgain).astype(bf16), to_rows(squares), jnp.zeros((8, 512), bf16)], axis=0
        )
    )
    wlat_all = lax.all_gather(behind(wlat, after(second[0])), WEIGHT, axis=0)
    numbers = jnp.arange(EXPERTS)[:, None]
    (
        mine,
        theirs,
        gained,
        inner,
        hidden_routed,
        hidden_shared,
        logits,
        routing,
        factors,
        inverse_two,
    ) = kernel_call(
        experts_body,
        [
            shape((2, 512, 512), f32),
            shape((2, 512, 512), bf16),
            shape((512, D), bf16),
            shape((8, 224, 512), f32),
            shape((8, 96, 512), bf16),
            shape((8, 24, 512), bf16),
            shape((8, 512), f32),
            shape((8, 512), f32),
            shape((2, 512), f32),
            shape((1, 512), f32),
        ],
        [
            second[0].reshape(8, 144, 512),
            second[1].reshape(8, 144, 512),
            units_own,
            units_beside,
            shared_down,
            router,
            chosen,
            (numbers == 2 * y_index + xl_index).astype(f32),
            (numbers == 2 * y_index + 1 - xl_index).astype(f32),
        ],
        2 * 512 * D * 2752,
        [
            pltpu.VMEM((2, 4, 96, 512), f32),
            pltpu.VMEM((8, 24, 512), f32),
            pltpu.VMEM((D, 512), bf16),
        ],
        [xl_index.reshape(1)],
    )
    final = mixed + sum_owners(owner_blocks(mine), owner_blocks(theirs))
    output = final.astype(bf16)

    difference = (final - teacher.astype(f32)) * own_valid[:, None]
    error_own = jnp.sum(difference * difference)
    grad_final = difference * (4096.0 / valid_count)
    grad_branch = gather_owners(grad_final.astype(bf16))

    grad_branch, grad_down, grad_shared_down = kernel_call(
        down_back_body,
        [shape((512, D), bf16), shape((768, D), bf16), shape((4, 8, 32, 512), bf16)],
        [part.reshape(8, 128, 512) for part in grad_branch]
        + [hidden_routed.reshape(768, 512), hidden_shared.reshape(192, 512)],
        2 * 512 * D * 960,
        anchors=[wlat_all],
    )
    down_sum = along_z(grad_down.reshape(4, 2, 96, D))
    expert = 2 * y_index + jnp.stack([xl_index, 1 - xl_index])[:, None]
    expert_place = (jnp.arange(1024)[None, :] // 128 == expert).astype(f32).reshape(2, 2, 512)
    mine, theirs, scaled_slopes, side = kernel_call(
        experts_back_body,
        [
            shape((2, 512, 512), f32),
            shape((2, 512, 512), bf16),
            shape((8, 224, 512), bf16),
            shape((4, 4, 512), f32),
        ],
        [grad_branch, units_own, units_beside, shared_down, inner, factors, inverse_two, gained]
        + [expert_place],
        2 * 512 * D * 2752,
        [
            pltpu.VMEM((2, 4, 224, 512), bf16),
            pltpu.VMEM((2, 512, 896), bf16),
            pltpu.VMEM((8, 24, 512), f32),
            pltpu.VMEM((D, 512), bf16),
        ],
    )
    side = jnp.broadcast_to(side[None, None], (2, 2, 4, 4, 512)).reshape(2, 8, 4, 512)
    grad_mid_own, side, ready = sum_owners(owner_blocks(mine), owner_blocks(theirs), side)
    inner_own = side[0, :128]
    combine_own = side[1:3].reshape(8, 128)
    grad_win = dot(
        "ft,td->fd", behind(scaled_slopes.reshape(1792, 512), ready), gained
    ).astype(bf16)
    unit_sum = along_z(grad_win.reshape(4, 2, 224, D))
    routing_own = lax.dynamic_slice_in_dim(routing, y_index * 128, 128, 1)
    logits_own = lax.dynamic_slice_in_dim(logits, y_index * 128, 128, 1)
    inverse_two_own = lax.dynamic_slice_in_dim(inverse_two[0], y_index * 128, 128, 0)[:, None]
    grad_routing = combine_own * chosen_own.T
    grad_logits = (
        routing_own
        * (grad_routing - jnp.sum(routing_own * grad_routing, axis=0, keepdims=True))
    ).astype(bf16)
    normed_mid_own = (mixed * inverse_two_own * secondgain).astype(bf16)
    grad_router = dot("et,td->ed", grad_logits, normed_mid_own)
    grad_mid_own = grad_mid_own + dot("et,de->td", grad_logits, wrouter)
    inner_own = inner_own + jnp.sum(grad_logits.astype(f32) * logits_own, axis=0)
    grad_mixed = (
        grad_final
        + grad_mid_own * secondgain * inverse_two_own
        - mixed * (inverse_two_own * inverse_two_own * inner_own[:, None] / D)
    )
    grad_second = jnp.sum(grad_mid_own * mixed * inverse_two_own, axis=0)


    grad_attn = [x.reshape(2, 512, 512) for x in gather_owners(grad_mixed.astype(bf16))]
    grad_kv, grad_query, outs_rows = kernel_call(
        attend_back_body,
        [shape((8, 320, 512), bf16), shape((192, 512), bf16), shape((4, 2, 288, 512), bf16)],
        [*grad_attn, wo_t, query, key_pack, key_place, *rows, attended, log_total, cosine, sine]
        + [normed_in, grad_shared_down],
        2 * 512 * (4096 * 832 + 512 * 2048),
        scalars=[xl_index.reshape(1)],
        anchors=[down_sum],
    )
    grad_kv = exchange(grad_kv, TOKEN)
    outs_sum = along_z(outs_rows)
    rope_rows = put_rope(jnp.zeros((768, ROPE), bf16), jnp.eye(ROPE, dtype=bf16))
    gain_rows = core_pick(gain_row_table(0), gain_row_table(1))
    mine, theirs, grad_keyvalue, grad_latent, late = kernel_call(
        latent_back_body,
        [
            shape((2, 512, 512), f32),
            shape((2, 512, 512), bf16),
            shape((256, 512), bf16),
            shape((768, 512), bf16),
            shape((16, 4, 512), f32),
        ],
        [
            grad_kv,
            cosine,
            sine,
            wkv,
            latent_head,
            latent_inverse,
            rank_gain,
            rope_rows,
            grad_query,
            wq,
            wlat_all,
            normed_in,
            gain_rows,
            gain_in,
        ],
        2 * 512 * (768 * 256 + 960 * 2048),
        [pltpu.VMEM((4, 768, 512), bf16)],
        [core],
        [unit_sum],
    )
    grad_wkv = dot("rt,ot->ro", compressed, grad_keyvalue)

    own_xh = (jnp.arange(2) == lax.axis_index("xh")).astype(f32)[:, None, None]

    def to_own(x, n):
        x = own_xh * x.reshape(1, 4, n)
        return jnp.stack([x, jnp.zeros_like(x)])

    early = jnp.concatenate(
        [
            jnp.pad(to_own(grad_second, 128), ((0, 0),) * 3 + ((256, 128),))
            + error_own * (jnp.arange(512) == 511).astype(f32),
            to_own(grad_router.reshape(8, 4, 128).transpose(1, 0, 2), 1024),
            jnp.zeros((2, 2, 4, 512), f32),
        ],
        axis=3,
    ).reshape(2, 8, 4, 512)
    unit_sum = jnp.concatenate([down_sum, unit_sum], axis=1)
    beside_sum = other_xl(unit_sum[1])
    side = early + late.reshape(2, 8, 4, 512) + after(beside_sum)
    grad_latent = grad_latent.reshape(2, 2, 4, 48, 512)
    got = sum_owners(
        jnp.concatenate([owner_blocks(mine), grad_latent[0].astype(f32)], axis=2),
        jnp.concatenate([owner_blocks(theirs), grad_latent[1]], axis=2),
        side,
        raw=True,
    )
    by_rank = unpad_latent(grad_wkv)[:KV_RANK].reshape(2, 2, 128, 256)
    by_rank = jnp.stack(
        [core_pick(by_rank[:, 0], by_rank[:, 1]), core_pick(by_rank[:, 1], by_rank[:, 0])]
    )
    wkv_rows = lanes_in(
        by_rank.reshape(4, 128, 2, 128).transpose(0, 2, 1, 3).reshape(8, 128, 128)
    ).astype(bf16)
    grad_in_own, side, pack = kernel_call(
        last_body,
        [shape((128, 512), f32), shape((4, 512), f32), shape((8, 80, 512), bf16)],
        [got, wkv_rows, normed_in],
        2 * 512 * 48 * 2048,
    )
    summed = after(grad_in_own)
    pack = exchange(pack, TOKEN)
    own_wide = states.astype(f32)
    inverse_own = lax.dynamic_slice_in_dim(inverse_one, y_index * 128, 128, 0)
    grad_states = (
        grad_mixed
        + grad_in_own * firstgain * inverse_own
        - own_wide * (inverse_own * inverse_own * side[0, :128, None] / D)
    )

    outs_sum = along_xl(outs_sum, summed)

    pack = jnp.sum(pack.astype(f32), axis=0)
    sums = pack[64:68] + pack[68:72]

    def own_part(row, at, n):
        return lax.dynamic_slice_in_dim(sums[row, at : at + 8 * n], group * n, n, 0)

    router_part = sums[1:3].reshape(8, 8, 16)
    router_part = lax.dynamic_index_in_dim(router_part, group, 1, keepdims=False)
    pack = jnp.concatenate([pack[:56].astype(bf16), outs_sum[192:]], axis=0)
    pack = from_head(pack).astype(f32)
    grad_wkeyvalue = lanes_out(pack[:32], 128)
    grad_wlatent = pack[32:50].T
    grad_wquery = pack[56:]
    loss_value = sums[0, 511] / (valid_count * D)

    unit_sum = (unit_sum[0].astype(f32) + beside_sum.astype(f32)).astype(bf16)
    me = lax.axis_index("xh") * 2 + lax.axis_index("co")
    back = []
    for k in range(4):
        at = (k % 2 * 2 + (lax.axis_index("xh") ^ (k // 2))) * 512 + after(got)
        block = lax.dynamic_slice_in_dim(unit_sum, at, 512, 1)
        back.append(row_permute(block, k) if k else block)
    grad_down, grad_gate, grad_up, grad_shared = kernel_call(
        returned_body,
        [
            shape((4, 88, 512), bf16),
            shape((4, 88, 512), f32),
            shape((4, 88, 512), f32),
            shape((4, 2, 24, 512), f32),
        ],
        back,
        0,
        scalars=[me.reshape(1)],
    )
    outs_part = jnp.concatenate(
        [outs_sum[:64].reshape(4, 16, 512), outs_sum[64:192].reshape(4, 32, 512)], axis=1
    )
    outs_part = swap_row_y(row_return(outs_part.reshape(2, 2, 48, 512)))
    grad_woutput = lanes_out(outs_part[:, :16], 128).astype(f32)
    grad_woutput = grad_woutput.transpose(0, 2, 1).reshape(512, 64)
    sd_sum = lanes_out(outs_part[:, 16:], 256)[:, :, :192].astype(f32)
    grad_shareddown = (
        sd_sum.reshape(4, 64, 4, 2, 24)[..., :22].transpose(3, 2, 0, 4, 1).reshape(704, 64)
    )
    grad_expertdown = swap_row_z(grad_down.reshape(352, 512)).astype(f32)
    grad_expertgate = grad_gate.reshape(352, 512)
    grad_expertup = grad_up.reshape(352, 512)
    grad_sharedgate = grad_shared[:, 0, :22].reshape(88, 512).T
    grad_sharedup = grad_shared[:, 1, :22].reshape(88, 512).T

    return (
        output,
        loss_value,
        grad_states,
        own_part(0, 128, 16),
        grad_wquery,
        grad_wlatent,
        own_part(0, 384, 4),
        grad_wkeyvalue,
        grad_woutput,
        own_part(0, 256, 16),
        router_part.T,
        grad_sharedgate,
        grad_sharedup,
        grad_shareddown,
        grad_expertgate,
        grad_expertup,
        grad_expertdown,
    )


def solution(mesh):
    parts = Mesh(mesh.devices.reshape(2, 2, 4, 2, 4), ("xh", "co", "y", "xl", "z"))
    both = ROW + COL
    return jax.shard_map(
        shards,
        mesh=parts,
        in_specs=(
            P(COL, ROW),
            P(COL, ROW),
            P(ROW),
            P(COL, ROW),
            P(ROW, COL),
            P(ROW),
            P(ROW, COL),
            P(ROW, COL),
            P(ROW),
            P(ROW, None),
            P(ROW, COL),
            P(ROW, COL),
            P(ROW, COL),
            P(COL, ROW),
            P(COL, ROW),
            P(ROW, COL),
            P(COL, None),
            P(),
            P(),
        ),
        out_specs=(
            P(COL, ROW),
            P(),
            P(COL, ROW),
            P(both),
            P(COL, ROW),
            P(ROW, COL),
            P(both),
            P(ROW, COL),
            P(ROW, COL),
            P(both),
            P(both, None),
            P(ROW, COL),
            P(ROW, COL),
            P(ROW, COL),
            P(COL, ROW),
            P(COL, ROW),
            P(ROW, COL),
        ),
        check_vma=False,
    )
```
